128 devices in a mesh: ctx: 32 (over y, x, z_lo), fsdp: 4 (over z_hi, core).
Axes of the slice: x: 4, y: 4, z: 4 (z_hi: 2, z_lo: 2; z = z_hi * 2 + z_lo), core: 2. Of those that a mesh axis runs over, the one named last changes fastest.
Arguments:
- tokens: bfloat16 [4, 2, 32, 64, 1024], P('fsdp', None, 'ctx'), may hold values from -6 to 6
- cotangent: bfloat16 [4, 2, 32, 64, 1024], P('fsdp', None, 'ctx'), may hold values from -6 to 6
- doc_ids: int32 [4, 4096], P('fsdp'), may hold values from 0 to 4, as said below
- wq: bfloat16 [1024, 2048], P('fsdp'), may hold values from -0.1875 to 0.1875
- wk: bfloat16 [1024, 1024], P('fsdp'), may hold values from -0.1875 to 0.1875
- wv: bfloat16 [1024, 1024], P('fsdp'), may hold values from -0.1875 to 0.1875
- wo: bfloat16 [2048, 1024], P('fsdp'), may hold values from -0.25 to 0.25
- q_gain: bfloat16 [128], P('fsdp'), may hold values from 0.25 to 1.75
- k_gain: bfloat16 [128], P('fsdp'), may hold values from 0.25 to 1.75
- attn_gain: bfloat16 [1024], P('fsdp'), may hold values from 0.25 to 1.75
- w_gate: bfloat16 [1024, 3072], P('fsdp'), may hold values from -0.1875 to 0.1875
- w_up: bfloat16 [1024, 3072], P('fsdp'), may hold values from -0.1875 to 0.1875
- w_down: bfloat16 [3072, 1024], P('fsdp'), may hold values from -0.109375 to 0.109375
- mlp_gain: bfloat16 [1024], P('fsdp'), may hold values from 0.25 to 1.75
Outputs:
- out: bfloat16 [4, 2, 32, 64, 1024], P('fsdp', None, 'ctx')
- x_grad: float32 [4, 2, 32, 64, 1024], P('fsdp', None, 'ctx')
- wq_grad: float32 [1024, 2048], P('fsdp')
- wk_grad: float32 [1024, 1024], P('fsdp')
- wv_grad: float32 [1024, 1024], P('fsdp')
- wo_grad: float32 [2048, 1024], P('fsdp')
- q_gain_grad: float32 [128], P('fsdp')
- k_gain_grad: float32 [128], P('fsdp')
- attn_gain_grad: float32 [1024], P('fsdp')
- gate_grad: float32 [1024, 3072], P('fsdp')
- up_grad: float32 [1024, 3072], P('fsdp')
- down_grad: float32 [3072, 1024], P('fsdp')
- mlp_gain_grad: float32 [1024], P('fsdp')
The draws below stay inside these ranges and needn't reach their ends.
Inputs may be any that keep to these rules, and one draw needn't show every extreme that they name: `doc_ids`: along each sequence the number starts at 0, never falls and rises by at most one from a token to the next; document 0 runs from position 0 through position 2112; the last token of every sequence has number 4.
All inputs are finite; a program needn't handle non-finite values.
Results may differ from the reference program's by a relative error of at most 0.035.
Values may be sent and summed in bfloat16 or wider, within the bound.
No kernel may reach another device: no remote copies, remote signals or barrier semaphores. Data moves between devices by JAX's collectives and lax.ppermute only.
A program may use at most 256 MiB of HBM per device.

```python
import math
import jax
import jax.numpy as jnp
from jax import lax

D = 1024
HEADS = 16
KV_HEADS = 8
HEAD = 128
FF = 3072
BLOCK = 64
NBLK = 32
SEQS = 4
LEN = 4096
QW = 2048
KW = 1024


def draw_doc_ids(key, part):
    key = jax.random.fold_in(key, 7)
    first_key, start_key = jax.random.split(key)
    first_end = jax.random.randint(first_key, (SEQS, 1), LEN // 2 + BLOCK + 1, LEN - BLOCK + 1)
    offsets = jnp.arange(LEN, dtype=jnp.int32)[None, :]
    coins = jax.random.randint(start_key, (SEQS, LEN), 0, max(LEN // 16, 2))
    forced = (offsets == first_end) | (offsets >= LEN - 3)
    starts = (forced | (offsets > first_end) & (coins == 0)).astype(jnp.int32)
    return jnp.minimum(jnp.cumsum(starts, axis=1), 4).astype(jnp.int32)


def block_levels(rng, extent, cuts, least, top_value):
    def one(axis_at, parts):
        heights = jax.random.uniform(jax.random.fold_in(jax.random.fold_in(rng, 6), axis_at), (parts,), jnp.float32, least / len(cuts), top_value / len(cuts))
        return jnp.repeat(jnp.exp(heights), extent[axis_at] // parts).reshape((-1,) + (1,) * (len(extent) - axis_at - 1))

    gain = one(*cuts[0])
    for cut in cuts[1:]:
        gain = gain * one(*cut)
    return gain


def scatter_about(own_key, shape, width, reach, cuts=(), kind=jnp.bfloat16):
    factor_of = block_levels(own_key, shape, cuts, -0.22, 0.18) if cuts else 1.0
    entries = jax.random.normal(own_key, shape, jnp.float32) * width * factor_of
    return jnp.minimum(jnp.maximum(entries, -reach), reach).astype(kind)


def setup_inputs(seed: int = 0) -> dict:
    key_list = jax.random.split(jax.random.key(seed), 15)
    return {
        "tokens": scatter_about(key_list[0], (SEQS, 2, NBLK, BLOCK, D), 1.0, 6.0, ((0, 4), (2, 32))),
        "cotangent": scatter_about(key_list[1], (SEQS, 2, NBLK, BLOCK, D), 1.0, 6.0, ((0, 4), (2, 32))),
        "doc_ids": draw_doc_ids(jax.random.fold_in(key_list[14], 71), 0),
        "wq": scatter_about(key_list[3], (D, QW), D ** -0.5, 0.1875, ((0, 4),)),
        "wk": scatter_about(key_list[4], (D, KW), D ** -0.5, 0.1875, ((0, 4),)),
        "wv": scatter_about(key_list[5], (D, KW), D ** -0.5, 0.1875, ((0, 4),)),
        "wo": scatter_about(key_list[6], (QW, D), (QW // 4) ** -0.5, 0.25, ((0, 4),)),
        "q_gain": jnp.clip(1.0 + 0.15 * jax.random.normal(key_list[7], (HEAD,), jnp.float32), 0.25, 1.75).astype(jnp.bfloat16),
        "k_gain": jnp.clip(1.0 + 0.15 * jax.random.normal(key_list[8], (HEAD,), jnp.float32), 0.25, 1.75).astype(jnp.bfloat16),
        "attn_gain": jnp.clip(1.0 + 0.15 * jax.random.normal(key_list[9], (D,), jnp.float32), 0.25, 1.75).astype(jnp.bfloat16),
        "w_gate": scatter_about(key_list[10], (D, FF), D ** -0.5, 0.1875, ((0, 4),)),
        "w_up": scatter_about(key_list[11], (D, FF), D ** -0.5, 0.1875, ((0, 4),)),
        "w_down": scatter_about(key_list[12], (FF, D), FF ** -0.5, 0.109375, ((0, 4),)),
        "mlp_gain": jnp.clip(1.0 + 0.15 * jax.random.normal(key_list[13], (D,), jnp.float32), 0.25, 1.75).astype(jnp.bfloat16),
    }


EPS = 1e-06
THETA = 500000.0
FAR = -1e+30
HIGH = lax.Precision.HIGHEST

@jax.custom_vjp
def low(v):
    return lax.optimization_barrier(v.astype(jnp.bfloat16)).astype(jnp.float32)

@jax.custom_vjp
def low_back(v):
    return v

def low_keep(v):
    return (low(v), None)

def low_pass(kept, grad):
    return (grad,)

def back_keep(v):
    return (v, None)

def back_low(kept, grad):
    return (low(grad),)
low.defvjp(low_keep, low_pass)
low_back.defvjp(back_keep, back_low)

def normalize(vector, scaling):
    return vector * lax.rsqrt(lax.optimization_barrier(jnp.mean(vector * vector, axis=-1, keepdims=True)) + EPS) * scaling

def doc_positions(seq_docs):
    offsets = jnp.arange(seq_docs.shape[0], dtype=jnp.int32)
    is_start = jnp.concatenate([jnp.ones((1,), jnp.int32), (seq_docs[1:] != seq_docs[:-1]).astype(jnp.int32)])
    return offsets - lax.cummax(offsets * is_start, axis=0)

def rope_tables(positions, head_width):
    half_width = head_width // 2
    frequency = jnp.exp(jnp.arange(half_width, dtype=jnp.float32) * (-2.0 * math.log(THETA) / head_width))
    angles = positions.astype(jnp.float32)[:, None] * frequency[None, :]
    return (jnp.cos(angles), jnp.sin(angles))

def rotate(vector, cos_table, sine_table):
    half_width = vector.shape[-1] // 2
    first_half = vector[..., :half_width]
    second_half = vector[..., half_width:]
    cos_part = cos_table[:, None, :]
    sine_part = sine_table[:, None, :]
    return jnp.concatenate([first_half * cos_part - second_half * sine_part, second_half * cos_part + first_half * sine_part], axis=-1)

def to_sequence(array):
    first_part = array[:, 0].reshape(array.shape[0], -1, array.shape[4])
    second_part = jnp.flip(array[:, 1], axis=1).reshape(array.shape[0], -1, array.shape[4])
    return jnp.concatenate([first_part, second_part], axis=1)

def from_sequence(array, block_count, block_len):
    split_up = array.reshape(array.shape[0], 2 * block_count, block_len, array.shape[2])
    return jnp.stack([split_up[:, :block_count], jnp.flip(split_up[:, block_count:], axis=1)], axis=1)

def layer(seq_input, weights_f, seq_docs):
    wq, wk, wv, wo, q_gain, k_gain, attn_gain, w_gate, w_up, w_down, mlp_gain = weights_f
    seq_len = seq_input.shape[0]
    groups = HEADS // KV_HEADS
    cos_table, sine_table = rope_tables(doc_positions(seq_docs), HEAD)
    proj_q = low_back(jnp.dot(seq_input, wq, precision=HIGH)).reshape(seq_len, HEADS, HEAD)
    proj_k = low_back(jnp.dot(seq_input, wk, precision=HIGH)).reshape(seq_len, KV_HEADS, HEAD)
    values = low(low_back(jnp.dot(seq_input, wv, precision=HIGH))).reshape(seq_len, KV_HEADS, HEAD)
    queries = low(rotate(normalize(proj_q, q_gain), cos_table, sine_table)).reshape(seq_len, KV_HEADS, groups, HEAD)
    keys = low(rotate(normalize(proj_k, k_gain), cos_table, sine_table))
    query_block = math.gcd(seq_len, 512)
    block_count = seq_len // query_block
    offsets = jnp.arange(seq_len, dtype=jnp.int32)
    score_scale = HEAD ** (-0.5)

    def attend(members):
        query_part, row_index, row_docs = members
        raw_scores = jnp.einsum('qkgd,tkd->kgqt', query_part, keys, precision=HIGH)
        scores = low_back(raw_scores) * score_scale
        allowed = (offsets[None, :] <= row_index[:, None]) & (seq_docs[None, :] == row_docs[:, None])
        scores = jnp.where(allowed[None, None], scores, FAR)
        weights_b = low(jax.nn.softmax(scores, axis=-1))
        return jnp.einsum('kgqt,tkd->qkgd', weights_b, values, precision=HIGH)
    mixed_heads = lax.map(jax.checkpoint(attend), (queries.reshape(block_count, query_block, KV_HEADS, groups, HEAD), offsets.reshape(block_count, query_block), seq_docs.reshape(block_count, query_block)))
    mixed_b = low(low_back(mixed_heads.reshape(seq_len, HEADS * HEAD)))
    branch = low_back(jnp.dot(mixed_b, wo, precision=HIGH))
    hidden = seq_input + normalize(branch, attn_gain)
    hidden_b = low(hidden)
    gate_pre = low_back(jnp.dot(hidden_b, w_gate, precision=HIGH))
    up_pre = low_back(jnp.dot(hidden_b, w_up, precision=HIGH))
    activated = low(jax.nn.silu(gate_pre) * up_pre)
    mlp_out = low_back(jnp.dot(activated, w_down, precision=HIGH))
    return hidden + normalize(mlp_out, mlp_gain)

def reference(tokens, cotangent, doc_ids, wq, wk, wv, wo, q_gain, k_gain, attn_gain, w_gate, w_up, w_down, mlp_gain):
    weights_f = tuple((w.astype(jnp.float32) for w in (wq, wk, wv, wo, q_gain, k_gain, attn_gain, w_gate, w_up, w_down, mlp_gain)))
    seq_input = to_sequence(tokens.astype(jnp.float32))
    seq_cot = to_sequence(cotangent.astype(jnp.float32))

    def per_sequence(running, members):
        one_input, one_cot, one_docs = members

        def forward(inner_input, inner_weights):
            return layer(inner_input, inner_weights, one_docs)
        result, pullback = jax.vjp(forward, one_input, weights_f)
        input_grad, weight_grads = pullback(one_cot)
        return (jax.tree.map(jnp.add, running, weight_grads), (result, input_grad))
    zeros_init = jax.tree.map(jnp.zeros_like, weights_f)
    grads, (results, input_grads) = lax.scan(per_sequence, zeros_init, (seq_input, seq_cot, doc_ids))
    block_count = tokens.shape[2]
    block_len = tokens.shape[3]
    out = from_sequence(results, block_count, block_len).astype(jnp.bfloat16)
    x_grad = from_sequence(input_grads, block_count, block_len)
    return (out, x_grad, grads[0], grads[1], grads[2], grads[3], grads[4], grads[5], grads[6], grads[7], grads[8], grads[9], grads[10])
```

```python
import math

import jax
import jax.numpy as jnp
from jax import lax
from jax.experimental import pallas as pl
from jax.experimental.pallas import tpu as pltpu
from jax.sharding import Mesh, PartitionSpec as P

HEADS = 16
KV_HEADS = 8
HEAD = 128
EPS = 1e-06
THETA = 500000.0

AXES = ("y", "x", "zl", "zh", "core")
CTX = ("y", "x", "zl")
PLANE = ("y", "x")
FSDP = ("zh", "core")
COLUMN = ("zl", "zh", "core")
NCTX = 32
SEQS = 4
BLOCK = 64
ROWS = 2 * BLOCK
LEN = 4096
DOCS = 5
PART = 16
TILES = 8
QT = 256
KT = 512
CHUNK = 320
BF = jnp.bfloat16
F32 = jnp.float32
SCALE = HEAD**-0.5
LOG2E = math.log2(math.e)


def key_block(j):
    return (j, 0) if j < NCTX else (2 * NCTX - 1 - j, 1)


def tile_bounds(meta, t):
    first, last = t * KT, t * KT + KT - 1
    low = jnp.int32(0)
    high = jnp.int32(0)
    for d in range(1, DOCS):
        start = meta[1 + d]
        low = jnp.where(start <= first, start, low)
        high = jnp.where(start <= last, start, high)
    return lax.div(low, KT), jnp.minimum(lax.div(high + (KT - 1), KT), t)


def row_places(meta, t):
    lane = lax.broadcasted_iota(jnp.int32, (1, QT), 1)
    within = lax.rem(lane, QT // 2)
    place = t * KT + lax.div(within, PART) * BLOCK + meta[0] * PART + lax.rem(within, PART)
    start = jnp.zeros((1, QT), jnp.int32)
    for d in range(1, DOCS):
        start = jnp.where(place >= meta[1 + d], meta[1 + d], start)
    return place, start


def allowed(kt, place, start):
    key = kt * KT + lax.broadcasted_iota(jnp.int32, (KT, QT), 0)
    return (key <= place) & (key >= start)


def gather_rows(src, t, rows_of):
    parts = []
    for g in range(2):
        for i in range(8):
            c, b = key_block(8 * t + i)
            parts.append(src[c, pl.ds(rows_of + g * 32 + b * 16, 16), :])
    return jnp.concatenate(parts, axis=0)


def transposed(x):
    return x.astype(F32).T.astype(x.dtype)


def forward_kernel(meta, recv, out, ot, lsum, ks, vt, qt):
    for j in range(2 * NCTX):
        c, b = key_block(j)
        ks[pl.ds(j * BLOCK, BLOCK), :] = recv[c, pl.ds(64 + b * BLOCK, BLOCK), :]
    for i in range(TILES):
        parts = []
        for j in range(8 * i, 8 * i + 8):
            c, b = key_block(j)
            parts.append(recv[c, pl.ds(192 + b * BLOCK, BLOCK), :])
        vt[i] = transposed(jnp.concatenate(parts, axis=0))
        qt[i] = transposed(gather_rows(recv, i, 0))

    def query_tile(t, _):
        q = qt[t]
        place, start = row_places(meta, t)
        low, clear = tile_bounds(meta, t)

        def step(kt, carry, masked):
            total, mixed = carry
            k = ks[pl.ds(pl.multiple_of(kt * KT, KT), KT), :]
            s = jnp.dot(k, q, preferred_element_type=F32)
            p = jnp.exp2(s * (SCALE * LOG2E))
            if masked:
                p = jnp.where(allowed(kt, place, start), p, 0.0)
            total = total + jnp.sum(p, axis=0, keepdims=True)
            mixed = mixed + jnp.dot(vt[kt], p.astype(BF), preferred_element_type=F32)
            return total, mixed

        carry = (jnp.zeros((1, QT), F32), jnp.zeros((HEAD, QT), F32))
        carry = lax.fori_loop(low, clear, lambda kt, cr: step(kt, cr, True), carry)
        carry = lax.fori_loop(jnp.maximum(low, clear), t, lambda kt, cr: step(kt, cr, False), carry)
        total, mixed = step(t, carry, True)
        mixed = mixed * (1.0 / total)
        ot[t] = mixed
        lsum[t] = total
        rows = mixed.T.astype(BF)
        for g in range(2):
            for i in range(8):
                j = 8 * t + i
                half = (j >= NCTX).astype(jnp.int32)
                c = jnp.where(half == 0, j, 2 * NCTX - 1 - j)
                at = pl.multiple_of(g * 32 + half * 16, 16)
                out[c, pl.ds(at, 16), :] = rows[g * 128 + i * 16 : g * 128 + i * 16 + 16]
        return 0

    lax.fori_loop(0, TILES, query_tile, 0)


def backward_kernel(meta, recv, drecv, ot, lsum, out, ks, vs, kt_, q_, qt, do_, dot_, dk, dv):
    for j in range(2 * NCTX):
        c, b = key_block(j)
        ks[pl.ds(j * BLOCK, BLOCK), :] = recv[c, pl.ds(64 + b * BLOCK, BLOCK), :]
        vs[pl.ds(j * BLOCK, BLOCK), :] = recv[c, pl.ds(192 + b * BLOCK, BLOCK), :]
    for i in range(TILES):
        kt_[i] = transposed(ks[pl.ds(i * KT, KT), :])
        rows = gather_rows(recv, i, 0)
        q_[i] = rows
        qt[i] = transposed(rows)
        rows = gather_rows(drecv, i, 0)
        do_[i] = rows
        dot_[i] = transposed(rows)
    dk[...] = jnp.zeros_like(dk)
    dv[...] = jnp.zeros_like(dv)

    def query_tile(t, _):
        q, q_t, d, d_t = q_[t], qt[t], do_[t], dot_[t]
        place, start = row_places(meta, t)
        low, clear = tile_bounds(meta, t)
        delta = jnp.sum(d_t.astype(F32) * ot[t], axis=0, keepdims=True)
        shift = jnp.log2(lsum[t])

        def step(kt, total, masked):
            at = pl.ds(pl.multiple_of(kt * KT, KT), KT)
            s = jnp.dot(ks[at, :], q_t, preferred_element_type=F32)
            p = jnp.exp2(s * (SCALE * LOG2E) - shift)
            if masked:
                p = jnp.where(allowed(kt, place, start), p, 0.0)
            dv[at, :] += jnp.dot(p.astype(BF), d, preferred_element_type=F32)
            dp = jnp.dot(vs[at, :], d_t, preferred_element_type=F32)
            ds = (p * (dp - delta)).astype(BF)
            dk[at, :] += jnp.dot(ds, q, preferred_element_type=F32)
            return total + jnp.dot(kt_[kt], ds, preferred_element_type=F32)

        total = jnp.zeros((HEAD, QT), F32)
        total = lax.fori_loop(low, clear, lambda kt, cr: step(kt, cr, True), total)
        total = lax.fori_loop(jnp.maximum(low, clear), t, lambda kt, cr: step(kt, cr, False), total)
        total = step(t, total, True)
        rows = (total * SCALE).T.astype(BF)
        for g in range(2):
            for i in range(8):
                j = 8 * t + i
                half = (j >= NCTX).astype(jnp.int32)
                c = jnp.where(half == 0, j, 2 * NCTX - 1 - j)
                at = pl.multiple_of(g * 32 + half * 16, 16)
                out[c, pl.ds(at, 16), :] = rows[g * 128 + i * 16 : g * 128 + i * 16 + 16]
        return 0

    lax.fori_loop(0, TILES, query_tile, 0)
    for j in range(2 * NCTX):
        c, b = key_block(j)
        at = pl.ds(j * BLOCK, BLOCK)
        out[c, pl.ds(64 + b * BLOCK, BLOCK), :] = (dk[at, :] * SCALE).astype(BF)
        out[c, pl.ds(192 + b * BLOCK, BLOCK), :] = dv[at, :].astype(BF)


VMEM = pl.BlockSpec(memory_space=pltpu.VMEM)
SMEM = pl.BlockSpec(memory_space=pltpu.SMEM)
PARAMS = pltpu.CompilerParams(vmem_limit_bytes=48 * 1024 * 1024)


def attend(meta, recv):
    return pl.pallas_call(
        forward_kernel,
        out_shape=(
            jax.ShapeDtypeStruct((NCTX, 64, HEAD), BF),
            jax.ShapeDtypeStruct((TILES, HEAD, QT), F32),
            jax.ShapeDtypeStruct((TILES, 1, QT), F32),
        ),
        in_specs=[SMEM, VMEM],
        out_specs=(VMEM, VMEM, VMEM),
        scratch_shapes=[
            pltpu.VMEM((LEN, HEAD), BF),
            pltpu.VMEM((TILES, HEAD, KT), BF),
            pltpu.VMEM((TILES, HEAD, QT), BF),
        ],
        compiler_params=PARAMS,
        cost_estimate=pl.CostEstimate(
            flops=15_000_000_000, bytes_accessed=5_000_000, transcendentals=4_700_000
        ),
        name="attention_forward",
    )(meta, recv)


def attend_back(meta, recv, drecv, ot, lsum):
    return pl.pallas_call(
        backward_kernel,
        out_shape=jax.ShapeDtypeStruct((NCTX, CHUNK, HEAD), BF),
        in_specs=[SMEM, VMEM, VMEM, VMEM, VMEM],
        out_specs=VMEM,
        scratch_shapes=[
            pltpu.VMEM((LEN, HEAD), BF),
            pltpu.VMEM((LEN, HEAD), BF),
            pltpu.VMEM((TILES, HEAD, KT), BF),
            pltpu.VMEM((TILES, QT, HEAD), BF),
            pltpu.VMEM((TILES, HEAD, QT), BF),
            pltpu.VMEM((TILES, QT, HEAD), BF),
            pltpu.VMEM((TILES, HEAD, QT), BF),
            pltpu.VMEM((LEN, HEAD), F32),
            pltpu.VMEM((LEN, HEAD), F32),
        ],
        compiler_params=PARAMS,
        cost_estimate=pl.CostEstimate(
            flops=20_000_000_000, bytes_accessed=8_000_000, transcendentals=4_700_000
        ),
        name="attention_backward",
    )(meta, recv, drecv, ot, lsum)


def rms(u):
    return lax.rsqrt(jnp.mean(u * u, axis=-1, keepdims=True) + EPS)


def dot(a, b):
    return jnp.dot(a, b, preferred_element_type=F32)


def dot_nt(a, b):
    return lax.dot_general(a, b, (((1,), (1,)), ((), ())), preferred_element_type=F32)


def dot_tn(a, b):
    return lax.dot_general(a, b, (((0,), (0,)), ((), ())), preferred_element_type=F32)


def project_kernel(place, group, w, cos, sin, gains, send, qk, tokens):
    for j in range(4):
        n = place[0] ^ j
        base = n * 8
        rows = pl.ds(j * ROWS, ROWS)
        x = group[n, pl.ds(0, ROWS), :]
        tokens[rows, :] = x
        y = dot(x, w[...])
        c, s = cos[n], sin[n]
        qk[rows, :] = y[:, :768]
        for h in range(6):
            u = y[:, h * HEAD : (h + 1) * HEAD]
            u = u * rms(u) * gains[pl.ds(h // 4, 1), :]
            u = (u * c + pltpu.roll(u, HEAD // 2, 1) * s).astype(BF)
            for r in range(4):
                if h < 4:
                    for b in range(2):
                        at = h % 2 * 32 + b * 16
                        send[base + h // 2 * 4 + r, pl.ds(at, 16), :] = u[
                            b * 64 + r * 16 : b * 64 + r * 16 + 16
                        ]
                else:
                    send[base + (h - 4) * 4 + r, pl.ds(64, ROWS), :] = u
        for h in range(2):
            u = y[:, 768 + h * HEAD : 896 + h * HEAD].astype(BF)
            for r in range(4):
                send[base + h * 4 + r, pl.ds(192, ROWS), :] = u


def project(place, group, w, cos, sin, gains):
    return pl.pallas_call(
        project_kernel,
        out_shape=(
            jax.ShapeDtypeStruct((NCTX, CHUNK, HEAD), BF),
            jax.ShapeDtypeStruct((512, 768), F32),
            jax.ShapeDtypeStruct((512, 1024), BF),
        ),
        in_specs=[SMEM] + [VMEM] * 5,
        out_specs=(VMEM,) * 3,
        compiler_params=PARAMS,
        cost_estimate=pl.CostEstimate(
            flops=1_070_000_000, bytes_accessed=9_000_000, transcendentals=4000
        ),
        name="project",
    )(place, group, w, cos, sin, gains)


def project_back_kernel(place, back, qk, cos, sin, gains, dgains_am, tokens, out, send, grads):
    totals = [jnp.zeros((1, HEAD), F32), jnp.zeros((1, HEAD), F32)]
    for j in range(4):
        n = place[0] ^ j
        base = n * 8
        rows = pl.ds(j * ROWS, ROWS)
        c, s = cos[n], sin[n]
        for h in range(6):
            if h < 4:
                at = base + h // 2 * 4
                parts = []
                for b in range(2):
                    for r in range(4):
                        parts.append(back[at + r, pl.ds(h % 2 * 32 + b * 16, 16), :])
                e = jnp.concatenate(parts, axis=0).astype(F32)
            else:
                at = base + (h - 4) * 4
                e = back[at, pl.ds(64, ROWS), :].astype(F32)
                for r in range(1, 4):
                    e = e + back[at + r, pl.ds(64, ROWS), :].astype(F32)
            e = e * c - pltpu.roll(e, HEAD // 2, 1) * s
            u = qk[rows, pl.ds(h * HEAD, HEAD)]
            inverse = rms(u)
            u = u * inverse
            totals[h // 4] = totals[h // 4] + jnp.sum(e * u, axis=0, keepdims=True)
            e = e * gains[pl.ds(h // 4, 1), :]
            e = inverse * (e - u * jnp.mean(e * u, axis=-1, keepdims=True))
            out[rows, pl.ds(h * HEAD, HEAD)] = e.astype(BF)
        for h in range(2):
            at = base + h * 4
            e = back[at, pl.ds(192, ROWS), :].astype(F32)
            for r in range(1, 4):
                e = e + back[at + r, pl.ds(192, ROWS), :].astype(F32)
            out[rows, pl.ds(768 + h * HEAD, HEAD)] = e.astype(BF)
    grads[...] = dot_tn(tokens[...], out[...])
    for f in range(4):
        gain_rows = jnp.concatenate(
            totals + [dgains_am[f], jnp.zeros((10, HEAD), F32)], axis=0
        ).astype(BF)
        for p in range(16):
            for half in range(2):
                to = (p * 2 + half) * 4 + f
                send[to, :, pl.ds(0, 512)] = grads[
                    pl.ds(256 * f + 16 * p, 16), pl.ds(512 * half, 512)
                ].astype(BF)
                send[to, :, pl.ds(512, HEAD)] = gain_rows


def project_back(place, back, qk, cos, sin, gains, dgains_am, tokens):
    return pl.pallas_call(
        project_back_kernel,
        out_shape=(
            jax.ShapeDtypeStruct((512, 1024), BF),
            jax.ShapeDtypeStruct((128, 16, 640), BF),
        ),
        in_specs=[SMEM] + [VMEM] * 7,
        out_specs=(VMEM, VMEM),
        scratch_shapes=[pltpu.VMEM((1024, 1024), F32)],
        compiler_params=PARAMS,
        cost_estimate=pl.CostEstimate(
            flops=1_100_000_000, bytes_accessed=9_000_000, transcendentals=4000
        ),
        name="project_back",
    )(place, back, qk, cos, sin, gains, dgains_am, tokens)


def feed_grads_kernel(pa, norms, mixed, d0, d1, d2, d3, send, db, gu, down, out):
    for j, d in enumerate((d0, d1, d2, d3)):
        db[pl.ds(j * ROWS, ROWS), :] = d[...]
    out[...] = dot_tn(mixed[...], db[...])
    gu[...] = dot_tn(norms[:, pl.ds(0, 1024)], pa[:, pl.ds(384, 768)])
    down[...] = dot_tn(pa[:, pl.ds(0, 384)], norms[:, pl.ds(1024, 1024)])
    for to in range(NCTX):
        p, half = to // 2, to % 2

        def put(tile, ref, row, column):
            send[to, pl.ds(16 * tile, 16), :] = ref[pl.ds(row, 16), pl.ds(column, 128)].astype(BF)

        for f in range(4):
            for k in range(3):
                put(f * 3 + k, gu, 256 * f + 16 * p, 384 * half + 128 * k)
        for k in range(3):
            for i in range(2):
                put(12 + 2 * k + i, down, to // 4 * 48 + 16 * k, to % 4 * 256 + 128 * i)
        for k in range(8):
            put(18 + k, out, 16 * to, 128 * k)


def feed_grads(parts, norms, mixed, d_branches):
    return pl.pallas_call(
        feed_grads_kernel,
        out_shape=jax.ShapeDtypeStruct((NCTX, 416, HEAD), BF),
        in_specs=[VMEM] * 7,
        out_specs=VMEM,
        scratch_shapes=[
            pltpu.VMEM((512, 1024), BF),
            pltpu.VMEM((1024, 768), F32),
            pltpu.VMEM((384, 1024), F32),
            pltpu.VMEM((512, 1024), F32),
        ],
        compiler_params=PARAMS,
        cost_estimate=pl.CostEstimate(
            flops=2_900_000_000, bytes_accessed=12_000_000, transcendentals=0
        ),
        name="feed_grads",
    )(parts, norms, mixed, *d_branches)


def feed_finish_kernel(tiles, gate, up, down, out):
    for c in range(NCTX):
        p, half = c // 2, c % 2
        for n in range(24):
            (up if half else gate)[pl.ds(16 * p, 16), pl.ds(128 * n, 128)] = tiles[c, n].astype(F32)
        for zl in range(2):
            for k in range(3):
                for i in range(2):
                    row = 384 * zl + c // 4 * 48 + 16 * k
                    down[pl.ds(row, 16), pl.ds(c % 4 * 256 + 128 * i, 128)] = tiles[
                        c, 24 + zl * 6 + 2 * k + i
                    ].astype(F32)
        for k in range(8):
            out[pl.ds(16 * c, 16), pl.ds(128 * k, 128)] = tiles[c, 36 + k].astype(F32)


def feed_finish(tiles):
    return pl.pallas_call(
        feed_finish_kernel,
        out_shape=(
            jax.ShapeDtypeStruct((256, 3072), F32),
            jax.ShapeDtypeStruct((256, 3072), F32),
            jax.ShapeDtypeStruct((768, 1024), F32),
            jax.ShapeDtypeStruct((512, 1024), F32),
        ),
        in_specs=[VMEM],
        out_specs=(VMEM,) * 4,
        compiler_params=PARAMS,
        cost_estimate=pl.CostEstimate(flops=0, bytes_accessed=18_000_000, transcendentals=0),
        name="feed_finish",
    )(tiles)


def project_finish_kernel(parts, gq, gk, gv):
    for p in range(16):
        rows = pl.ds(16 * p, 16)
        gq[rows, :] = parts[2 * p].astype(F32)
        for f in range(4):
            at = pl.ds(256 * f, 256)
            gk[rows, at] = parts[2 * p + 1, :, pl.ds(512 * f, 256)].astype(F32)
            gv[rows, at] = parts[2 * p + 1, :, pl.ds(512 * f + 256, 256)].astype(F32)


def project_finish(parts):
    return pl.pallas_call(
        project_finish_kernel,
        out_shape=(
            jax.ShapeDtypeStruct((256, 2048), F32),
            jax.ShapeDtypeStruct((256, 1024), F32),
            jax.ShapeDtypeStruct((256, 1024), F32),
        ),
        in_specs=[VMEM],
        out_specs=(VMEM,) * 3,
        compiler_params=PARAMS,
        cost_estimate=pl.CostEstimate(flops=0, bytes_accessed=6_000_000, transcendentals=0),
        name="project_finish",
    )(parts)


def merge_kernel(place, recv, wo, mixed, keep, give):
    for j in range(4):
        base = (place[0] ^ j) * 8
        for h in range(4):
            parts = []
            for b in range(2):
                for r in range(4):
                    parts.append(recv[base + h // 2 * 4 + r, pl.ds(h % 2 * 32 + b * 16, 16), :])
            mixed[pl.ds(j * ROWS, ROWS), pl.ds(h * HEAD, HEAD)] = jnp.concatenate(parts, axis=0)
    for j in (1, 3, 0, 2):
        y = dot(mixed[pl.ds(j * ROWS, ROWS), :], wo[...])
        if j % 2:
            give[j // 2] = y.astype(BF)
        else:
            keep[j // 2] = y


def merge(place, recv, wo):
    return pl.pallas_call(
        merge_kernel,
        out_shape=(
            jax.ShapeDtypeStruct((512, 512), BF),
            jax.ShapeDtypeStruct((2, ROWS, 1024), F32),
            jax.ShapeDtypeStruct((2, ROWS, 1024), BF),
        ),
        in_specs=[SMEM] + [VMEM] * 2,
        out_specs=(VMEM, VMEM, VMEM),
        compiler_params=PARAMS,
        cost_estimate=pl.CostEstimate(
            flops=540_000_000, bytes_accessed=4_000_000, transcendentals=0
        ),
        name="merge",
    )(place, recv, wo)


def split_kernel(place, d0, d1, d2, d3, wo, send):
    for j, d in enumerate((d0, d1, d2, d3)):
        base = (place[0] ^ j) * 8
        y = dot_nt(d[...], wo[...]).astype(BF)
        for h in range(4):
            for b in range(2):
                for r in range(4):
                    send[base + h // 2 * 4 + r, pl.ds(h % 2 * 32 + b * 16, 16), :] = y[
                        b * 64 + r * 16 : b * 64 + r * 16 + 16, h * HEAD : (h + 1) * HEAD
                    ]


def split(place, ds, wo):
    return pl.pallas_call(
        split_kernel,
        out_shape=jax.ShapeDtypeStruct((NCTX, 64, HEAD), BF),
        in_specs=[SMEM] + [VMEM] * 5,
        out_specs=VMEM,
        compiler_params=PARAMS,
        cost_estimate=pl.CostEstimate(
            flops=540_000_000, bytes_accessed=3_000_000, transcendentals=0
        ),
        name="split",
    )(place, *ds, wo)


def feed_kernel(
    place,
    keep,
    got,
    last,
    x,
    g,
    gains,
    gate0,
    up0,
    down0,
    gate1,
    up1,
    down1,
    cat2,
    cat3,
    result,
    d_hidden,
    d_branch,
    norms,
    eighths,
    dgains,
    w,
    sems,
    parts,
    hb,
    gate,
    up,
    dh,
):
    copies = []

    def fetch(k, src, dst):
        copy = pltpu.make_async_copy(src, dst, sems.at[k])
        copy.start()
        copies.append(copy)

    fetch(0, gate0, w.at[0, :, pl.ds(0, 3072)])
    fetch(1, up0, w.at[0, :, pl.ds(3072, 3072)])
    fetch(2, gate1, w.at[1, :, pl.ds(0, 3072)])
    fetch(3, up1, w.at[1, :, pl.ds(3072, 3072)])
    fetch(4, cat2.at[:, pl.ds(0, 6144)], w.at[2, :, pl.ds(0, 6144)])
    fetch(5, cat3.at[:, pl.ds(0, 6144)], w.at[3, :, pl.ds(0, 6144)])
    for b in range(3):
        rows, at = pl.ds(256 * b, 256), pl.ds(6144 + 1024 * b, 1024)
        fetch(6 + b, down0.at[rows, :], w.at[0, :, at])
        fetch(9 + b, down1.at[rows, :], w.at[1, :, at])
    fetch(12, cat2.at[:, pl.ds(6144, 3072)], w.at[2, :, pl.ds(6144, 3072)])
    fetch(13, cat3.at[:, pl.ds(6144, 3072)], w.at[3, :, pl.ds(6144, 3072)])

    me = place[0]
    gain_a, gain_m = gains[pl.ds(0, 1), :], gains[pl.ds(1, 1), :]
    a = keep[0] + got[0].astype(F32) + last[...].astype(F32)
    inverse_a = rms(a)
    normed_a = a * inverse_a
    h = x[...].astype(F32) + normed_a * gain_a
    for n in range(4):
        hb[n] = h[:, 256 * n : 256 * n + 256].astype(BF)
    norms[:, pl.ds(0, 1024)] = h.astype(BF)
    for k in range(6):
        copies[k].wait()
    for n in range(4):
        at = 768 * n
        u = dot(hb[me], w[0, :, pl.ds(at, 768)])
        v = dot(hb[me], w[0, :, pl.ds(3072 + at, 768)])
        for j in range(1, 4):
            u = u + dot(hb[me ^ j], w[j, :, pl.ds(at, 768)])
            v = v + dot(hb[me ^ j], w[j, :, pl.ds(3072 + at, 768)])
        gate[n] = u
        up[n] = v
        parts[n, :, pl.ds(0, 768)] = (u / (1.0 + jnp.exp(-u)) * v).astype(BF)
    for k in range(6, 14):
        copies[k].wait()
    z = jnp.zeros((ROWS, 1024), F32)
    for j in range(4):
        for b in range(3):
            z = z + dot(
                parts[me ^ j, :, pl.ds(256 * b, 256)], w[j, :, pl.ds(6144 + 1024 * b, 1024)]
            )
    inverse_z = rms(z)
    normed_z = z * inverse_z
    result[...] = (h + normed_z * gain_m).astype(BF)
    e = g[...].astype(F32)
    dgains[pl.ds(1, 1), :] = jnp.sum(e * normed_z, axis=0, keepdims=True)
    weighted = e * gain_m
    dz = inverse_z * (weighted - normed_z * jnp.mean(weighted * normed_z, axis=-1, keepdims=True))
    dz = dz.astype(BF)
    norms[:, pl.ds(1024, 1024)] = dz
    for j in range(4):
        n = me ^ j
        for b in range(3):
            at = pl.ds(256 * b, 256)
            d_act = dot_nt(dz, w[j, :, pl.ds(6144 + 1024 * b, 1024)])
            u, v = gate[n, :, at], up[n, :, at]
            s = 1.0 / (1.0 + jnp.exp(-u))
            parts[n, :, pl.ds(768 + 256 * b, 256)] = (
                d_act * v * (s * (1.0 + u * (1.0 - s)))
            ).astype(BF)
            parts[n, :, pl.ds(1536 + 256 * b, 256)] = (d_act * (u * s)).astype(BF)
    for n in range(8):
        for k in range(3):
            eighths[n, :, pl.ds(384 * k, 384)] = parts[
                n % 4, :, pl.ds(768 * k + 384 * (n // 4), 384)
            ]
    for j in range(4):
        total = jnp.zeros((ROWS, 256), F32)
        for n in range(4):
            total = total + dot_nt(parts[n, :, pl.ds(768, 768)], w[j, :, pl.ds(768 * n, 768)])
            total = total + dot_nt(
                parts[n, :, pl.ds(1536, 768)], w[j, :, pl.ds(3072 + 768 * n, 768)]
            )
        dh[me ^ j] = total
    total = g[...].astype(F32) + jnp.concatenate([dh[n] for n in range(4)], axis=1)
    d_hidden[...] = total
    dgains[pl.ds(0, 1), :] = jnp.sum(total * normed_a, axis=0, keepdims=True)
    weighted = total * gain_a
    d_branch[...] = (
        inverse_a * (weighted - normed_a * jnp.mean(weighted * normed_a, axis=-1, keepdims=True))
    ).astype(BF)


ANY = pl.BlockSpec(memory_space=pl.ANY)


def feed(place, keep, got, last, x, g, gains, weights):
    return pl.pallas_call(
        feed_kernel,
        out_shape=(
            jax.ShapeDtypeStruct((ROWS, 1024), BF),
            jax.ShapeDtypeStruct((ROWS, 1024), F32),
            jax.ShapeDtypeStruct((ROWS, 1024), BF),
            jax.ShapeDtypeStruct((ROWS, 2048), BF),
            jax.ShapeDtypeStruct((8, ROWS, 1152), BF),
            jax.ShapeDtypeStruct((2, 1024), F32),
        ),
        in_specs=[SMEM] + [VMEM] * 6 + [ANY] * 8,
        out_specs=(VMEM,) * 6,
        scratch_shapes=[
            pltpu.VMEM((4, 256, 9216), BF),
            pltpu.SemaphoreType.DMA((14,)),
            pltpu.VMEM((4, ROWS, 2304), BF),
            pltpu.VMEM((4, ROWS, 256), BF),
            pltpu.VMEM((4, ROWS, 768), F32),
            pltpu.VMEM((4, ROWS, 768), F32),
            pltpu.VMEM((4, ROWS, 256), F32),
        ],
        compiler_params=PARAMS,
        cost_estimate=pl.CostEstimate(
            flops=15_000_000_000, bytes_accessed=25_000_000, transcendentals=800_000
        ),
        name="feed_forward",
    )(place, keep, got, last, x, g, gains, *weights)


SWAP = [(0, 1), (1, 0)]


def swap(x, axis):
    return lax.ppermute(x, axis, SWAP)


def flip(x, axes):
    n = 2 ** len(axes)
    return lax.ppermute(x, axes, [(i, n - 1 - i) for i in range(n)])


def in_order(place, own, other):
    return jnp.where(place == 0, jnp.stack([own, other]), jnp.stack([other, own]))


def relative(x):
    far = swap(x, "zh")
    return [x, swap(x, "core"), far, swap(far, "core")]


def absolute(four):
    zh, core = lax.axis_index("zh"), lax.axis_index("core")
    near = in_order(core, four[0], four[1])
    far = in_order(core, four[2], four[3])
    return in_order(zh, near, far).reshape((4,) + four[0].shape)


def exchange(x, axes):
    return lax.all_to_all(x, axes, split_axis=0, concat_axis=0, tiled=True)


def gather_ctx(piece):
    pair = in_order(lax.axis_index("zl"), piece, swap(piece, "zl"))
    return lax.all_gather(pair, PLANE, axis=0, tiled=True)


def after(xs, *others):
    return lax.optimization_barrier((xs,) + others)[0]


def local(
    tokens,
    cotangent,
    doc_ids,
    wq,
    wk,
    wv,
    wo,
    q_gain,
    k_gain,
    attn_gain,
    w_gate,
    w_up,
    w_down,
    mlp_gain,
):
    c = lax.axis_index(CTX)
    f = lax.axis_index(FSDP)
    place = f[None].astype(jnp.int32)
    inputs = tokens.reshape(ROWS, 1024)

    w_qkv = jnp.concatenate(
        [wq.reshape(256, 4, 512), wk.reshape(256, 4, 256), wv.reshape(256, 4, 256)], axis=2
    )
    w_qkv = exchange(jnp.swapaxes(w_qkv, 0, 1), FSDP).reshape(1024, 1024)

    starts = jnp.sum(
        (doc_ids[0][None, :] < jnp.arange(DOCS, dtype=jnp.int32)[:, None]).astype(jnp.int32), axis=1
    )
    misc = jnp.concatenate(
        [
            q_gain,
            k_gain,
            (starts // 64).astype(BF),
            (starts % 64).astype(BF),
            jnp.zeros((54,), BF),
            attn_gain,
            mlp_gain,
            jnp.zeros((384,), BF),
        ]
    )
    pack = jnp.concatenate([inputs, jnp.broadcast_to(misc[None], (16, 1024))], axis=0)
    group = lax.all_gather(pack, FSDP, axis=0, tiled=True).reshape(4, ROWS + 16, 1024)
    gains = group[:, ROWS].astype(F32)
    gains_qk = jnp.stack([gains[:, :32].reshape(HEAD), gains[:, 32:64].reshape(HEAD)])
    gains_am = jnp.stack([gains[:, 128:384].reshape(1024), gains[:, 384:640].reshape(1024)])
    starts_f = (gains[:, 64:69] * 64.0 + gains[:, 69:74]).astype(jnp.int32)

    at = (lax.axis_index("y") * 4 + lax.axis_index("x")) * 16
    piece = jnp.concatenate(
        [lax.dynamic_slice_in_dim(w, at, 16, 0) for w in (w_gate, w_up)]
        + [lax.dynamic_slice_in_dim(w_down, 256 * b + at, 16, 0) for b in range(3)],
        axis=1,
    )
    piece = swap(after(piece, w_qkv), "zh")
    step = jnp.arange(BLOCK, dtype=jnp.int32)
    spot = jnp.concatenate([c * BLOCK + step, (2 * NCTX - 1 - c) * BLOCK + step])
    start = jnp.max(
        jnp.where(starts_f[:, :, None] <= spot[None, None, :], starts_f[:, :, None], 0), axis=1
    )
    position = spot[None, :] - start
    half = jnp.arange(HEAD, dtype=jnp.int32) % (HEAD // 2)
    frequency = jnp.exp(half.astype(F32) * (-2.0 * math.log(THETA) / HEAD))
    angles = position.astype(F32)[:, :, None] * frequency
    sign = jnp.where(jnp.arange(HEAD) < HEAD // 2, -1.0, 1.0).astype(F32)
    cos, sin = jnp.cos(angles), jnp.sin(angles) * sign

    send, qk, tokens_f = project(place, group, w_qkv, cos, sin, gains_qk)
    far = lax.all_gather(after(piece, send), PLANE, axis=0, tiled=True)
    recv = exchange(send, CTX)
    my_starts = lax.dynamic_index_in_dim(starts_f, c // 8, 0, keepdims=False)
    meta = jnp.concatenate([(c % 4)[None].astype(jnp.int32), my_starts, jnp.zeros((2,), jnp.int32)])
    mixed_t, ot, lsum = attend(meta, recv)
    mixed_t = exchange(mixed_t, CTX)
    far = after(far, mixed_t)
    feed_weights = (
        w_gate,
        w_up,
        w_down,
        swap(w_gate, "core"),
        swap(w_up, "core"),
        swap(w_down, "core"),
        far,
        swap(far, "core"),
    )
    mixed, keep, give = merge(place, mixed_t, wo)
    got = swap(give, "core")
    last = swap((keep[1] + got[1].astype(F32)).astype(BF), "zh")
    result, d_hidden, d_branch, norms, parts, d_gains_am = feed(
        place, keep, got, last, inputs, cotangent.reshape(ROWS, 1024), gains_am, feed_weights
    )
    d_branches = relative(d_branch)
    drecv = exchange(split(place, d_branches, wo), CTX)

    norms = lax.all_gather(norms, COLUMN, axis=0, tiled=True)
    parts = exchange(after(parts, drecv), COLUMN).reshape(1024, 1152)
    back = attend_back(meta, recv, drecv, ot, lsum)
    parts = after(parts, back)
    back = exchange(after(back, parts), CTX)
    g_feed = feed_grads(parts, norms, mixed, d_branches)

    g_feed = exchange(after(g_feed, back), CTX)
    d_gains_am = d_gains_am.reshape(2, 4, 2, HEAD).swapaxes(0, 1).reshape(4, 4, HEAD)
    d_qkv, g_qkv = project_back(place, back, qk, cos, sin, gains_qk, d_gains_am, tokens_f)

    g_feed, g_qkv = lax.optimization_barrier((g_feed, g_qkv))
    g_feed = g_feed.reshape(16, 2, 26, 16, HEAD)
    g_out = jnp.sum(g_feed[:, :, 18:].astype(F32), axis=(0, 1)).astype(BF)
    g_feed = jnp.sum(g_feed[:, :, :18].astype(F32), axis=0).astype(BF)
    g_gu = g_feed[:, :12].reshape(2, 4, 3, 16, HEAD).swapaxes(0, 1)
    g_gu = [lax.dynamic_index_in_dim(g_gu, f ^ j, 0, keepdims=False) for j in range(4)]
    g_gu = absolute([g_gu[0], swap(g_gu[1], "core"), swap(g_gu[2], "zh"), flip(g_gu[3], FSDP)])
    g_feed = jnp.concatenate(
        [g_gu.reshape(24, 16, HEAD), g_feed[:, 12:].reshape(12, 16, HEAD), g_out], axis=0
    )
    g_feed = gather_ctx(g_feed.reshape(44 * 16, HEAD)).reshape(NCTX, 44, 16, HEAD)

    g_qkv = exchange(g_qkv, AXES)
    partial = dot_nt(d_qkv, w_qkv).reshape(4, ROWS, 1024)
    got = swap(jnp.stack([partial[1], partial[3]]).astype(BF), "core").astype(F32)
    last = swap((partial[2] + got[1]).astype(BF), "zh").astype(F32)
    d_inputs = d_hidden + partial[0] + got[0] + last

    g_qkv, d_inputs = lax.optimization_barrier((g_qkv, d_inputs))
    g_qkv = jnp.sum(g_qkv.reshape(NCTX, 4, 16, 640).astype(F32), axis=0)
    gains = jnp.sum(g_qkv[:, :, 512:], axis=0)
    g_qkv = g_qkv[:, :, :512].swapaxes(0, 1).reshape(16, 2048).astype(BF)
    g_qkv = exchange(jnp.broadcast_to(g_qkv[None], (NCTX, 16, 2048)), CTX)

    gate_grad, up_grad, down_grad, out_grad = feed_finish(g_feed)
    g_qkv = after(g_qkv, gate_grad)
    g_q, g_k, g_v = project_finish(g_qkv)
    gain_place = f * 32
    gain_q = lax.dynamic_slice_in_dim(gains[0], gain_place, 32, 0)
    gain_k = lax.dynamic_slice_in_dim(gains[1], gain_place, 32, 0)
    return (
        result.reshape(tokens.shape),
        d_inputs.reshape(tokens.shape),
        g_q,
        g_k,
        g_v,
        out_grad,
        gain_q,
        gain_k,
        gains[2:4].reshape(256),
        gate_grad,
        up_grad,
        down_grad,
        gains[4:6].reshape(256),
    )


def solution(mesh):
    whole = Mesh(mesh.devices.reshape(4, 4, 2, 2, 2), AXES)
    blocks = P(FSDP, None, CTX, None, None)
    rows = P(FSDP, None)
    vector = P(FSDP)
    return jax.shard_map(
        local,
        mesh=whole,
        in_specs=(
            blocks,
            blocks,
            rows,
            rows,
            rows,
            rows,
            rows,
            vector,
            vector,
            vector,
            rows,
            rows,
            rows,
            vector,
        ),
        out_specs=(
            blocks,
            blocks,
            rows,
            rows,
            rows,
            rows,
            vector,
            vector,
            vector,
            rows,
            rows,
            rows,
            vector,
        ),
        check_vma=False,
    )
```

```python
import math

import jax
import jax.numpy as jnp
from jax import lax
from jax.experimental import pallas as pl
from jax.experimental.pallas import tpu as pltpu
from jax.sharding import Mesh, PartitionSpec as P

HEADS = 16
KV_HEADS = 8
HEAD = 128
EPS = 1e-06
THETA = 500000.0

AXES = ("y", "x", "zl", "zh", "core")
CTX = ("y", "x", "zl")
PLANE = ("y", "x")
FSDP = ("zh", "core")
COLUMN = ("zl", "zh", "core")
NCTX = 32
SEQS = 4
BLOCK = 64
ROWS = 2 * BLOCK
LEN = 4096
DOCS = 5
PART = 32
TILES = 8
QT = 256
KT = 512
CHUNK = 192
BF = jnp.bfloat16
F32 = jnp.float32
SCALE = HEAD**-0.5
LOG2E = math.log2(math.e)


def key_block(j):
    return (j, 0) if j < NCTX else (2 * NCTX - 1 - j, 1)


def tile_bounds(meta, t):
    first, last = t * KT, t * KT + KT - 1
    low = jnp.int32(0)
    high = jnp.int32(0)
    for d in range(1, DOCS):
        start = meta[1 + d]
        low = jnp.where(start <= first, start, low)
        high = jnp.where(start <= last, start, high)
    return lax.div(low, KT), jnp.minimum(lax.div(high + (KT - 1), KT), t)


def row_places(meta, t):
    lane = lax.broadcasted_iota(jnp.int32, (1, QT), 1)
    place = t * KT + lax.div(lane, PART) * BLOCK + meta[0] * PART + lax.rem(lane, PART)
    start = jnp.zeros((1, QT), jnp.int32)
    for d in range(1, DOCS):
        start = jnp.where(place >= meta[1 + d], meta[1 + d], start)
    return place, start


def allowed(kt, place, start):
    key = kt * KT + lax.broadcasted_iota(jnp.int32, (KT, QT), 0)
    return (key <= place) & (key >= start)


def gather_rows(src, t):
    parts = []
    for i in range(8):
        c, b = key_block(8 * t + i)
        parts.append(src[c, pl.ds(b * PART, PART), :])
    return jnp.concatenate(parts, axis=0)


def sort_keys(src, dst):
    for j in range(2 * NCTX):
        c, b = key_block(j)
        dst[pl.ds(j * BLOCK, BLOCK), :] = src[c, pl.ds(64 + b * BLOCK, BLOCK), :]


def sort_both(meta, mine, other, ks, vs):
    @pl.when(meta[6] == 0)
    def _():
        sort_keys(mine, ks)
        sort_keys(other, vs)

    @pl.when(meta[6] != 0)
    def _():
        sort_keys(other, ks)
        sort_keys(mine, vs)


def put_rows(out, t, rows):
    for i in range(8):
        j = 8 * t + i
        half = (j >= NCTX).astype(jnp.int32)
        c = jnp.where(half == 0, j, 2 * NCTX - 1 - j)
        out[c, pl.ds(pl.multiple_of(half * PART, PART), PART), :] = rows[i * PART : (i + 1) * PART]


def transposed(x):
    return x.astype(F32).T.astype(x.dtype)


def forward_kernel(meta, mine, other, out, ot, lsum, ks, vs, vt, qt):
    sort_both(meta, mine, other, ks, vs)
    for i in range(TILES):
        vt[i] = transposed(vs[pl.ds(i * KT, KT), :])
        qt[i] = transposed(gather_rows(mine, i))

    def query_tile(t, _):
        q = qt[t]
        place, start = row_places(meta, t)
        low, clear = tile_bounds(meta, t)

        def step(kt, carry, masked):
            total, mixed = carry
            k = ks[pl.ds(pl.multiple_of(kt * KT, KT), KT), :]
            s = jnp.dot(k, q, preferred_element_type=F32)
            p = jnp.exp2(s * (SCALE * LOG2E))
            if masked:
                p = jnp.where(allowed(kt, place, start), p, 0.0)
            total = total + jnp.sum(p, axis=0, keepdims=True)
            mixed = mixed + jnp.dot(vt[kt], p.astype(BF), preferred_element_type=F32)
            return total, mixed

        carry = (jnp.zeros((1, QT), F32), jnp.zeros((HEAD, QT), F32))
        carry = lax.fori_loop(low, clear, lambda kt, cr: step(kt, cr, True), carry)
        carry = lax.fori_loop(jnp.maximum(low, clear), t, lambda kt, cr: step(kt, cr, False), carry)
        total, mixed = step(t, carry, True)
        mixed = mixed * (1.0 / total)
        ot[t] = mixed
        lsum[t] = total
        rows = mixed.T.astype(BF)
        put_rows(out, t, rows)
        return 0

    lax.fori_loop(0, TILES, query_tile, 0)


def backward_kernel(
    meta, mine, other, drecv, ot, lsum, out, keep, give, ks, vs, kt_, q_, qt, do_, dot_, dk, dv
):
    sort_both(meta, mine, other, ks, vs)
    for i in range(TILES):
        kt_[i] = transposed(ks[pl.ds(i * KT, KT), :])
        rows = gather_rows(mine, i)
        q_[i] = rows
        qt[i] = transposed(rows)
        rows = gather_rows(drecv, i)
        do_[i] = rows
        dot_[i] = transposed(rows)
    dk[...] = jnp.zeros_like(dk)
    dv[...] = jnp.zeros_like(dv)

    def query_tile(t, _):
        q, q_t, d, d_t = q_[t], qt[t], do_[t], dot_[t]
        place, start = row_places(meta, t)
        low, clear = tile_bounds(meta, t)
        delta = jnp.sum(d_t.astype(F32) * ot[t], axis=0, keepdims=True)
        shift = jnp.log2(lsum[t])

        def step(kt, total, masked):
            at = pl.ds(pl.multiple_of(kt * KT, KT), KT)
            s = jnp.dot(ks[at, :], q_t, preferred_element_type=F32)
            p = jnp.exp2(s * (SCALE * LOG2E) - shift)
            if masked:
                p = jnp.where(allowed(kt, place, start), p, 0.0)
            dv[at, :] += jnp.dot(p.astype(BF), d, preferred_element_type=F32)
            dp = jnp.dot(vs[at, :], d_t, preferred_element_type=F32)
            ds = (p * (dp - delta)).astype(BF)
            dk[at, :] += jnp.dot(ds, q, preferred_element_type=F32)
            return total + jnp.dot(kt_[kt], ds, preferred_element_type=F32)

        total = jnp.zeros((HEAD, QT), F32)
        total = lax.fori_loop(low, clear, lambda kt, cr: step(kt, cr, True), total)
        total = lax.fori_loop(jnp.maximum(low, clear), t, lambda kt, cr: step(kt, cr, False), total)
        total = step(t, total, True)
        rows = (total * SCALE).T.astype(BF)
        put_rows(out, t, rows)
        return 0

    lax.fori_loop(0, TILES, query_tile, 0)

    def unsort(src, scale, dst):
        for j in range(2 * NCTX):
            c, b = key_block(j)
            dst[c, pl.ds(b * BLOCK, BLOCK), :] = (src[pl.ds(j * BLOCK, BLOCK), :] * scale).astype(BF)

    @pl.when(meta[6] == 0)
    def _():
        unsort(dk, SCALE, keep)
        unsort(dv, 1.0, give)

    @pl.when(meta[6] != 0)
    def _():
        unsort(dv, 1.0, keep)
        unsort(dk, SCALE, give)


VMEM = pl.BlockSpec(memory_space=pltpu.VMEM)
SMEM = pl.BlockSpec(memory_space=pltpu.SMEM)
ANY = pl.BlockSpec(memory_space=pl.ANY)
PARAMS = pltpu.CompilerParams(vmem_limit_bytes=48 * 1024 * 1024)
LARGE = pltpu.CompilerParams(vmem_limit_bytes=60 * 1024 * 1024)


def attend(meta, mine, other):
    return pl.pallas_call(
        forward_kernel,
        out_shape=(
            jax.ShapeDtypeStruct((NCTX, 64, HEAD), BF),
            jax.ShapeDtypeStruct((TILES, HEAD, QT), F32),
            jax.ShapeDtypeStruct((TILES, 1, QT), F32),
        ),
        in_specs=[SMEM, VMEM, VMEM],
        out_specs=(VMEM, VMEM, VMEM),
        scratch_shapes=[
            pltpu.VMEM((LEN, HEAD), BF),
            pltpu.VMEM((LEN, HEAD), BF),
            pltpu.VMEM((TILES, HEAD, KT), BF),
            pltpu.VMEM((TILES, HEAD, QT), BF),
        ],
        compiler_params=PARAMS,
        cost_estimate=pl.CostEstimate(
            flops=15_000_000_000, bytes_accessed=5_000_000, transcendentals=4_700_000
        ),
        name="attention_forward",
    )(meta, mine, other)


def attend_back(meta, mine, other, drecv, ot, lsum):
    return pl.pallas_call(
        backward_kernel,
        out_shape=(
            jax.ShapeDtypeStruct((NCTX, 64, HEAD), BF),
            jax.ShapeDtypeStruct((NCTX, ROWS, HEAD), BF),
            jax.ShapeDtypeStruct((NCTX, ROWS, HEAD), BF),
        ),
        in_specs=[SMEM] + [VMEM] * 5,
        out_specs=(VMEM,) * 3,
        scratch_shapes=[
            pltpu.VMEM((LEN, HEAD), BF),
            pltpu.VMEM((LEN, HEAD), BF),
            pltpu.VMEM((TILES, HEAD, KT), BF),
            pltpu.VMEM((TILES, QT, HEAD), BF),
            pltpu.VMEM((TILES, HEAD, QT), BF),
            pltpu.VMEM((TILES, QT, HEAD), BF),
            pltpu.VMEM((TILES, HEAD, QT), BF),
            pltpu.VMEM((LEN, HEAD), F32),
            pltpu.VMEM((LEN, HEAD), F32),
        ],
        compiler_params=PARAMS,
        cost_estimate=pl.CostEstimate(
            flops=10_000_000, bytes_accessed=10_000, transcendentals=0
        ),
        name="attention_backward",
    )(meta, mine, other, drecv, ot, lsum)


def rms(u):
    return lax.rsqrt(jnp.mean(u * u, axis=-1, keepdims=True) + EPS)


def dot(a, b):
    return jnp.dot(a, b, preferred_element_type=F32)


def dot_nt(a, b):
    return lax.dot_general(a, b, (((1,), (1,)), ((), ())), preferred_element_type=F32)


def dot_tn(a, b):
    return lax.dot_general(a, b, (((0,), (0,)), ((), ())), preferred_element_type=F32)


def pack_kernel(at, x, docs, q_gain, k_gain, attn_gain, mlp_gain, gate, up, down, out, row, sem):
    copies = []
    for n in range(3):
        for src, row_at, lane_at, width in (
            (gate, 0, 1024 * n, 1024),
            (up, 0, 1024 * n, 1024),
            (down, 256 * n, 0, 1024),
        ):
            k = len(copies)
            first = pl.multiple_of(row_at + at[0] * 16, 16)
            copies.append(
                pltpu.make_async_copy(
                    src.at[pl.ds(first, 16), pl.ds(lane_at, width)],
                    out.at[pl.ds(144 + 16 * (3 * (k % 3) + n), 16), :],
                    sem.at[k],
                )
            )
            copies[-1].start()
    out[pl.ds(0, ROWS), :] = x[...]
    row[...] = jnp.zeros_like(row)
    row[:, pl.ds(0, 32)] = q_gain[...].astype(F32)
    row[:, pl.ds(128, 32)] = k_gain[...].astype(F32)
    lane = lax.broadcasted_iota(jnp.int32, (1, HEAD), 1)
    high = jnp.zeros((1, HEAD), F32)
    low = jnp.zeros((1, HEAD), F32)
    for d in range(1, DOCS):
        start = jnp.sum((docs[...] < d).astype(F32), axis=1, keepdims=True)
        whole = jnp.floor(start * (1.0 / 64.0))
        high = jnp.where(lane == d, whole, high)
        low = jnp.where(lane == d, start - whole * 64.0, low)
    row[:, pl.ds(256, HEAD)] = high
    row[:, pl.ds(384, HEAD)] = low
    row[:, pl.ds(512, 256)] = attn_gain[...].astype(F32)
    row[:, pl.ds(768, 256)] = mlp_gain[...].astype(F32)
    out[pl.ds(ROWS, 16), :] = jnp.broadcast_to(row[...], (16, 1024)).astype(BF)
    for copy in copies:
        copy.wait()


def pack_group(at, x, docs, gains, weights):
    return pl.pallas_call(
        pack_kernel,
        out_shape=jax.ShapeDtypeStruct((288, 1024), BF),
        in_specs=[SMEM] + [VMEM] * 6 + [ANY] * 3,
        out_specs=VMEM,
        scratch_shapes=[pltpu.VMEM((1, 1024), F32), pltpu.SemaphoreType.DMA((9,))],
        compiler_params=LARGE,
        name="pack_group",
    )(at, x, docs, *[g[None] for g in gains], *weights)


def deal_kernel(place, wq, wkv, own, near, far, sem):
    copies = []

    def columns(f, dst, rows):
        zh, core = lax.div(f, 2), lax.rem(f, 2)
        slices = [(wq, (8 * zh + 2 * n + core) * HEAD, HEAD, n * HEAD) for n in range(4)]
        for src, lane, width, at in slices + [(wkv, 1024 * core + 512 * zh, 512, 512)]:
            lanes = pl.ds(pl.multiple_of(lane, HEAD), width)
            copies.append(
                pltpu.make_async_copy(
                    src.at[rows, lanes], dst.at[:, pl.ds(at, width)], sem.at[len(copies)]
                )
            )
            copies[-1].start()

    quarter = pl.ds(pl.multiple_of(place[1] * 64, 64), 64)
    columns(place[0] ^ 2, far.at[0], quarter)
    columns(place[0] ^ 3, far.at[1], quarter)
    columns(place[0] ^ 1, near, pl.ds(0, 256))
    columns(place[0], own, pl.ds(0, 256))
    for copy in copies:
        copy.wait()


def deal(place, wq, wkv):
    return pl.pallas_call(
        deal_kernel,
        out_shape=(
            jax.ShapeDtypeStruct((256, 1024), BF),
            jax.ShapeDtypeStruct((256, 1024), BF),
            jax.ShapeDtypeStruct((2, 64, 1024), BF),
        ),
        in_specs=[SMEM] + [ANY] * 2,
        out_specs=(VMEM,) * 3,
        scratch_shapes=[pltpu.SemaphoreType.DMA((20,))],
        compiler_params=LARGE,
        name="deal",
    )(place, wq, wkv)


def project_kernel(place, group, own, near, far, cos, sin, gains, send, qk, tokens, w):
    w[pl.ds(pl.multiple_of(place[0] * 256, 256), 256), :] = own[...]
    w[pl.ds(pl.multiple_of((place[0] ^ 1) * 256, 256), 256), :] = near[...]
    for i in range(4):
        for k in range(2):
            at = pl.multiple_of((place[0] ^ (2 + k)) * 256 + 64 * i, 64)
            w[pl.ds(at, 64), :] = far[i, k]
    for j in range(4):
        n = place[0] ^ j
        base = n * 8
        rows = pl.ds(j * ROWS, ROWS)
        x = group[n, pl.ds(0, ROWS), :]
        tokens[rows, :] = x
        y = dot(x, w[...])
        c, s = cos[n], sin[n]
        qk[rows, :] = y
        core = lax.rem(place[0], 2)
        for h in range(8):
            v = y[:, h * HEAD : (h + 1) * HEAD]
            u = v * rms(v) * gains[pl.ds(h // 4, 1), :]
            u = u * c + pltpu.roll(u, HEAD // 2, 1) * s
            if h < 4:
                u = u.astype(BF)
                for half in range(2):
                    for b in range(2):
                        at = b * 64 + half * PART
                        send[base + h * 2 + half, pl.ds(b * PART, PART), :] = u[at : at + PART]
            else:
                u = jnp.where(core == 0, u, v).astype(BF)
                for half in range(2):
                    send[base + (h - 4) * 2 + half, pl.ds(64, ROWS), :] = u


def project(place, group, own, near, far, cos, sin, gains):
    return pl.pallas_call(
        project_kernel,
        out_shape=(
            jax.ShapeDtypeStruct((NCTX, CHUNK, HEAD), BF),
            jax.ShapeDtypeStruct((512, 1024), F32),
            jax.ShapeDtypeStruct((512, 1024), BF),
            jax.ShapeDtypeStruct((1024, 1024), BF),
        ),
        in_specs=[SMEM] + [VMEM] * 7,
        out_specs=(VMEM,) * 4,
        compiler_params=PARAMS,
        cost_estimate=pl.CostEstimate(
            flops=60_000_000_000, bytes_accessed=9_000_000, transcendentals=4000
        ),
        name="project",
    )(place, group, own, near, far, cos, sin, gains)


def project_back_kernel(place, back, qk, cos, sin, gains, dgains_am, tokens, out, send, grads):
    totals = [jnp.zeros((1, HEAD), F32), jnp.zeros((1, HEAD), F32)]
    for j in range(4):
        n = place[0] ^ j
        base = n * 8
        rows = pl.ds(j * ROWS, ROWS)
        c, s = cos[n], sin[n]
        core = lax.rem(place[0], 2)
        for h in range(8):
            at = base + h % 4 * 2
            if h < 4:
                parts = []
                for b in range(2):
                    for half in range(2):
                        parts.append(back[at + half, pl.ds(b * PART, PART), :])
                raw = jnp.concatenate(parts, axis=0).astype(F32)
            else:
                raw = back[at, pl.ds(64, ROWS), :].astype(F32)
                raw = raw + back[at + 1, pl.ds(64, ROWS), :].astype(F32)
            e = raw * c - pltpu.roll(raw, HEAD // 2, 1) * s
            u = qk[rows, pl.ds(h * HEAD, HEAD)]
            inverse = rms(u)
            u = u * inverse
            total = jnp.sum(e * u, axis=0, keepdims=True)
            if h >= 4:
                total = jnp.where(core == 0, total, 0.0)
            totals[h // 4] = totals[h // 4] + total
            e = e * gains[pl.ds(h // 4, 1), :]
            e = inverse * (e - u * jnp.mean(e * u, axis=-1, keepdims=True))
            if h >= 4:
                e = jnp.where(core == 0, e, raw)
            out[rows, pl.ds(h * HEAD, HEAD)] = e.astype(BF)
    grads[...] = dot_tn(tokens[...], out[...])
    for f in range(4):
        gain_rows = jnp.concatenate(
            totals + [dgains_am[f], jnp.zeros((10, HEAD), F32)], axis=0
        ).astype(BF)
        for p in range(16):
            for half in range(2):
                to = (p * 2 + half) * 4 + f
                send[to, :, pl.ds(0, 512)] = grads[
                    pl.ds(256 * f + 16 * p, 16), pl.ds(512 * half, 512)
                ].astype(BF)
                send[to, :, pl.ds(512, HEAD)] = gain_rows


def project_back(place, back, qk, cos, sin, gains, dgains_am, tokens):
    return pl.pallas_call(
        project_back_kernel,
        out_shape=(
            jax.ShapeDtypeStruct((512, 1024), BF),
            jax.ShapeDtypeStruct((128, 16, 640), BF),
        ),
        in_specs=[SMEM] + [VMEM] * 7,
        out_specs=(VMEM, VMEM),
        scratch_shapes=[pltpu.VMEM((1024, 1024), F32)],
        compiler_params=PARAMS,
        cost_estimate=pl.CostEstimate(
            flops=60_000_000_000, bytes_accessed=9_000_000, transcendentals=4000
        ),
        name="project_back",
    )(place, back, qk, cos, sin, gains, dgains_am, tokens)


def feed_grads_kernel(pa, norms, mixed, d0, d1, d2, d3, send, db, gu, down, out):
    for j, d in enumerate((d0, d1, d2, d3)):
        db[pl.ds(j * ROWS, ROWS), :] = d[...]
    out[...] = dot_tn(mixed[...], db[...])
    gu[...] = dot_tn(norms[:, pl.ds(0, 1024)], pa[:, pl.ds(384, 768)])
    down[...] = dot_tn(pa[:, pl.ds(0, 384)], norms[:, pl.ds(1024, 1024)])
    for to in range(NCTX):
        p, half = to // 2, to % 2

        def put(tile, ref, row, column):
            send[to, pl.ds(16 * tile, 16), :] = ref[pl.ds(row, 16), pl.ds(column, 128)].astype(BF)

        for f in range(4):
            for k in range(3):
                put(f * 3 + k, gu, 256 * f + 16 * p, 384 * half + 128 * k)
        for k in range(3):
            for i in range(2):
                put(12 + 2 * k + i, down, to // 4 * 48 + 16 * k, to % 4 * 256 + 128 * i)
        for b in range(2):
            for k in range(4):
                put(18 + 4 * b + k, out, 256 * b + 16 * p, 512 * half + 128 * k)


def feed_grads(parts, norms, mixed, d_branches):
    return pl.pallas_call(
        feed_grads_kernel,
        out_shape=jax.ShapeDtypeStruct((NCTX, 416, HEAD), BF),
        in_specs=[VMEM] * 7,
        out_specs=VMEM,
        scratch_shapes=[
            pltpu.VMEM((512, 1024), BF),
            pltpu.VMEM((1024, 768), F32),
            pltpu.VMEM((384, 1024), F32),
            pltpu.VMEM((512, 1024), F32),
        ],
        compiler_params=PARAMS,
        cost_estimate=pl.CostEstimate(
            flops=2_900_000_000, bytes_accessed=12_000_000, transcendentals=0
        ),
        name="feed_grads",
    )(parts, norms, mixed, *d_branches)


def feed_finish_kernel(tiles, gate, up, down, out):
    for c in range(NCTX):
        p, half = c // 2, c % 2
        for n in range(24):
            (up if half else gate)[pl.ds(16 * p, 16), pl.ds(128 * n, 128)] = tiles[c, n].astype(F32)
        for zl in range(2):
            for k in range(3):
                for i in range(2):
                    row = 384 * zl + c // 4 * 48 + 16 * k
                    down[pl.ds(row, 16), pl.ds(c % 4 * 256 + 128 * i, 128)] = tiles[
                        c, 24 + zl * 6 + 2 * k + i
                    ].astype(F32)
        for core in range(2):
            for k in range(4):
                row = 128 * (2 * (p // 8) + core) + 16 * (p % 8)
                out[pl.ds(row, 16), pl.ds(512 * half + 128 * k, 128)] = tiles[
                    c, 36 + 4 * core + k
                ].astype(F32)


def feed_finish(tiles):
    return pl.pallas_call(
        feed_finish_kernel,
        out_shape=(
            jax.ShapeDtypeStruct((256, 3072), F32),
            jax.ShapeDtypeStruct((256, 3072), F32),
            jax.ShapeDtypeStruct((768, 1024), F32),
            jax.ShapeDtypeStruct((512, 1024), F32),
        ),
        in_specs=[VMEM],
        out_specs=(VMEM,) * 4,
        compiler_params=PARAMS,
        cost_estimate=pl.CostEstimate(flops=0, bytes_accessed=18_000_000, transcendentals=0),
        name="feed_finish",
    )(tiles)


def project_finish_kernel(parts, gq, gk, gv):
    for p in range(16):
        rows = pl.ds(16 * p, 16)
        for f in range(4):
            zh, core = f // 2, f % 2
            for n in range(4):
                gq[rows, pl.ds((8 * zh + 2 * n + core) * HEAD, HEAD)] = parts[
                    2 * p, :, pl.ds(512 * f + HEAD * n, HEAD)
                ].astype(F32)
            (gv if core else gk)[rows, pl.ds(512 * zh, 512)] = parts[
                2 * p + 1, :, pl.ds(512 * f, 512)
            ].astype(F32)


def project_finish(parts):
    return pl.pallas_call(
        project_finish_kernel,
        out_shape=(
            jax.ShapeDtypeStruct((256, 2048), F32),
            jax.ShapeDtypeStruct((256, 1024), F32),
            jax.ShapeDtypeStruct((256, 1024), F32),
        ),
        in_specs=[VMEM],
        out_specs=(VMEM,) * 3,
        compiler_params=PARAMS,
        cost_estimate=pl.CostEstimate(flops=0, bytes_accessed=6_000_000, transcendentals=0),
        name="project_finish",
    )(parts)


def merge_kernel(place, recv, wo, mixed, keep, give):
    for j in range(4):
        base = (place[0] ^ j) * 8
        for h in range(4):
            parts = []
            for b in range(2):
                for half in range(2):
                    parts.append(recv[base + h * 2 + half, pl.ds(b * PART, PART), :])
            mixed[pl.ds(j * ROWS, ROWS), pl.ds(h * HEAD, HEAD)] = jnp.concatenate(parts, axis=0)
    for j in (1, 3, 0, 2):
        y = dot(mixed[pl.ds(j * ROWS, ROWS), :], wo[...])
        if j % 2:
            give[j // 2] = y.astype(BF)
        else:
            keep[j // 2] = y


def merge(place, recv, wo):
    return pl.pallas_call(
        merge_kernel,
        out_shape=(
            jax.ShapeDtypeStruct((512, 512), BF),
            jax.ShapeDtypeStruct((2, ROWS, 1024), F32),
            jax.ShapeDtypeStruct((2, ROWS, 1024), BF),
        ),
        in_specs=[SMEM] + [VMEM] * 2,
        out_specs=(VMEM, VMEM, VMEM),
        compiler_params=PARAMS,
        cost_estimate=pl.CostEstimate(
            flops=540_000_000, bytes_accessed=4_000_000, transcendentals=0
        ),
        name="merge",
    )(place, recv, wo)


def split_kernel(place, d0, d1, d2, d3, wo, send):
    for j, d in enumerate((d0, d1, d2, d3)):
        base = (place[0] ^ j) * 8
        y = dot_nt(d[...], wo[...]).astype(BF)
        for h in range(4):
            for b in range(2):
                for half in range(2):
                    at = b * 64 + half * PART
                    send[base + h * 2 + half, pl.ds(b * PART, PART), :] = y[
                        at : at + PART, h * HEAD : (h + 1) * HEAD
                    ]


def split(place, ds, wo):
    return pl.pallas_call(
        split_kernel,
        out_shape=jax.ShapeDtypeStruct((NCTX, 64, HEAD), BF),
        in_specs=[SMEM] + [VMEM] * 5,
        out_specs=VMEM,
        compiler_params=PARAMS,
        cost_estimate=pl.CostEstimate(
            flops=10_000_000, bytes_accessed=10_000, transcendentals=0
        ),
        name="split",
    )(place, *ds, wo)


def feed_kernel(
    place,
    a,
    hidden,
    x,
    g,
    gains,
    gate0,
    up0,
    down0,
    gate1,
    up1,
    down1,
    cat2,
    cat3,
    result,
    d_hidden,
    d_branch,
    norms,
    eighths,
    dgains,
    w,
    sems,
    parts,
    hb,
    gate,
    up,
    dh,
):
    copies = []

    def fetch(src, dst):
        copy = pltpu.make_async_copy(src, dst, sems.at[len(copies)])
        copy.start()
        copies.append(copy)

    for j, (gate_src, up_src) in enumerate(((gate0, up0), (gate1, up1))):
        fetch(gate_src, w.at[j, :, :, pl.ds(0, 3072)])
        fetch(up_src, w.at[j, :, :, pl.ds(3072, 3072)])
    for n in range(6):
        for j, src in ((2, cat2), (3, cat3)):
            fetch(src.at[:, pl.ds(16 * n, 16), :], w.at[j, :, :, pl.ds(1024 * n, 1024)])
    first_needed = len(copies)
    for n in range(3):
        at = pl.ds(6144 + 1024 * n, 1024)
        for j, src in ((0, down0), (1, down1)):
            fetch(src.at[pl.ds(16 * n, 16), :, :], w.at[j, :, :, at])
        for j, src in ((2, cat2), (3, cat3)):
            fetch(src.at[:, pl.ds(96 + 16 * n, 16), :], w.at[j, :, :, at])

    def rows_of(j, at, width):
        return w[j, :, :, pl.ds(at, width)].reshape(256, width)

    me = place[0]
    gain_a, gain_m = gains[pl.ds(0, 1), :], gains[pl.ds(1, 1), :]
    inverse_a = rms(a[...])
    normed_a = a[...] * inverse_a
    h = x[...].astype(F32) + normed_a * gain_a
    for n in range(4):
        hb[n] = hidden[:, pl.ds(256 * n, 256)]
    norms[:, pl.ds(0, 1024)] = hidden[...]
    for copy in copies[:first_needed]:
        copy.wait()
    for n in range(4):
        at = 768 * n
        u = dot(hb[me], rows_of(0, at, 768))
        v = dot(hb[me], rows_of(0, 3072 + at, 768))
        for j in range(1, 4):
            u = u + dot(hb[me ^ j], rows_of(j, at, 768))
            v = v + dot(hb[me ^ j], rows_of(j, 3072 + at, 768))
        gate[n] = u
        up[n] = v
        parts[n, :, pl.ds(0, 768)] = (u / (1.0 + jnp.exp(-u)) * v).astype(BF)
    for copy in copies[first_needed:]:
        copy.wait()
    z = jnp.zeros((ROWS, 1024), F32)
    for j in range(4):
        for b in range(3):
            z = z + dot(
                parts[me ^ j, :, pl.ds(256 * b, 256)], rows_of(j, 6144 + 1024 * b, 1024)
            )
    inverse_z = rms(z)
    normed_z = z * inverse_z
    result[...] = (h + normed_z * gain_m).astype(BF)
    e = g[...].astype(F32)
    dgains[pl.ds(1, 1), :] = jnp.sum(e * normed_z, axis=0, keepdims=True)
    weighted = e * gain_m
    dz = inverse_z * (weighted - normed_z * jnp.mean(weighted * normed_z, axis=-1, keepdims=True))
    dz = dz.astype(BF)
    norms[:, pl.ds(1024, 1024)] = dz
    for j in range(4):
        n = me ^ j
        for b in range(3):
            at = pl.ds(256 * b, 256)
            d_act = dot_nt(dz, rows_of(j, 6144 + 1024 * b, 1024))
            u, v = gate[n, :, at], up[n, :, at]
            s = 1.0 / (1.0 + jnp.exp(-u))
            parts[n, :, pl.ds(768 + 256 * b, 256)] = (
                d_act * v * (s * (1.0 + u * (1.0 - s)))
            ).astype(BF)
            parts[n, :, pl.ds(1536 + 256 * b, 256)] = (d_act * (u * s)).astype(BF)
    for n in range(8):
        for k in range(3):
            eighths[n, :, pl.ds(384 * k, 384)] = parts[
                n % 4, :, pl.ds(768 * k + 384 * (n // 4), 384)
            ]
    for j in range(4):
        total = jnp.zeros((ROWS, 256), F32)
        for n in range(4):
            total = total + dot_nt(parts[n, :, pl.ds(768, 768)], rows_of(j, 768 * n, 768))
            total = total + dot_nt(
                parts[n, :, pl.ds(1536, 768)], rows_of(j, 3072 + 768 * n, 768)
            )
        dh[me ^ j] = total
    total = g[...].astype(F32) + jnp.concatenate([dh[n] for n in range(4)], axis=1)
    d_hidden[...] = total
    dgains[pl.ds(0, 1), :] = jnp.sum(total * normed_a, axis=0, keepdims=True)
    weighted = total * gain_a
    d_branch[...] = (
        inverse_a * (weighted - normed_a * jnp.mean(weighted * normed_a, axis=-1, keepdims=True))
    ).astype(BF)


def feed(place, a, hidden, x, g, gains, weights):
    return pl.pallas_call(
        feed_kernel,
        out_shape=(
            jax.ShapeDtypeStruct((ROWS, 1024), BF),
            jax.ShapeDtypeStruct((ROWS, 1024), F32),
            jax.ShapeDtypeStruct((ROWS, 1024), BF),
            jax.ShapeDtypeStruct((ROWS, 2048), BF),
            jax.ShapeDtypeStruct((8, ROWS, 1152), BF),
            jax.ShapeDtypeStruct((2, 1024), F32),
        ),
        in_specs=[SMEM] + [VMEM] * 5 + [ANY] * 8,
        out_specs=(VMEM,) * 6,
        scratch_shapes=[
            pltpu.VMEM((4, 16, 16, 9216), BF),
            pltpu.SemaphoreType.DMA((28,)),
            pltpu.VMEM((4, ROWS, 2304), BF),
            pltpu.VMEM((4, ROWS, 256), BF),
            pltpu.VMEM((4, ROWS, 768), F32),
            pltpu.VMEM((4, ROWS, 768), F32),
            pltpu.VMEM((4, ROWS, 256), F32),
        ],
        compiler_params=LARGE,
        cost_estimate=pl.CostEstimate(
            flops=10_000_000, bytes_accessed=10_000, transcendentals=0
        ),
        name="feed_forward",
    )(
        place,
        a,
        hidden,
        x,
        g,
        gains,
        *[v.reshape(-1, 16, v.shape[1]) for v in weights[:6]],
        *[v.reshape(16, -1, 1024) for v in weights[6:]],
    )


SWAP = [(0, 1), (1, 0)]


def swap(x, axis):
    return lax.ppermute(x, axis, SWAP)


def flip(x, axes):
    n = 2 ** len(axes)
    return lax.ppermute(x, axes, [(i, n - 1 - i) for i in range(n)])


def in_order(place, own, other):
    return jnp.where(place == 0, jnp.stack([own, other]), jnp.stack([other, own]))


def relative(x):
    far = swap(x, "zh")
    return [x, swap(x, "core"), far, swap(far, "core")]


def absolute(four):
    zh, core = lax.axis_index("zh"), lax.axis_index("core")
    near = in_order(core, four[0], four[1])
    far = in_order(core, four[2], four[3])
    return in_order(zh, near, far).reshape((4,) + four[0].shape)


def exchange(x, axes):
    return lax.all_to_all(x, axes, split_axis=0, concat_axis=0, tiled=True)


def after(xs, *others):
    return lax.optimization_barrier((xs,) + others)[0]


def local(
    tokens,
    cotangent,
    doc_ids,
    wq,
    wk,
    wv,
    wo,
    q_gain,
    k_gain,
    attn_gain,
    w_gate,
    w_up,
    w_down,
    mlp_gain,
):
    c = lax.axis_index(CTX)
    f = lax.axis_index(FSDP)
    place = f[None].astype(jnp.int32)
    inputs = tokens.reshape(ROWS, 1024)

    core = lax.axis_index("core")
    wkv = jnp.concatenate([wk, wv], axis=1)
    own, near, quarter = deal(jnp.stack([f, lax.axis_index("x")]).astype(jnp.int32), wq, wkv)
    near = swap(near, "core")
    quarter = swap(quarter, "zh")
    quarter = jnp.stack([quarter[0], swap(quarter[1], "core")])
    quarter = exchange(jnp.broadcast_to(quarter[None], (4, 2, 64, 1024)), ("x",))

    spot = lax.axis_index("y") * 4 + lax.axis_index("x")
    pack = pack_group(
        spot[None].astype(jnp.int32),
        inputs,
        doc_ids,
        (q_gain, k_gain, attn_gain, mlp_gain),
        (w_gate, w_up, w_down),
    )
    group = lax.all_gather(pack, FSDP, axis=0, tiled=True).reshape(4, 288, 1024)
    gains = group[:, ROWS].astype(F32)
    gains_qk = jnp.stack([gains[:, :32].reshape(HEAD), gains[:, 128:160].reshape(HEAD)])
    gains_am = jnp.stack([gains[:, 512:768].reshape(1024), gains[:, 768:].reshape(1024)])
    starts_f = (gains[:, 256:261] * 64.0 + gains[:, 384:389]).astype(jnp.int32)
    far = lax.dynamic_slice(group, (f ^ 2, ROWS + 16, 0), (1, 144, 1024))[0]
    far = lax.all_gather(far, PLANE, axis=0, tiled=True)

    step = jnp.arange(BLOCK, dtype=jnp.int32)
    spot = jnp.concatenate([c * BLOCK + step, (2 * NCTX - 1 - c) * BLOCK + step])
    start = jnp.max(
        jnp.where(starts_f[:, :, None] <= spot[None, None, :], starts_f[:, :, None], 0), axis=1
    )
    position = spot[None, :] - start
    half = jnp.arange(HEAD, dtype=jnp.int32) % (HEAD // 2)
    frequency = jnp.exp(half.astype(F32) * (-2.0 * math.log(THETA) / HEAD))
    angles = position.astype(F32)[:, :, None] * frequency
    sign = jnp.where(jnp.arange(HEAD) < HEAD // 2, -1.0, 1.0).astype(F32)
    cos, sin = jnp.cos(angles), jnp.sin(angles) * sign

    send, qk, tokens_f, w_qkv = project(place, group, own, near, quarter, cos, sin, gains_qk)
    recv = exchange(send, CTX)
    near = (swap(w_gate, "core"), swap(w_up, "core"), swap(w_down, "core"))
    pairs = wo.reshape(2, 2, HEAD, 1024)
    heads = lax.dynamic_index_in_dim(pairs, core, 1, keepdims=False)
    others = swap(lax.dynamic_index_in_dim(pairs, 1 - core, 1, keepdims=False), "core")
    wo = in_order(core, heads, others).reshape(512, 1024)
    recv, near, wo = lax.optimization_barrier((recv, near, wo))
    other = swap(recv, "core")
    my_starts = lax.dynamic_index_in_dim(starts_f, c // 8, 0, keepdims=False)
    meta = [(c % 2)[None].astype(jnp.int32), my_starts, core[None].astype(jnp.int32)]
    meta = jnp.concatenate(meta + [jnp.zeros((1,), jnp.int32)])
    mixed_t, ot, lsum = attend(meta, recv, other)
    far = after(far, mixed_t)
    mixed_t = exchange(mixed_t, CTX)
    feed_weights = (
        w_gate,
        w_up,
        w_down,
        *near,
        far,
        swap(far, "core"),
    )
    mixed, keep, give = merge(place, mixed_t, wo)
    got = swap(give, "core")
    last = swap((keep[1] + got[1].astype(F32)).astype(BF), "zh")
    branch = keep[0] + got[0].astype(F32) + last.astype(F32)
    hidden = branch * rms(branch) * gains_am[0] + inputs.astype(F32)
    hidden = hidden.astype(BF)
    result, d_hidden, d_branch, norms, parts, d_gains_am = feed(
        place, branch, hidden, inputs, cotangent.reshape(ROWS, 1024), gains_am, feed_weights
    )
    norms = lax.all_gather(norms, COLUMN, axis=0, tiled=True)
    d_branches = relative(d_branch)
    drecv = exchange(split(place, d_branches, wo), CTX)

    parts = exchange(after(parts, drecv), COLUMN).reshape(1024, 1152)
    dq, keep, give = attend_back(meta, recv, other, drecv, ot, lsum)
    keep = (keep.astype(F32) + swap(give, "core").astype(F32)).astype(BF)
    back = jnp.concatenate([dq, keep], axis=1)
    parts = after(parts, back)
    g_feed = feed_grads(parts, norms, mixed, d_branches)
    g_feed = exchange(g_feed, CTX)
    back = exchange(after(back, g_feed), CTX)

    d_gains_am = d_gains_am.reshape(2, 4, 2, HEAD).swapaxes(0, 1).reshape(4, 4, HEAD)
    d_qkv, g_qkv = project_back(place, back, qk, cos, sin, gains_qk, d_gains_am, tokens_f)

    g_feed = g_feed.reshape(16, 2, 26, 16, HEAD)
    g_out = jnp.sum(g_feed[:, :, 18:].astype(F32), axis=(0, 1)).astype(BF).reshape(2, 4, 16, HEAD)
    others = swap(lax.dynamic_index_in_dim(g_out, 1 - core, 0, keepdims=False), "core")
    g_out = lax.dynamic_index_in_dim(g_out, core, 0, keepdims=False)
    g_out = in_order(core, g_out, others).reshape(8, 16, HEAD)
    g_feed = jnp.sum(g_feed[:, :, :18].astype(F32), axis=0).astype(BF)
    g_gu = g_feed[:, :12].reshape(2, 4, 3, 16, HEAD).swapaxes(0, 1)
    g_gu = [lax.dynamic_index_in_dim(g_gu, f ^ j, 0, keepdims=False) for j in range(4)]
    g_gu = absolute([g_gu[0], swap(g_gu[1], "core"), swap(g_gu[2], "zh"), flip(g_gu[3], FSDP)])
    g_feed = jnp.concatenate(
        [g_gu.reshape(24, 16, HEAD), g_feed[:, 12:].reshape(12, 16, HEAD), g_out], axis=0
    ).reshape(704, HEAD)
    g_feed = in_order(lax.axis_index("zl"), g_feed, swap(g_feed, "zl"))
    g_feed = lax.all_gather(g_feed, PLANE, axis=0, tiled=True).reshape(NCTX, 44, 16, HEAD)

    g_qkv = exchange(g_qkv, AXES)
    partial = dot_nt(d_qkv, w_qkv).reshape(4, ROWS, 1024)
    got = swap(jnp.stack([partial[1], partial[3]]).astype(BF), "core").astype(F32)
    last = swap((partial[2] + got[1]).astype(BF), "zh").astype(F32)
    d_inputs = d_hidden + partial[0] + got[0] + last

    g_qkv, d_inputs = lax.optimization_barrier((g_qkv, d_inputs))
    g_qkv = jnp.sum(g_qkv.reshape(NCTX, 4, 16, 640).astype(F32), axis=0)
    gains = jnp.sum(g_qkv[:, :, 512:], axis=0)
    g_qkv = g_qkv[:, :, :512].swapaxes(0, 1).reshape(16, 2048).astype(BF)
    g_qkv = exchange(jnp.broadcast_to(g_qkv[None], (NCTX, 16, 2048)), CTX)

    gate_grad, up_grad, down_grad, out_grad = feed_finish(g_feed)
    g_q, g_k, g_v = project_finish(after(g_qkv, gate_grad))
    gain_place = f * 32
    gain_q = lax.dynamic_slice_in_dim(gains[0], gain_place, 32, 0)
    gain_k = lax.dynamic_slice_in_dim(gains[1], gain_place, 32, 0)
    return (
        result.reshape(tokens.shape),
        d_inputs.reshape(tokens.shape),
        g_q,
        g_k,
        g_v,
        out_grad,
        gain_q,
        gain_k,
        gains[2:4].reshape(256),
        gate_grad,
        up_grad,
        down_grad,
        gains[4:6].reshape(256),
    )


def solution(mesh):
    whole = Mesh(mesh.devices.reshape(4, 4, 2, 2, 2), AXES)
    blocks = P(FSDP, None, CTX, None, None)
    rows = P(FSDP, None)
    vector = P(FSDP)
    return jax.shard_map(
        local,
        mesh=whole,
        in_specs=(
            blocks,
            blocks,
            rows,
            rows,
            rows,
            rows,
            rows,
            vector,
            vector,
            vector,
            rows,
            rows,
            rows,
            vector,
        ),
        out_specs=(
            blocks,
            blocks,
            rows,
            rows,
            rows,
            rows,
            vector,
            vector,
            vector,
            rows,
            rows,
            rows,
            vector,
        ),
        check_vma=False,
    )
```

```python
import math

import jax
import jax.numpy as jnp
from jax import lax
from jax.experimental import pallas as pl
from jax.experimental.pallas import tpu as pltpu
from jax.sharding import Mesh, PartitionSpec as P

HEADS = 16
KV_HEADS = 8
HEAD = 128
EPS = 1e-06
THETA = 500000.0

AXES = ("y", "x", "zl", "zh", "core")
CTX = ("y", "x", "zl")
PLANE = ("y", "x")
FSDP = ("zh", "core")
COLUMN = ("zl", "zh", "core")
NCTX = 32
SEQS = 4
BLOCK = 64
ROWS = 2 * BLOCK
LEN = 4096
DOCS = 5
PART = 32
TILES = 8
QT = 256
KT = 512
CHUNK = 192
BF = jnp.bfloat16
F32 = jnp.float32
SCALE = HEAD**-0.5
LOG2E = math.log2(math.e)


def key_block(j):
    return (j, 0) if j < NCTX else (2 * NCTX - 1 - j, 1)


def tile_bounds(meta, t):
    first, last = t * KT, t * KT + KT - 1
    low = jnp.int32(0)
    high = jnp.int32(0)
    for d in range(1, DOCS):
        start = meta[1 + d]
        low = jnp.where(start <= first, start, low)
        high = jnp.where(start <= last, start, high)
    return lax.div(low, KT), jnp.minimum(lax.div(high + (KT - 1), KT), t)


def row_places(meta, t):
    lane = lax.broadcasted_iota(jnp.int32, (1, QT), 1)
    place = t * KT + lax.div(lane, PART) * BLOCK + meta[0] * PART + lax.rem(lane, PART)
    start = jnp.zeros((1, QT), jnp.int32)
    for d in range(1, DOCS):
        start = jnp.where(place >= meta[1 + d], meta[1 + d], start)
    return place, start


def allowed(kt, place, start):
    key = kt * KT + lax.broadcasted_iota(jnp.int32, (KT, QT), 0)
    return (key <= place) & (key >= start)


def gather_rows(src, t):
    parts = []
    for i in range(8):
        c, b = key_block(8 * t + i)
        parts.append(src[c, pl.ds(b * PART, PART), :])
    return jnp.concatenate(parts, axis=0)


def sort_keys(src, dst):
    for j in range(2 * NCTX):
        c, b = key_block(j)
        dst[pl.ds(j * BLOCK, BLOCK), :] = src[c, pl.ds(64 + b * BLOCK, BLOCK), :]


def sort_both(meta, mine, other, ks, vs):
    @pl.when(meta[6] == 0)
    def _():
        sort_keys(mine, ks)
        sort_keys(other, vs)

    @pl.when(meta[6] != 0)
    def _():
        sort_keys(other, ks)
        sort_keys(mine, vs)


def put_rows(out, t, rows):
    for i in range(8):
        j = 8 * t + i
        half = (j >= NCTX).astype(jnp.int32)
        c = jnp.where(half == 0, j, 2 * NCTX - 1 - j)
        out[c, pl.ds(pl.multiple_of(half * PART, PART), PART), :] = rows[i * PART : (i + 1) * PART]


def transposed(x):
    return x.astype(F32).T.astype(x.dtype)


def forward_kernel(meta, mine, other, out, ot, lsum, ks, vs, vt, qt):
    sort_both(meta, mine, other, ks, vs)
    for i in range(TILES):
        vt[i] = transposed(vs[pl.ds(i * KT, KT), :])
        qt[i] = transposed(gather_rows(mine, i))

    def query_tile(t, _):
        q = qt[t]
        place, start = row_places(meta, t)
        low, clear = tile_bounds(meta, t)

        def step(kt, carry, masked):
            total, mixed = carry
            k = ks[pl.ds(pl.multiple_of(kt * KT, KT), KT), :]
            s = jnp.dot(k, q, preferred_element_type=F32)
            p = jnp.exp2(s * (SCALE * LOG2E))
            if masked:
                p = jnp.where(allowed(kt, place, start), p, 0.0)
            total = total + jnp.sum(p, axis=0, keepdims=True)
            mixed = mixed + jnp.dot(vt[kt], p.astype(BF), preferred_element_type=F32)
            return total, mixed

        carry = (jnp.zeros((1, QT), F32), jnp.zeros((HEAD, QT), F32))
        carry = lax.fori_loop(low, clear, lambda kt, cr: step(kt, cr, True), carry)
        carry = lax.fori_loop(jnp.maximum(low, clear), t, lambda kt, cr: step(kt, cr, False), carry)
        total, mixed = step(t, carry, True)
        mixed = mixed * (1.0 / total)
        ot[t] = mixed
        lsum[t] = total
        rows = mixed.T.astype(BF)
        put_rows(out, t, rows)
        return 0

    lax.fori_loop(0, TILES, query_tile, 0)


def backward_kernel(
    meta, mine, other, drecv, ot, lsum, out, keep, give, ks, vs, kt_, q_, qt, do_, dot_, dk, dv
):
    sort_both(meta, mine, other, ks, vs)
    for i in range(TILES):
        kt_[i] = transposed(ks[pl.ds(i * KT, KT), :])
        rows = gather_rows(mine, i)
        q_[i] = rows
        qt[i] = transposed(rows)
        rows = gather_rows(drecv, i)
        do_[i] = rows
        dot_[i] = transposed(rows)
    dk[...] = jnp.zeros_like(dk)
    dv[...] = jnp.zeros_like(dv)

    def query_tile(t, _):
        q, q_t, d, d_t = q_[t], qt[t], do_[t], dot_[t]
        place, start = row_places(meta, t)
        low, clear = tile_bounds(meta, t)
        delta = jnp.sum(d_t.astype(F32) * ot[t], axis=0, keepdims=True)
        shift = jnp.log2(lsum[t])

        def step(kt, total, masked):
            at = pl.ds(pl.multiple_of(kt * KT, KT), KT)
            s = jnp.dot(ks[at, :], q_t, preferred_element_type=F32)
            p = jnp.exp2(s * (SCALE * LOG2E) - shift)
            if masked:
                p = jnp.where(allowed(kt, place, start), p, 0.0)
            dv[at, :] += jnp.dot(p.astype(BF), d, preferred_element_type=F32)
            dp = jnp.dot(vs[at, :], d_t, preferred_element_type=F32)
            ds = (p * (dp - delta)).astype(BF)
            dk[at, :] += jnp.dot(ds, q, preferred_element_type=F32)
            return total + jnp.dot(kt_[kt], ds, preferred_element_type=F32)

        total = jnp.zeros((HEAD, QT), F32)
        total = lax.fori_loop(low, clear, lambda kt, cr: step(kt, cr, True), total)
        total = lax.fori_loop(jnp.maximum(low, clear), t, lambda kt, cr: step(kt, cr, False), total)
        total = step(t, total, True)
        rows = (total * SCALE).T.astype(BF)
        put_rows(out, t, rows)
        return 0

    lax.fori_loop(0, TILES, query_tile, 0)

    def unsort(src, scale, dst):
        for j in range(2 * NCTX):
            c, b = key_block(j)
            dst[c, pl.ds(b * BLOCK, BLOCK), :] = (src[pl.ds(j * BLOCK, BLOCK), :] * scale).astype(BF)

    @pl.when(meta[6] == 0)
    def _():
        unsort(dk, SCALE, keep)
        unsort(dv, 1.0, give)

    @pl.when(meta[6] != 0)
    def _():
        unsort(dv, 1.0, keep)
        unsort(dk, SCALE, give)


VMEM = pl.BlockSpec(memory_space=pltpu.VMEM)
SMEM = pl.BlockSpec(memory_space=pltpu.SMEM)
ANY = pl.BlockSpec(memory_space=pl.ANY)
PARAMS = pltpu.CompilerParams(vmem_limit_bytes=48 * 1024 * 1024)
LARGE = pltpu.CompilerParams(vmem_limit_bytes=60 * 1024 * 1024)


def attend(meta, mine, other):
    return pl.pallas_call(
        forward_kernel,
        out_shape=(
            jax.ShapeDtypeStruct((NCTX, 64, HEAD), BF),
            jax.ShapeDtypeStruct((TILES, HEAD, QT), F32),
            jax.ShapeDtypeStruct((TILES, 1, QT), F32),
        ),
        in_specs=[SMEM, VMEM, VMEM],
        out_specs=(VMEM, VMEM, VMEM),
        scratch_shapes=[
            pltpu.VMEM((LEN, HEAD), BF),
            pltpu.VMEM((LEN, HEAD), BF),
            pltpu.VMEM((TILES, HEAD, KT), BF),
            pltpu.VMEM((TILES, HEAD, QT), BF),
        ],
        compiler_params=PARAMS,
        cost_estimate=pl.CostEstimate(
            flops=15_000_000_000, bytes_accessed=5_000_000, transcendentals=4_700_000
        ),
        name="attention_forward",
    )(meta, mine, other)


def attend_back(meta, mine, other, drecv, ot, lsum):
    return pl.pallas_call(
        backward_kernel,
        out_shape=(
            jax.ShapeDtypeStruct((NCTX, 64, HEAD), BF),
            jax.ShapeDtypeStruct((NCTX, ROWS, HEAD), BF),
            jax.ShapeDtypeStruct((NCTX, ROWS, HEAD), BF),
        ),
        in_specs=[SMEM] + [VMEM] * 5,
        out_specs=(VMEM,) * 3,
        scratch_shapes=[
            pltpu.VMEM((LEN, HEAD), BF),
            pltpu.VMEM((LEN, HEAD), BF),
            pltpu.VMEM((TILES, HEAD, KT), BF),
            pltpu.VMEM((TILES, QT, HEAD), BF),
            pltpu.VMEM((TILES, HEAD, QT), BF),
            pltpu.VMEM((TILES, QT, HEAD), BF),
            pltpu.VMEM((TILES, HEAD, QT), BF),
            pltpu.VMEM((LEN, HEAD), F32),
            pltpu.VMEM((LEN, HEAD), F32),
        ],
        compiler_params=PARAMS,
        cost_estimate=pl.CostEstimate(
            flops=10_000_000, bytes_accessed=10_000, transcendentals=0
        ),
        name="attention_backward",
    )(meta, mine, other, drecv, ot, lsum)


def rms(u):
    return lax.rsqrt(jnp.mean(u * u, axis=-1, keepdims=True) + EPS)


def dot(a, b):
    return jnp.dot(a, b, preferred_element_type=F32)


def dot_nt(a, b):
    return lax.dot_general(a, b, (((1,), (1,)), ((), ())), preferred_element_type=F32)


def dot_tn(a, b):
    return lax.dot_general(a, b, (((0,), (0,)), ((), ())), preferred_element_type=F32)


def pack_kernel(at, x, docs, q_gain, k_gain, am_gain, gate, up, down, out, row, sem):
    copies = []
    for n in range(3):
        for src, row_at, lane_at, width in (
            (gate, 0, 1024 * n, 1024),
            (up, 0, 1024 * n, 1024),
            (down, 256 * n, 0, 1024),
        ):
            k = len(copies)
            first = pl.multiple_of(row_at + at[0] * 16, 16)
            copies.append(
                pltpu.make_async_copy(
                    src.at[pl.ds(first, 16), pl.ds(lane_at, width)],
                    out.at[pl.ds(144 + 16 * (3 * (k % 3) + n), 16), :],
                    sem.at[k],
                )
            )
            copies[-1].start()
    out[pl.ds(0, ROWS), :] = x[...]
    row[...] = jnp.zeros_like(row)
    row[:, pl.ds(0, 32)] = q_gain[...].astype(F32)
    row[:, pl.ds(128, 32)] = k_gain[...].astype(F32)
    lane = lax.broadcasted_iota(jnp.int32, (1, HEAD), 1)
    high = jnp.zeros((1, HEAD), F32)
    low = jnp.zeros((1, HEAD), F32)
    for d in range(1, DOCS):
        start = jnp.sum((docs[...] < d).astype(F32), axis=1, keepdims=True)
        whole = jnp.floor(start * (1.0 / 64.0))
        high = jnp.where(lane == d, whole, high)
        low = jnp.where(lane == d, start - whole * 64.0, low)
    row[:, pl.ds(256, HEAD)] = high
    row[:, pl.ds(384, HEAD)] = low
    row[:, pl.ds(512, 256)] = am_gain[pl.ds(0, 1), :].astype(F32)
    row[:, pl.ds(768, 256)] = am_gain[pl.ds(1, 1), :].astype(F32)
    out[pl.ds(ROWS, 16), :] = jnp.broadcast_to(row[...], (16, 1024)).astype(BF)
    for copy in copies:
        copy.wait()


def pack_group(at, x, docs, gains, weights):
    return pl.pallas_call(
        pack_kernel,
        out_shape=jax.ShapeDtypeStruct((288, 1024), BF),
        in_specs=[SMEM] + [VMEM] * 5 + [ANY] * 3,
        out_specs=VMEM,
        scratch_shapes=[pltpu.VMEM((1, 1024), F32), pltpu.SemaphoreType.DMA((9,))],
        compiler_params=LARGE,
        name="pack_group",
    )(at, x, docs, *gains, *weights)


def deal_kernel(place, wq, wkv, own, near, far, sem):
    copies = []

    def columns(f, dst, rows):
        zh, core = lax.div(f, 2), lax.rem(f, 2)
        slices = [(wq, (8 * zh + 2 * n + core) * HEAD, HEAD, n * HEAD) for n in range(4)]
        for src, lane, width, at in slices + [(wkv, 1024 * core + 512 * zh, 512, 512)]:
            lanes = pl.ds(pl.multiple_of(lane, HEAD), width)
            copies.append(
                pltpu.make_async_copy(
                    src.at[rows, lanes], dst.at[:, pl.ds(at, width)], sem.at[len(copies)]
                )
            )
            copies[-1].start()

    quarter = pl.ds(pl.multiple_of(place[1] * 64, 64), 64)
    columns(place[0] ^ 2, far.at[0], quarter)
    columns(place[0] ^ 3, far.at[1], quarter)
    columns(place[0] ^ 1, near, pl.ds(0, 256))
    columns(place[0], own, pl.ds(0, 256))
    for copy in copies:
        copy.wait()


def deal(place, wq, wkv):
    return pl.pallas_call(
        deal_kernel,
        out_shape=(
            jax.ShapeDtypeStruct((256, 1024), BF),
            jax.ShapeDtypeStruct((256, 1024), BF),
            jax.ShapeDtypeStruct((2, 64, 1024), BF),
        ),
        in_specs=[SMEM] + [ANY] * 2,
        out_specs=(VMEM,) * 3,
        scratch_shapes=[pltpu.SemaphoreType.DMA((20,))],
        compiler_params=LARGE,
        name="deal",
    )(place, wq, wkv)


def project_kernel(place, group, own, near, far, cos, sin, gains, send, qk, tokens, w):
    w[pl.ds(pl.multiple_of(place[0] * 256, 256), 256), :] = own[...]
    w[pl.ds(pl.multiple_of((place[0] ^ 1) * 256, 256), 256), :] = near[...]
    for i in range(4):
        for k in range(2):
            at = pl.multiple_of((place[0] ^ (2 + k)) * 256 + 64 * i, 64)
            w[pl.ds(at, 64), :] = far[i, k]
    for j in range(4):
        n = place[0] ^ j
        base = n * 8
        rows = pl.ds(j * ROWS, ROWS)
        x = group[n, pl.ds(0, ROWS), :]
        tokens[rows, :] = x
        y = dot(x, w[...])
        c, s = cos[n], sin[n]
        qk[rows, :] = y
        core = lax.rem(place[0], 2)
        for h in range(8):
            v = y[:, h * HEAD : (h + 1) * HEAD]
            u = v * rms(v) * gains[pl.ds(h // 4, 1), :]
            u = u * c + pltpu.roll(u, HEAD // 2, 1) * s
            if h < 4:
                u = u.astype(BF)
                for half in range(2):
                    for b in range(2):
                        at = b * 64 + half * PART
                        send[base + h * 2 + half, pl.ds(b * PART, PART), :] = u[at : at + PART]
            else:
                u = jnp.where(core == 0, u, v).astype(BF)
                for half in range(2):
                    send[base + (h - 4) * 2 + half, pl.ds(64, ROWS), :] = u


def project(place, group, own, near, far, cos, sin, gains):
    return pl.pallas_call(
        project_kernel,
        out_shape=(
            jax.ShapeDtypeStruct((NCTX, CHUNK, HEAD), BF),
            jax.ShapeDtypeStruct((512, 1024), F32),
            jax.ShapeDtypeStruct((512, 1024), BF),
            jax.ShapeDtypeStruct((1024, 1024), BF),
        ),
        in_specs=[SMEM] + [VMEM] * 7,
        out_specs=(VMEM,) * 4,
        compiler_params=PARAMS,
        cost_estimate=pl.CostEstimate(
            flops=60_000_000_000, bytes_accessed=9_000_000, transcendentals=4000
        ),
        name="project",
    )(place, group, own, near, far, cos, sin, gains)


def project_back_kernel(place, back, qk, cos, sin, gains, tokens, out, send, dgains, grads):
    totals = [jnp.zeros((1, HEAD), F32), jnp.zeros((1, HEAD), F32)]
    for j in range(4):
        n = place[0] ^ j
        base = n * 8
        rows = pl.ds(j * ROWS, ROWS)
        c, s = cos[n], sin[n]
        core = lax.rem(place[0], 2)
        for h in range(8):
            at = base + h % 4 * 2
            if h < 4:
                parts = []
                for b in range(2):
                    for half in range(2):
                        parts.append(back[at + half, pl.ds(b * PART, PART), :])
                raw = jnp.concatenate(parts, axis=0).astype(F32)
            else:
                raw = back[at, pl.ds(64, ROWS), :].astype(F32)
                raw = raw + back[at + 1, pl.ds(64, ROWS), :].astype(F32)
            e = raw * c - pltpu.roll(raw, HEAD // 2, 1) * s
            u = qk[rows, pl.ds(h * HEAD, HEAD)]
            inverse = rms(u)
            u = u * inverse
            total = jnp.sum(e * u, axis=0, keepdims=True)
            if h >= 4:
                total = jnp.where(core == 0, total, 0.0)
            totals[h // 4] = totals[h // 4] + total
            e = e * gains[pl.ds(h // 4, 1), :]
            e = inverse * (e - u * jnp.mean(e * u, axis=-1, keepdims=True))
            if h >= 4:
                e = jnp.where(core == 0, e, raw)
            out[rows, pl.ds(h * HEAD, HEAD)] = e.astype(BF)
    grads[...] = dot_tn(tokens[...], out[...])
    for f in range(4):
        for p in range(16):
            for half in range(2):
                send[(p * 2 + half) * 4 + f] = grads[
                    pl.ds(256 * f + 16 * p, 16), pl.ds(512 * half, 512)
                ].astype(BF)
    dgains[...] = jnp.concatenate(totals, axis=0)


def project_back(place, back, qk, cos, sin, gains, tokens):
    return pl.pallas_call(
        project_back_kernel,
        out_shape=(
            jax.ShapeDtypeStruct((512, 1024), BF),
            jax.ShapeDtypeStruct((128, 16, 512), BF),
            jax.ShapeDtypeStruct((2, HEAD), F32),
        ),
        in_specs=[SMEM] + [VMEM] * 6,
        out_specs=(VMEM,) * 3,
        scratch_shapes=[pltpu.VMEM((1024, 1024), F32)],
        compiler_params=PARAMS,
        cost_estimate=pl.CostEstimate(
            flops=60_000_000_000, bytes_accessed=9_000_000, transcendentals=4000
        ),
        name="project_back",
    )(place, back, qk, cos, sin, gains, tokens)


def feed_grads_kernel(pa, norms, mixed, d0, d1, d2, d3, dgains, send, db, gu, down, out):
    for j, d in enumerate((d0, d1, d2, d3)):
        db[pl.ds(j * ROWS, ROWS), :] = d[...]
    out[...] = dot_tn(mixed[...], db[...])
    gu[...] = dot_tn(norms[:, pl.ds(0, 1024)], pa[:, pl.ds(384, 768)])
    down[...] = dot_tn(pa[:, pl.ds(0, 384)], norms[:, pl.ds(1024, 1024)])
    for to in range(NCTX):
        p, half = to // 2, to % 2

        def put(tile, ref, row, column):
            send[to, pl.ds(16 * tile, 16), :] = ref[pl.ds(row, 16), pl.ds(column, 128)].astype(BF)

        for f in range(4):
            for k in range(3):
                put(f * 3 + k, gu, 256 * f + 16 * p, 384 * half + 128 * k)
        for k in range(3):
            for i in range(2):
                put(12 + 2 * k + i, down, to // 4 * 48 + 16 * k, to % 4 * 256 + 128 * i)
        for b in range(2):
            for k in range(4):
                put(18 + 4 * b + k, out, 256 * b + 16 * p, 512 * half + 128 * k)
        put(26, dgains, 0, 0)


def feed_grads(parts, norms, mixed, d_branches, dgains):
    return pl.pallas_call(
        feed_grads_kernel,
        out_shape=jax.ShapeDtypeStruct((NCTX, 432, HEAD), BF),
        in_specs=[VMEM] * 8,
        out_specs=VMEM,
        scratch_shapes=[
            pltpu.VMEM((512, 1024), BF),
            pltpu.VMEM((1024, 768), F32),
            pltpu.VMEM((384, 1024), F32),
            pltpu.VMEM((512, 1024), F32),
        ],
        compiler_params=PARAMS,
        cost_estimate=pl.CostEstimate(
            flops=2_900_000_000, bytes_accessed=12_000_000, transcendentals=0
        ),
        name="feed_grads",
    )(parts, norms, mixed, *d_branches, dgains)


def feed_finish_kernel(tiles, gate, up, down, out):
    for c in range(NCTX):
        p, half = c // 2, c % 2
        for n in range(24):
            (up if half else gate)[pl.ds(16 * p, 16), pl.ds(128 * n, 128)] = tiles[c, n].astype(F32)
        for zl in range(2):
            for k in range(3):
                for i in range(2):
                    row = 384 * zl + c // 4 * 48 + 16 * k
                    down[pl.ds(row, 16), pl.ds(c % 4 * 256 + 128 * i, 128)] = tiles[
                        c, 24 + zl * 6 + 2 * k + i
                    ].astype(F32)
        for core in range(2):
            for k in range(4):
                row = 128 * (2 * (p // 8) + core) + 16 * (p % 8)
                out[pl.ds(row, 16), pl.ds(512 * half + 128 * k, 128)] = tiles[
                    c, 36 + 4 * core + k
                ].astype(F32)


def feed_finish(tiles):
    return pl.pallas_call(
        feed_finish_kernel,
        out_shape=(
            jax.ShapeDtypeStruct((256, 3072), F32),
            jax.ShapeDtypeStruct((256, 3072), F32),
            jax.ShapeDtypeStruct((768, 1024), F32),
            jax.ShapeDtypeStruct((512, 1024), F32),
        ),
        in_specs=[VMEM],
        out_specs=(VMEM,) * 4,
        compiler_params=PARAMS,
        cost_estimate=pl.CostEstimate(flops=0, bytes_accessed=18_000_000, transcendentals=0),
        name="feed_finish",
    )(tiles)


def project_finish_kernel(parts, gq, gk, gv):
    for p in range(16):
        rows = pl.ds(16 * p, 16)
        for f in range(4):
            zh, core = f // 2, f % 2
            for n in range(4):
                gq[rows, pl.ds((8 * zh + 2 * n + core) * HEAD, HEAD)] = parts[
                    2 * p, :, pl.ds(512 * f + HEAD * n, HEAD)
                ].astype(F32)
            (gv if core else gk)[rows, pl.ds(512 * zh, 512)] = parts[
                2 * p + 1, :, pl.ds(512 * f, 512)
            ].astype(F32)


def project_finish(parts):
    return pl.pallas_call(
        project_finish_kernel,
        out_shape=(
            jax.ShapeDtypeStruct((256, 2048), F32),
            jax.ShapeDtypeStruct((256, 1024), F32),
            jax.ShapeDtypeStruct((256, 1024), F32),
        ),
        in_specs=[VMEM],
        out_specs=(VMEM,) * 3,
        compiler_params=PARAMS,
        cost_estimate=pl.CostEstimate(flops=0, bytes_accessed=6_000_000, transcendentals=0),
        name="project_finish",
    )(parts)


def merge_kernel(place, recv, wo, mixed, keep, give):
    for j in range(4):
        base = (place[0] ^ j) * 8
        for h in range(4):
            parts = []
            for b in range(2):
                for half in range(2):
                    parts.append(recv[base + h * 2 + half, pl.ds(b * PART, PART), :])
            mixed[pl.ds(j * ROWS, ROWS), pl.ds(h * HEAD, HEAD)] = jnp.concatenate(parts, axis=0)
    for j in (1, 3, 0, 2):
        y = dot(mixed[pl.ds(j * ROWS, ROWS), :], wo[...])
        if j % 2:
            give[j // 2] = y.astype(BF)
        else:
            keep[j // 2] = y


def merge(place, recv, wo):
    return pl.pallas_call(
        merge_kernel,
        out_shape=(
            jax.ShapeDtypeStruct((512, 512), BF),
            jax.ShapeDtypeStruct((2, ROWS, 1024), F32),
            jax.ShapeDtypeStruct((2, ROWS, 1024), BF),
        ),
        in_specs=[SMEM] + [VMEM] * 2,
        out_specs=(VMEM, VMEM, VMEM),
        compiler_params=PARAMS,
        cost_estimate=pl.CostEstimate(
            flops=540_000_000, bytes_accessed=4_000_000, transcendentals=0
        ),
        name="merge",
    )(place, recv, wo)


def split_kernel(place, d0, d1, d2, d3, wo, send):
    for j, d in enumerate((d0, d1, d2, d3)):
        base = (place[0] ^ j) * 8
        y = dot_nt(d[...], wo[...]).astype(BF)
        for h in range(4):
            for b in range(2):
                for half in range(2):
                    at = b * 64 + half * PART
                    send[base + h * 2 + half, pl.ds(b * PART, PART), :] = y[
                        at : at + PART, h * HEAD : (h + 1) * HEAD
                    ]


def split(place, ds, wo):
    return pl.pallas_call(
        split_kernel,
        out_shape=jax.ShapeDtypeStruct((NCTX, 64, HEAD), BF),
        in_specs=[SMEM] + [VMEM] * 5,
        out_specs=VMEM,
        compiler_params=PARAMS,
        cost_estimate=pl.CostEstimate(
            flops=10_000_000, bytes_accessed=10_000, transcendentals=0
        ),
        name="split",
    )(place, *ds, wo)


def feed_kernel(
    place,
    a,
    hidden,
    x,
    g,
    gains,
    gate0,
    up0,
    down0,
    gate1,
    up1,
    down1,
    cat2,
    cat3,
    result,
    d_hidden,
    d_branch,
    norms,
    eighths,
    dgains,
    w,
    sems,
    parts,
    hb,
    gate,
    up,
    dh,
):
    copies = []

    def fetch(src, dst):
        copy = pltpu.make_async_copy(src, dst, sems.at[len(copies)])
        copy.start()
        copies.append(copy)

    for j, (gate_src, up_src) in enumerate(((gate0, up0), (gate1, up1))):
        fetch(gate_src, w.at[j, :, :, pl.ds(0, 3072)])
        fetch(up_src, w.at[j, :, :, pl.ds(3072, 3072)])
    for n in range(6):
        for j, src in ((2, cat2), (3, cat3)):
            fetch(src.at[:, pl.ds(16 * n, 16), :], w.at[j, :, :, pl.ds(1024 * n, 1024)])
    first_needed = len(copies)
    for n in range(3):
        at = pl.ds(6144 + 1024 * n, 1024)
        for j, src in ((0, down0), (1, down1)):
            fetch(src.at[pl.ds(16 * n, 16), :, :], w.at[j, :, :, at])
        for j, src in ((2, cat2), (3, cat3)):
            fetch(src.at[:, pl.ds(96 + 16 * n, 16), :], w.at[j, :, :, at])

    def rows_of(j, at, width):
        return w[j, :, :, pl.ds(at, width)].reshape(256, width)

    me = place[0]
    gain_a, gain_m = gains[pl.ds(0, 1), :], gains[pl.ds(1, 1), :]
    inverse_a = rms(a[...])
    normed_a = a[...] * inverse_a
    h = x[...].astype(F32) + normed_a * gain_a
    for n in range(4):
        hb[n] = hidden[:, pl.ds(256 * n, 256)]
    norms[:, pl.ds(0, 1024)] = hidden[...]
    for copy in copies[:first_needed]:
        copy.wait()
    for n in range(4):
        at = 768 * n
        u = dot(hb[me], rows_of(0, at, 768))
        v = dot(hb[me], rows_of(0, 3072 + at, 768))
        for j in range(1, 4):
            u = u + dot(hb[me ^ j], rows_of(j, at, 768))
            v = v + dot(hb[me ^ j], rows_of(j, 3072 + at, 768))
        gate[n] = u
        up[n] = v
        parts[n, :, pl.ds(0, 768)] = (u / (1.0 + jnp.exp(-u)) * v).astype(BF)
    for copy in copies[first_needed:]:
        copy.wait()
    z = jnp.zeros((ROWS, 1024), F32)
    for j in range(4):
        for b in range(3):
            z = z + dot(
                parts[me ^ j, :, pl.ds(256 * b, 256)], rows_of(j, 6144 + 1024 * b, 1024)
            )
    inverse_z = rms(z)
    normed_z = z * inverse_z
    result[...] = (h + normed_z * gain_m).astype(BF)
    e = g[...].astype(F32)
    dgains[pl.ds(1, 1), :] = jnp.sum(e * normed_z, axis=0, keepdims=True)
    weighted = e * gain_m
    dz = inverse_z * (weighted - normed_z * jnp.mean(weighted * normed_z, axis=-1, keepdims=True))
    dz = dz.astype(BF)
    norms[:, pl.ds(1024, 1024)] = dz
    for j in range(4):
        n = me ^ j
        for b in range(3):
            at = pl.ds(256 * b, 256)
            d_act = dot_nt(dz, rows_of(j, 6144 + 1024 * b, 1024))
            u, v = gate[n, :, at], up[n, :, at]
            s = 1.0 / (1.0 + jnp.exp(-u))
            parts[n, :, pl.ds(768 + 256 * b, 256)] = (
                d_act * v * (s * (1.0 + u * (1.0 - s)))
            ).astype(BF)
            parts[n, :, pl.ds(1536 + 256 * b, 256)] = (d_act * (u * s)).astype(BF)
    for n in range(8):
        for k in range(3):
            eighths[n, :, pl.ds(384 * k, 384)] = parts[
                n % 4, :, pl.ds(768 * k + 384 * (n // 4), 384)
            ]
    for j in range(4):
        total = jnp.zeros((ROWS, 256), F32)
        for n in range(4):
            total = total + dot_nt(parts[n, :, pl.ds(768, 768)], rows_of(j, 768 * n, 768))
            total = total + dot_nt(
                parts[n, :, pl.ds(1536, 768)], rows_of(j, 3072 + 768 * n, 768)
            )
        dh[me ^ j] = total
    total = g[...].astype(F32) + jnp.concatenate([dh[n] for n in range(4)], axis=1)
    d_hidden[...] = total
    dgains[pl.ds(0, 1), :] = jnp.sum(total * normed_a, axis=0, keepdims=True)
    weighted = total * gain_a
    d_branch[...] = (
        inverse_a * (weighted - normed_a * jnp.mean(weighted * normed_a, axis=-1, keepdims=True))
    ).astype(BF)


def feed(place, a, hidden, x, g, gains, weights):
    return pl.pallas_call(
        feed_kernel,
        out_shape=(
            jax.ShapeDtypeStruct((ROWS, 1024), BF),
            jax.ShapeDtypeStruct((ROWS, 1024), F32),
            jax.ShapeDtypeStruct((ROWS, 1024), BF),
            jax.ShapeDtypeStruct((ROWS, 2048), BF),
            jax.ShapeDtypeStruct((8, ROWS, 1152), BF),
            jax.ShapeDtypeStruct((2, 1024), F32),
        ),
        in_specs=[SMEM] + [VMEM] * 5 + [ANY] * 8,
        out_specs=(VMEM,) * 6,
        scratch_shapes=[
            pltpu.VMEM((4, 16, 16, 9216), BF),
            pltpu.SemaphoreType.DMA((28,)),
            pltpu.VMEM((4, ROWS, 2304), BF),
            pltpu.VMEM((4, ROWS, 256), BF),
            pltpu.VMEM((4, ROWS, 768), F32),
            pltpu.VMEM((4, ROWS, 768), F32),
            pltpu.VMEM((4, ROWS, 256), F32),
        ],
        compiler_params=LARGE,
        cost_estimate=pl.CostEstimate(
            flops=10_000_000, bytes_accessed=10_000, transcendentals=0
        ),
        name="feed_forward",
    )(
        place,
        a,
        hidden,
        x,
        g,
        gains,
        *[v.reshape(-1, 16, v.shape[1]) for v in weights[:6]],
        *[v.reshape(16, -1, 1024) for v in weights[6:]],
    )


SWAP = [(0, 1), (1, 0)]


def swap(x, axis):
    return lax.ppermute(x, axis, SWAP)


def in_order(place, own, other):
    return jnp.where(place == 0, jnp.stack([own, other]), jnp.stack([other, own]))


def relative(x):
    far = swap(x, "zh")
    return [x, swap(x, "core"), far, swap(far, "core")]


def exchange(x, axes):
    return lax.all_to_all(x, axes, split_axis=0, concat_axis=0, tiled=True)


def after(xs, *others):
    return lax.optimization_barrier((xs,) + others)[0]


def local(
    tokens,
    cotangent,
    doc_ids,
    wq,
    wk,
    wv,
    wo,
    q_gain,
    k_gain,
    attn_gain,
    w_gate,
    w_up,
    w_down,
    mlp_gain,
):
    c = lax.axis_index(CTX)
    f = lax.axis_index(FSDP)
    place = f[None].astype(jnp.int32)
    inputs = tokens.reshape(ROWS, 1024)

    core = lax.axis_index("core")
    wkv = jnp.concatenate([wk, wv], axis=1)
    own, near, quarter = deal(jnp.stack([f, lax.axis_index("x")]).astype(jnp.int32), wq, wkv)
    near = swap(near, "core")
    quarter = swap(quarter, "zh")
    quarter = jnp.stack([quarter[0], swap(quarter[1], "core")])
    quarter = exchange(jnp.broadcast_to(quarter[None], (4, 2, 64, 1024)), ("x",))

    spot = lax.axis_index("y") * 4 + lax.axis_index("x")
    pack = pack_group(
        spot[None].astype(jnp.int32),
        inputs,
        doc_ids,
        (q_gain[None], k_gain[None], jnp.stack([attn_gain, mlp_gain])),
        (w_gate, w_up, w_down),
    )
    group = lax.all_gather(pack, FSDP, axis=0, tiled=True).reshape(4, 288, 1024)
    gains = group[:, ROWS].astype(F32)
    gains_qk = jnp.stack([gains[:, :32].reshape(HEAD), gains[:, 128:160].reshape(HEAD)])
    gains_am = jnp.stack([gains[:, 512:768].reshape(1024), gains[:, 768:].reshape(1024)])
    starts_f = (gains[:, 256:261] * 64.0 + gains[:, 384:389]).astype(jnp.int32)
    far = lax.dynamic_slice(group, (f ^ 2, ROWS + 16, 0), (1, 144, 1024))[0]
    far = lax.all_gather(far, PLANE, axis=0, tiled=True)

    step = jnp.arange(BLOCK, dtype=jnp.int32)
    spot = jnp.concatenate([c * BLOCK + step, (2 * NCTX - 1 - c) * BLOCK + step])
    start = jnp.max(
        jnp.where(starts_f[:, :, None] <= spot[None, None, :], starts_f[:, :, None], 0), axis=1
    )
    position = spot[None, :] - start
    half = jnp.arange(HEAD, dtype=jnp.int32) % (HEAD // 2)
    frequency = jnp.exp(half.astype(F32) * (-2.0 * math.log(THETA) / HEAD))
    angles = position.astype(F32)[:, :, None] * frequency
    sign = jnp.where(jnp.arange(HEAD) < HEAD // 2, -1.0, 1.0).astype(F32)
    cos, sin = jnp.cos(angles), jnp.sin(angles) * sign

    send, qk, tokens_f, w_qkv = project(place, group, own, near, quarter, cos, sin, gains_qk)
    recv = exchange(send, CTX)
    near = (swap(w_gate, "core"), swap(w_up, "core"), swap(w_down, "core"))
    pairs = wo.reshape(2, 2, HEAD, 1024)
    heads = lax.dynamic_index_in_dim(pairs, core, 1, keepdims=False)
    others = swap(lax.dynamic_index_in_dim(pairs, 1 - core, 1, keepdims=False), "core")
    wo = in_order(core, heads, others).reshape(512, 1024)
    recv, near, wo = lax.optimization_barrier((recv, near, wo))
    other = swap(recv, "core")
    my_starts = lax.dynamic_index_in_dim(starts_f, c // 8, 0, keepdims=False)
    meta = [(c % 2)[None].astype(jnp.int32), my_starts, core[None].astype(jnp.int32)]
    meta = jnp.concatenate(meta + [jnp.zeros((1,), jnp.int32)])
    mixed_t, ot, lsum = attend(meta, recv, other)
    far = after(far, mixed_t)
    mixed_t = exchange(mixed_t, CTX)
    feed_weights = (
        w_gate,
        w_up,
        w_down,
        *near,
        far,
        swap(far, "core"),
    )
    mixed, keep, give = merge(place, mixed_t, wo)
    got = swap(give, "core")
    last = swap((keep[1] + got[1].astype(F32)).astype(BF), "zh")
    branch = keep[0] + got[0].astype(F32) + last.astype(F32)
    hidden = branch * rms(branch) * gains_am[0] + inputs.astype(F32)
    hidden = hidden.astype(BF)
    result, d_hidden, d_branch, norms, parts, d_gains_am = feed(
        place, branch, hidden, inputs, cotangent.reshape(ROWS, 1024), gains_am, feed_weights
    )
    norms = lax.all_gather(norms, COLUMN, axis=0, tiled=True)
    d_branches = relative(d_branch)
    drecv = exchange(split(place, d_branches, wo), CTX)

    parts = exchange(after(parts, drecv), COLUMN).reshape(1024, 1152)
    dq, keep, give = attend_back(meta, recv, other, drecv, ot, lsum)
    keep = (keep.astype(F32) + swap(give, "core").astype(F32)).astype(BF)
    back = jnp.concatenate([dq, keep], axis=1)
    parts = after(parts, back)
    back = exchange(after(back, parts), CTX)
    g_feed = feed_grads(parts, norms, mixed, d_branches, d_gains_am.reshape(16, HEAD))
    g_feed = exchange(after(g_feed, back), CTX)

    d_qkv, g_qkv, d_gains_qk = project_back(place, back, qk, cos, sin, gains_qk, tokens_f)

    partial = dot_nt(d_qkv, w_qkv).reshape(4, ROWS, 1024)
    got = swap(jnp.stack([partial[1], partial[3]]).astype(BF), "core").astype(F32)
    last = swap((partial[2] + got[1]).astype(BF), "zh").astype(F32)
    d_inputs = d_hidden + partial[0] + got[0] + last

    g_feed, g_qkv, d_inputs = lax.optimization_barrier((g_feed, g_qkv, d_inputs))
    g_feed = g_feed.reshape(16, 2, 27, 16, HEAD)
    g_out = jnp.sum(g_feed[:, :, 18:].astype(F32), axis=(0, 1))
    d_gains_am = g_out[8]
    g_out = g_out[:8].astype(BF).reshape(2, 4, 16, HEAD)
    others = swap(lax.dynamic_index_in_dim(g_out, 1 - core, 0, keepdims=False), "core")
    g_out = lax.dynamic_index_in_dim(g_out, core, 0, keepdims=False)
    g_out = in_order(core, g_out, others).reshape(8, 16, HEAD)
    g_feed = jnp.sum(g_feed[:, :, :18].astype(F32), axis=0).astype(BF)
    g_gu = g_feed[:, :12].reshape(2, 4, 3, 16, HEAD).swapaxes(0, 1)
    g_gu = jnp.broadcast_to(g_gu[None], (2, 4, 2, 3, 16, HEAD)).reshape(8, 96, HEAD)
    g_gu = exchange(g_gu, COLUMN).reshape(2, 384, HEAD)
    g_feed = jnp.concatenate([g_feed[:, 12:].reshape(12, 16, HEAD), g_out], axis=0)
    g_feed = g_feed.reshape(320, HEAD)
    g_feed = in_order(lax.axis_index("zl"), g_feed, swap(g_feed, "zl"))
    g_feed = jnp.concatenate([g_gu, g_feed], axis=1)
    g_qkv = after(g_qkv, g_feed)
    g_feed = lax.all_gather(g_feed, PLANE, axis=0, tiled=True).reshape(NCTX, 44, 16, HEAD)

    g_qkv = exchange(g_qkv, AXES)
    gains = jnp.concatenate([d_gains_am, d_gains_qk, jnp.zeros((14, HEAD), F32)], axis=0)
    gains = gains + swap(gains.astype(BF), "core").astype(F32)
    gains = gains + swap(gains.astype(BF), "zh").astype(F32)

    g_qkv, gains = lax.optimization_barrier((g_qkv, gains))
    g_qkv = jnp.sum(g_qkv.reshape(NCTX, 4, 16, 512).astype(F32), axis=0)
    g_qkv = g_qkv.swapaxes(0, 1).reshape(16, 2048)
    g_qkv = jnp.concatenate([g_qkv, gains[16:]], axis=1).astype(BF)
    g_qkv = exchange(jnp.broadcast_to(g_qkv[None], (NCTX, 16, 2176)), CTX)
    gains_qk = jnp.sum(g_qkv[:, :2, 2048:].astype(F32), axis=0)
    gains_am = lax.dynamic_index_in_dim(gains[:16].reshape(2, 4, 256), f, 1, keepdims=False)

    g_q, g_k, g_v = project_finish(g_qkv)
    gate_grad, up_grad, down_grad, out_grad = feed_finish(after(g_feed, g_q))
    gains_qk = lax.dynamic_slice_in_dim(gains_qk, f * 32, 32, 1)
    return (
        result.reshape(tokens.shape),
        d_inputs.reshape(tokens.shape),
        g_q,
        g_k,
        g_v,
        out_grad,
        gains_qk[0],
        gains_qk[1],
        gains_am[0],
        gate_grad,
        up_grad,
        down_grad,
        gains_am[1],
    )


def solution(mesh):
    whole = Mesh(mesh.devices.reshape(4, 4, 2, 2, 2), AXES)
    blocks = P(FSDP, None, CTX, None, None)
    rows = P(FSDP, None)
    vector = P(FSDP)
    return jax.shard_map(
        local,
        mesh=whole,
        in_specs=(
            blocks,
            blocks,
            rows,
            rows,
            rows,
            rows,
            rows,
            vector,
            vector,
            vector,
            rows,
            rows,
            rows,
            vector,
        ),
        out_specs=(
            blocks,
            blocks,
            rows,
            rows,
            rows,
            rows,
            vector,
            vector,
            vector,
            rows,
            rows,
            rows,
            vector,
        ),
        check_vma=False,
    )
```

```python
import math

import jax
import jax.numpy as jnp
from jax import lax
from jax.experimental import pallas as pl
from jax.experimental.pallas import tpu as pltpu
from jax.sharding import Mesh, PartitionSpec as P

HEADS = 16
KV_HEADS = 8
HEAD = 128
EPS = 1e-06
THETA = 500000.0

AXES = ("y", "x", "zl", "zh", "core")
CTX = ("y", "x", "zl")
PLANE = ("y", "x")
FSDP = ("zh", "core")
COLUMN = ("zl", "zh", "core")
NCTX = 32
SEQS = 4
BLOCK = 64
ROWS = 2 * BLOCK
LEN = 4096
DOCS = 5
PART = 32
TILES = 8
QT = 256
KT = 512
CHUNK = 192
BF = jnp.bfloat16
F32 = jnp.float32
SCALE = HEAD**-0.5
LOG2E = math.log2(math.e)


def key_block(j):
    return (j, 0) if j < NCTX else (2 * NCTX - 1 - j, 1)


def tile_bounds(meta, t):
    first, last = t * KT, t * KT + KT - 1
    low = jnp.int32(0)
    high = jnp.int32(0)
    for d in range(1, DOCS):
        start = meta[1 + d]
        low = jnp.where(start <= first, start, low)
        high = jnp.where(start <= last, start, high)
    return lax.div(low, KT), jnp.minimum(lax.div(high + (KT - 1), KT), t)


def row_places(meta, t):
    lane = lax.broadcasted_iota(jnp.int32, (1, QT), 1)
    place = t * KT + lax.div(lane, PART) * BLOCK + meta[0] * PART + lax.rem(lane, PART)
    start = jnp.zeros((1, QT), jnp.int32)
    for d in range(1, DOCS):
        start = jnp.where(place >= meta[1 + d], meta[1 + d], start)
    return place, start


def allowed(kt, place, start):
    key = kt * KT + lax.broadcasted_iota(jnp.int32, (KT, QT), 0)
    return (key <= place) & (key >= start)


def gather_rows(src, t):
    parts = []
    for i in range(8):
        c, b = key_block(8 * t + i)
        parts.append(src[c, pl.ds(b * PART, PART), :])
    return jnp.concatenate(parts, axis=0)


def sort_keys(src, dst):
    for j in range(2 * NCTX):
        c, b = key_block(j)
        dst[pl.ds(j * BLOCK, BLOCK), :] = src[c, pl.ds(64 + b * BLOCK, BLOCK), :]


def sort_both(meta, mine, other, ks, vs):
    @pl.when(meta[6] == 0)
    def _():
        sort_keys(mine, ks)
        sort_keys(other, vs)

    @pl.when(meta[6] != 0)
    def _():
        sort_keys(other, ks)
        sort_keys(mine, vs)


def put_rows(out, t, rows):
    for i in range(8):
        j = 8 * t + i
        half = (j >= NCTX).astype(jnp.int32)
        c = jnp.where(half == 0, j, 2 * NCTX - 1 - j)
        out[c, pl.ds(pl.multiple_of(half * PART, PART), PART), :] = rows[i * PART : (i + 1) * PART]


def transposed(x):
    return x.astype(F32).T.astype(x.dtype)


def forward_kernel(meta, mine, other, out, ot, lsum, ks, vs, vt, qt):
    sort_both(meta, mine, other, ks, vs)
    for i in range(TILES):
        vt[i] = transposed(vs[pl.ds(i * KT, KT), :])
        qt[i] = transposed(gather_rows(mine, i))

    def query_tile(t, _):
        q = qt[t]
        place, start = row_places(meta, t)
        low, clear = tile_bounds(meta, t)

        def step(kt, carry, masked):
            total, mixed = carry
            k = ks[pl.ds(pl.multiple_of(kt * KT, KT), KT), :]
            s = jnp.dot(k, q, preferred_element_type=F32)
            p = jnp.exp2(s * (SCALE * LOG2E))
            if masked:
                p = jnp.where(allowed(kt, place, start), p, 0.0)
            total = total + jnp.sum(p, axis=0, keepdims=True)
            mixed = mixed + jnp.dot(vt[kt], p.astype(BF), preferred_element_type=F32)
            return total, mixed

        carry = (jnp.zeros((1, QT), F32), jnp.zeros((HEAD, QT), F32))
        carry = lax.fori_loop(low, clear, lambda kt, cr: step(kt, cr, True), carry)
        carry = lax.fori_loop(jnp.maximum(low, clear), t, lambda kt, cr: step(kt, cr, False), carry)
        total, mixed = step(t, carry, True)
        mixed = mixed * (1.0 / total)
        ot[t] = mixed
        lsum[t] = total
        rows = mixed.T.astype(BF)
        put_rows(out, t, rows)
        return 0

    lax.fori_loop(0, TILES, query_tile, 0)


def backward_kernel(
    meta, mine, other, drecv, ot, lsum, out, keep, give, ks, vs, kt_, q_, qt, do_, dot_, dk, dv
):
    sort_both(meta, mine, other, ks, vs)
    for i in range(TILES):
        kt_[i] = transposed(ks[pl.ds(i * KT, KT), :])
        rows = gather_rows(mine, i)
        q_[i] = rows
        qt[i] = transposed(rows)
        rows = gather_rows(drecv, i)
        do_[i] = rows
        dot_[i] = transposed(rows)
    dk[...] = jnp.zeros_like(dk)
    dv[...] = jnp.zeros_like(dv)

    def query_tile(t, _):
        q, q_t, d, d_t = q_[t], qt[t], do_[t], dot_[t]
        place, start = row_places(meta, t)
        low, clear = tile_bounds(meta, t)
        delta = jnp.sum(d_t.astype(F32) * ot[t], axis=0, keepdims=True)
        shift = jnp.log2(lsum[t])

        def step(kt, total, masked):
            at = pl.ds(pl.multiple_of(kt * KT, KT), KT)
            s = jnp.dot(ks[at, :], q_t, preferred_element_type=F32)
            p = jnp.exp2(s * (SCALE * LOG2E) - shift)
            if masked:
                p = jnp.where(allowed(kt, place, start), p, 0.0)
            dv[at, :] += jnp.dot(p.astype(BF), d, preferred_element_type=F32)
            dp = jnp.dot(vs[at, :], d_t, preferred_element_type=F32)
            ds = (p * (dp - delta)).astype(BF)
            dk[at, :] += jnp.dot(ds, q, preferred_element_type=F32)
            return total + jnp.dot(kt_[kt], ds, preferred_element_type=F32)

        total = jnp.zeros((HEAD, QT), F32)
        total = lax.fori_loop(low, clear, lambda kt, cr: step(kt, cr, True), total)
        total = lax.fori_loop(jnp.maximum(low, clear), t, lambda kt, cr: step(kt, cr, False), total)
        total = step(t, total, True)
        rows = (total * SCALE).T.astype(BF)
        put_rows(out, t, rows)
        return 0

    lax.fori_loop(0, TILES, query_tile, 0)

    def unsort(src, scale, dst):
        for j in range(2 * NCTX):
            c, b = key_block(j)
            dst[c, pl.ds(b * BLOCK, BLOCK), :] = (src[pl.ds(j * BLOCK, BLOCK), :] * scale).astype(BF)

    @pl.when(meta[6] == 0)
    def _():
        unsort(dk, SCALE, keep)
        unsort(dv, 1.0, give)

    @pl.when(meta[6] != 0)
    def _():
        unsort(dv, 1.0, keep)
        unsort(dk, SCALE, give)


VMEM = pl.BlockSpec(memory_space=pltpu.VMEM)
SMEM = pl.BlockSpec(memory_space=pltpu.SMEM)
ANY = pl.BlockSpec(memory_space=pl.ANY)
PARAMS = pltpu.CompilerParams(vmem_limit_bytes=48 * 1024 * 1024)
LARGE = pltpu.CompilerParams(vmem_limit_bytes=60 * 1024 * 1024)


def attend(meta, mine, other):
    return pl.pallas_call(
        forward_kernel,
        out_shape=(
            jax.ShapeDtypeStruct((NCTX, 64, HEAD), BF),
            jax.ShapeDtypeStruct((TILES, HEAD, QT), F32),
            jax.ShapeDtypeStruct((TILES, 1, QT), F32),
        ),
        in_specs=[SMEM, VMEM, VMEM],
        out_specs=(VMEM, VMEM, VMEM),
        scratch_shapes=[
            pltpu.VMEM((LEN, HEAD), BF),
            pltpu.VMEM((LEN, HEAD), BF),
            pltpu.VMEM((TILES, HEAD, KT), BF),
            pltpu.VMEM((TILES, HEAD, QT), BF),
        ],
        compiler_params=PARAMS,
        cost_estimate=pl.CostEstimate(
            flops=15_000_000_000, bytes_accessed=5_000_000, transcendentals=4_700_000
        ),
        name="attention_forward",
    )(meta, mine, other)


def attend_back(meta, mine, other, drecv, ot, lsum):
    return pl.pallas_call(
        backward_kernel,
        out_shape=(
            jax.ShapeDtypeStruct((NCTX, 64, HEAD), BF),
            jax.ShapeDtypeStruct((NCTX, ROWS, HEAD), BF),
            jax.ShapeDtypeStruct((NCTX, ROWS, HEAD), BF),
        ),
        in_specs=[SMEM] + [VMEM] * 5,
        out_specs=(VMEM,) * 3,
        scratch_shapes=[
            pltpu.VMEM((LEN, HEAD), BF),
            pltpu.VMEM((LEN, HEAD), BF),
            pltpu.VMEM((TILES, HEAD, KT), BF),
            pltpu.VMEM((TILES, QT, HEAD), BF),
            pltpu.VMEM((TILES, HEAD, QT), BF),
            pltpu.VMEM((TILES, QT, HEAD), BF),
            pltpu.VMEM((TILES, HEAD, QT), BF),
            pltpu.VMEM((LEN, HEAD), F32),
            pltpu.VMEM((LEN, HEAD), F32),
        ],
        compiler_params=PARAMS,
        cost_estimate=pl.CostEstimate(
            flops=10_000_000, bytes_accessed=10_000, transcendentals=0
        ),
        name="attention_backward",
    )(meta, mine, other, drecv, ot, lsum)


def rms(u):
    return lax.rsqrt(jnp.mean(u * u, axis=-1, keepdims=True) + EPS)


def dot(a, b):
    return jnp.dot(a, b, preferred_element_type=F32)


def dot_nt(a, b):
    return lax.dot_general(a, b, (((1,), (1,)), ((), ())), preferred_element_type=F32)


def dot_tn(a, b):
    return lax.dot_general(a, b, (((0,), (0,)), ((), ())), preferred_element_type=F32)


def pack_kernel(at, x, docs, q_gain, k_gain, am_gain, gate, up, down, out, row, sem):
    copies = []
    for n in range(3):
        for src, row_at, lane_at, width in (
            (gate, 0, 1024 * n, 1024),
            (up, 0, 1024 * n, 1024),
            (down, 256 * n, 0, 1024),
        ):
            k = len(copies)
            first = pl.multiple_of(row_at + at[0] * 16, 16)
            copies.append(
                pltpu.make_async_copy(
                    src.at[pl.ds(first, 16), pl.ds(lane_at, width)],
                    out.at[pl.ds(144 + 16 * (3 * (k % 3) + n), 16), :],
                    sem.at[k],
                )
            )
            copies[-1].start()
    out[pl.ds(0, ROWS), :] = x[...]
    row[...] = jnp.zeros_like(row)
    row[:, pl.ds(0, 32)] = q_gain[...].astype(F32)
    row[:, pl.ds(128, 32)] = k_gain[...].astype(F32)
    lane = lax.broadcasted_iota(jnp.int32, (1, HEAD), 1)
    high = jnp.zeros((1, HEAD), F32)
    low = jnp.zeros((1, HEAD), F32)
    for d in range(1, DOCS):
        start = jnp.sum((docs[...] < d).astype(F32), axis=1, keepdims=True)
        whole = jnp.floor(start * (1.0 / 64.0))
        high = jnp.where(lane == d, whole, high)
        low = jnp.where(lane == d, start - whole * 64.0, low)
    row[:, pl.ds(256, HEAD)] = high
    row[:, pl.ds(384, HEAD)] = low
    row[:, pl.ds(512, 256)] = am_gain[pl.ds(0, 1), :].astype(F32)
    row[:, pl.ds(768, 256)] = am_gain[pl.ds(1, 1), :].astype(F32)
    out[pl.ds(ROWS, 16), :] = jnp.broadcast_to(row[...], (16, 1024)).astype(BF)
    for copy in copies:
        copy.wait()


def pack_group(at, x, docs, gains, weights):
    return pl.pallas_call(
        pack_kernel,
        out_shape=jax.ShapeDtypeStruct((288, 1024), BF),
        in_specs=[SMEM] + [VMEM] * 5 + [ANY] * 3,
        out_specs=VMEM,
        scratch_shapes=[pltpu.VMEM((1, 1024), F32), pltpu.SemaphoreType.DMA((9,))],
        compiler_params=LARGE,
        name="pack_group",
    )(at, x, docs, *gains, *weights)


def deal_kernel(place, wq, wkv, own, near, far, sem):
    copies = []

    def columns(f, dst, rows):
        zh, core = lax.div(f, 2), lax.rem(f, 2)
        slices = [(wq, (8 * zh + 2 * n + core) * HEAD, HEAD, n * HEAD) for n in range(4)]
        for src, lane, width, at in slices + [(wkv, 1024 * core + 512 * zh, 512, 512)]:
            lanes = pl.ds(pl.multiple_of(lane, HEAD), width)
            copies.append(
                pltpu.make_async_copy(
                    src.at[rows, lanes], dst.at[:, pl.ds(at, width)], sem.at[len(copies)]
                )
            )
            copies[-1].start()

    quarter = pl.ds(pl.multiple_of(place[1] * 64, 64), 64)
    columns(place[0] ^ 2, far.at[0], quarter)
    columns(place[0] ^ 3, far.at[1], quarter)
    columns(place[0] ^ 1, near, pl.ds(0, 256))
    columns(place[0], own, pl.ds(0, 256))
    for copy in copies:
        copy.wait()


def deal(place, wq, wkv):
    return pl.pallas_call(
        deal_kernel,
        out_shape=(
            jax.ShapeDtypeStruct((256, 1024), BF),
            jax.ShapeDtypeStruct((256, 1024), BF),
            jax.ShapeDtypeStruct((2, 64, 1024), BF),
        ),
        in_specs=[SMEM] + [ANY] * 2,
        out_specs=(VMEM,) * 3,
        scratch_shapes=[pltpu.SemaphoreType.DMA((20,))],
        compiler_params=LARGE,
        name="deal",
    )(place, wq, wkv)


def project_kernel(place, group, own, near, far, cos, sin, gains, send, qk, tokens, w):
    w[pl.ds(pl.multiple_of(place[0] * 256, 256), 256), :] = own[...]
    w[pl.ds(pl.multiple_of((place[0] ^ 1) * 256, 256), 256), :] = near[...]
    for i in range(4):
        for k in range(2):
            at = pl.multiple_of((place[0] ^ (2 + k)) * 256 + 64 * i, 64)
            w[pl.ds(at, 64), :] = far[i, k]
    for j in range(4):
        n = place[0] ^ j
        base = n * 8
        rows = pl.ds(j * ROWS, ROWS)
        x = group[n, pl.ds(0, ROWS), :]
        tokens[rows, :] = x
        y = dot(x, w[...])
        c, s = cos[n], sin[n]
        qk[rows, :] = y
        core = lax.rem(place[0], 2)
        for h in range(8):
            v = y[:, h * HEAD : (h + 1) * HEAD]
            u = v * rms(v) * gains[pl.ds(h // 4, 1), :]
            u = u * c + pltpu.roll(u, HEAD // 2, 1) * s
            if h < 4:
                u = u.astype(BF)
                for half in range(2):
                    for b in range(2):
                        at = b * 64 + half * PART
                        send[base + h * 2 + half, pl.ds(b * PART, PART), :] = u[at : at + PART]
            else:
                u = jnp.where(core == 0, u, v).astype(BF)
                for half in range(2):
                    send[base + (h - 4) * 2 + half, pl.ds(64, ROWS), :] = u


def project(place, group, own, near, far, cos, sin, gains):
    return pl.pallas_call(
        project_kernel,
        out_shape=(
            jax.ShapeDtypeStruct((NCTX, CHUNK, HEAD), BF),
            jax.ShapeDtypeStruct((512, 1024), F32),
            jax.ShapeDtypeStruct((512, 1024), BF),
            jax.ShapeDtypeStruct((1024, 1024), BF),
        ),
        in_specs=[SMEM] + [VMEM] * 7,
        out_specs=(VMEM,) * 4,
        compiler_params=PARAMS,
        cost_estimate=pl.CostEstimate(
            flops=60_000_000_000, bytes_accessed=9_000_000, transcendentals=4000
        ),
        name="project",
    )(place, group, own, near, far, cos, sin, gains)


def project_back_kernel(place, back, qk, cos, sin, gains, tokens, out, send, dgains, grads):
    totals = [jnp.zeros((1, HEAD), F32), jnp.zeros((1, HEAD), F32)]
    for j in range(4):
        n = place[0] ^ j
        base = n * 8
        rows = pl.ds(j * ROWS, ROWS)
        c, s = cos[n], sin[n]
        core = lax.rem(place[0], 2)
        for h in range(8):
            at = base + h % 4 * 2
            if h < 4:
                parts = []
                for b in range(2):
                    for half in range(2):
                        parts.append(back[at + half, pl.ds(b * PART, PART), :])
                raw = jnp.concatenate(parts, axis=0).astype(F32)
            else:
                raw = back[at, pl.ds(64, ROWS), :].astype(F32)
                raw = raw + back[at + 1, pl.ds(64, ROWS), :].astype(F32)
            e = raw * c - pltpu.roll(raw, HEAD // 2, 1) * s
            u = qk[rows, pl.ds(h * HEAD, HEAD)]
            inverse = rms(u)
            u = u * inverse
            total = jnp.sum(e * u, axis=0, keepdims=True)
            if h >= 4:
                total = jnp.where(core == 0, total, 0.0)
            totals[h // 4] = totals[h // 4] + total
            e = e * gains[pl.ds(h // 4, 1), :]
            e = inverse * (e - u * jnp.mean(e * u, axis=-1, keepdims=True))
            if h >= 4:
                e = jnp.where(core == 0, e, raw)
            out[rows, pl.ds(h * HEAD, HEAD)] = e.astype(BF)
    grads[...] = dot_tn(tokens[...], out[...])
    for f in range(4):
        for p in range(16):
            for half in range(2):
                send[(p * 2 + half) * 4 + f] = grads[
                    pl.ds(256 * f + 16 * p, 16), pl.ds(512 * half, 512)
                ].astype(BF)
    dgains[...] = jnp.concatenate(totals, axis=0)


def project_back(place, back, qk, cos, sin, gains, tokens):
    return pl.pallas_call(
        project_back_kernel,
        out_shape=(
            jax.ShapeDtypeStruct((512, 1024), BF),
            jax.ShapeDtypeStruct((128, 16, 512), BF),
            jax.ShapeDtypeStruct((2, HEAD), F32),
        ),
        in_specs=[SMEM] + [VMEM] * 6,
        out_specs=(VMEM,) * 3,
        scratch_shapes=[pltpu.VMEM((1024, 1024), F32)],
        compiler_params=PARAMS,
        cost_estimate=pl.CostEstimate(
            flops=60_000_000_000, bytes_accessed=9_000_000, transcendentals=4000
        ),
        name="project_back",
    )(place, back, qk, cos, sin, gains, tokens)


def feed_grads_kernel(pa, norms, mixed, d0, d1, d2, d3, dgains, send, db, gu, down, out):
    for j, d in enumerate((d0, d1, d2, d3)):
        db[pl.ds(j * ROWS, ROWS), :] = d[...]
    out[...] = dot_tn(mixed[...], db[...])
    gu[...] = dot_tn(norms[:, pl.ds(0, 1024)], pa[:, pl.ds(384, 768)])
    down[...] = dot_tn(pa[:, pl.ds(0, 384)], norms[:, pl.ds(1024, 1024)])
    for to in range(NCTX):
        p, half = to // 2, to % 2

        def put(tile, ref, row, column):
            send[to, pl.ds(16 * tile, 16), :] = ref[pl.ds(row, 16), pl.ds(column, 128)].astype(BF)

        for f in range(4):
            for k in range(3):
                put(f * 3 + k, gu, 256 * f + 16 * p, 384 * half + 128 * k)
        for k in range(3):
            for i in range(2):
                put(12 + 2 * k + i, down, to // 4 * 48 + 16 * k, to % 4 * 256 + 128 * i)
        for b in range(2):
            for k in range(4):
                put(18 + 4 * b + k, out, 256 * b + 16 * p, 512 * half + 128 * k)
        put(26, dgains, 0, 0)


def feed_grads(parts, norms, mixed, d_branches, dgains):
    return pl.pallas_call(
        feed_grads_kernel,
        out_shape=jax.ShapeDtypeStruct((NCTX, 432, HEAD), BF),
        in_specs=[VMEM] * 8,
        out_specs=VMEM,
        scratch_shapes=[
            pltpu.VMEM((512, 1024), BF),
            pltpu.VMEM((1024, 768), F32),
            pltpu.VMEM((384, 1024), F32),
            pltpu.VMEM((512, 1024), F32),
        ],
        compiler_params=PARAMS,
        cost_estimate=pl.CostEstimate(
            flops=2_900_000_000, bytes_accessed=12_000_000, transcendentals=0
        ),
        name="feed_grads",
    )(parts, norms, mixed, *d_branches, dgains)


def feed_finish_kernel(tiles, gate, up, down, out):
    for c in range(NCTX):
        p, half = c // 2, c % 2
        for n in range(24):
            (up if half else gate)[pl.ds(16 * p, 16), pl.ds(128 * n, 128)] = tiles[c, n].astype(F32)
        for zl in range(2):
            for k in range(3):
                for i in range(2):
                    row = 384 * zl + c // 4 * 48 + 16 * k
                    down[pl.ds(row, 16), pl.ds(c % 4 * 256 + 128 * i, 128)] = tiles[
                        c, 24 + zl * 6 + 2 * k + i
                    ].astype(F32)
        for core in range(2):
            for k in range(4):
                row = 128 * (2 * (p // 8) + core) + 16 * (p % 8)
                out[pl.ds(row, 16), pl.ds(512 * half + 128 * k, 128)] = tiles[
                    c, 36 + 4 * core + k
                ].astype(F32)


def feed_finish(tiles):
    return pl.pallas_call(
        feed_finish_kernel,
        out_shape=(
            jax.ShapeDtypeStruct((256, 3072), F32),
            jax.ShapeDtypeStruct((256, 3072), F32),
            jax.ShapeDtypeStruct((768, 1024), F32),
            jax.ShapeDtypeStruct((512, 1024), F32),
        ),
        in_specs=[VMEM],
        out_specs=(VMEM,) * 4,
        compiler_params=PARAMS,
        cost_estimate=pl.CostEstimate(flops=0, bytes_accessed=18_000_000, transcendentals=0),
        name="feed_finish",
    )(tiles)


def project_finish_kernel(parts, gq, gk, gv):
    for p in range(16):
        rows = pl.ds(16 * p, 16)
        for f in range(4):
            zh, core = f // 2, f % 2
            for n in range(4):
                gq[rows, pl.ds((8 * zh + 2 * n + core) * HEAD, HEAD)] = parts[
                    2 * p, :, pl.ds(512 * f + HEAD * n, HEAD)
                ].astype(F32)
            (gv if core else gk)[rows, pl.ds(512 * zh, 512)] = parts[
                2 * p + 1, :, pl.ds(512 * f, 512)
            ].astype(F32)


def project_finish(parts):
    return pl.pallas_call(
        project_finish_kernel,
        out_shape=(
            jax.ShapeDtypeStruct((256, 2048), F32),
            jax.ShapeDtypeStruct((256, 1024), F32),
            jax.ShapeDtypeStruct((256, 1024), F32),
        ),
        in_specs=[VMEM],
        out_specs=(VMEM,) * 3,
        compiler_params=PARAMS,
        cost_estimate=pl.CostEstimate(flops=0, bytes_accessed=6_000_000, transcendentals=0),
        name="project_finish",
    )(parts)


def merge_kernel(place, recv, wo, mixed, keep, give):
    for j in range(4):
        base = (place[0] ^ j) * 8
        for h in range(4):
            parts = []
            for b in range(2):
                for half in range(2):
                    parts.append(recv[base + h * 2 + half, pl.ds(b * PART, PART), :])
            mixed[pl.ds(j * ROWS, ROWS), pl.ds(h * HEAD, HEAD)] = jnp.concatenate(parts, axis=0)
    for j in (1, 3, 0, 2):
        y = dot(mixed[pl.ds(j * ROWS, ROWS), :], wo[...])
        if j % 2:
            give[j // 2] = y.astype(BF)
        else:
            keep[j // 2] = y


def merge(place, recv, wo):
    return pl.pallas_call(
        merge_kernel,
        out_shape=(
            jax.ShapeDtypeStruct((512, 512), BF),
            jax.ShapeDtypeStruct((2, ROWS, 1024), F32),
            jax.ShapeDtypeStruct((2, ROWS, 1024), BF),
        ),
        in_specs=[SMEM] + [VMEM] * 2,
        out_specs=(VMEM, VMEM, VMEM),
        compiler_params=PARAMS,
        cost_estimate=pl.CostEstimate(
            flops=540_000_000, bytes_accessed=4_000_000, transcendentals=0
        ),
        name="merge",
    )(place, recv, wo)


def split_kernel(place, d0, d1, d2, d3, wo, send):
    for j, d in enumerate((d0, d1, d2, d3)):
        base = (place[0] ^ j) * 8
        y = dot_nt(d[...], wo[...]).astype(BF)
        for h in range(4):
            for b in range(2):
                for half in range(2):
                    at = b * 64 + half * PART
                    send[base + h * 2 + half, pl.ds(b * PART, PART), :] = y[
                        at : at + PART, h * HEAD : (h + 1) * HEAD
                    ]


def split(place, ds, wo):
    return pl.pallas_call(
        split_kernel,
        out_shape=jax.ShapeDtypeStruct((NCTX, 64, HEAD), BF),
        in_specs=[SMEM] + [VMEM] * 5,
        out_specs=VMEM,
        compiler_params=PARAMS,
        cost_estimate=pl.CostEstimate(
            flops=10_000_000, bytes_accessed=10_000, transcendentals=0
        ),
        name="split",
    )(place, *ds, wo)


def feed_kernel(
    place,
    a,
    hidden,
    x,
    g,
    gains,
    gate0,
    up0,
    down0,
    gate1,
    up1,
    down1,
    cat2,
    cat3,
    result,
    d_hidden,
    d_branch,
    norms,
    eighths,
    dgains,
    w,
    sems,
    parts,
    hb,
    gate,
    up,
    dh,
):
    copies = []

    def fetch(src, dst):
        copy = pltpu.make_async_copy(src, dst, sems.at[len(copies)])
        copy.start()
        copies.append(copy)

    for j, (gate_src, up_src) in enumerate(((gate0, up0), (gate1, up1))):
        fetch(gate_src, w.at[j, :, :, pl.ds(0, 3072)])
        fetch(up_src, w.at[j, :, :, pl.ds(3072, 3072)])
    for n in range(6):
        for j, src in ((2, cat2), (3, cat3)):
            fetch(src.at[:, pl.ds(16 * n, 16), :], w.at[j, :, :, pl.ds(1024 * n, 1024)])
    first_needed = len(copies)
    for n in range(3):
        at = pl.ds(6144 + 1024 * n, 1024)
        for j, src in ((0, down0), (1, down1)):
            fetch(src.at[pl.ds(16 * n, 16), :, :], w.at[j, :, :, at])
        for j, src in ((2, cat2), (3, cat3)):
            fetch(src.at[:, pl.ds(96 + 16 * n, 16), :], w.at[j, :, :, at])

    def rows_of(j, at, width):
        return w[j, :, :, pl.ds(at, width)].reshape(256, width)

    me = place[0]
    gain_a, gain_m = gains[pl.ds(0, 1), :], gains[pl.ds(1, 1), :]
    inverse_a = rms(a[...])
    normed_a = a[...] * inverse_a
    h = x[...].astype(F32) + normed_a * gain_a
    for n in range(4):
        hb[n] = hidden[:, pl.ds(256 * n, 256)]
    norms[:, pl.ds(0, 1024)] = hidden[...]
    for copy in copies[:first_needed]:
        copy.wait()
    for n in range(4):
        at = 768 * n
        u = dot(hb[me], rows_of(0, at, 768))
        v = dot(hb[me], rows_of(0, 3072 + at, 768))
        for j in range(1, 4):
            u = u + dot(hb[me ^ j], rows_of(j, at, 768))
            v = v + dot(hb[me ^ j], rows_of(j, 3072 + at, 768))
        gate[n] = u
        up[n] = v
        parts[n, :, pl.ds(0, 768)] = (u / (1.0 + jnp.exp(-u)) * v).astype(BF)
    for copy in copies[first_needed:]:
        copy.wait()
    z = jnp.zeros((ROWS, 1024), F32)
    for j in range(4):
        for b in range(3):
            z = z + dot(
                parts[me ^ j, :, pl.ds(256 * b, 256)], rows_of(j, 6144 + 1024 * b, 1024)
            )
    inverse_z = rms(z)
    normed_z = z * inverse_z
    result[...] = (h + normed_z * gain_m).astype(BF)
    e = g[...].astype(F32)
    dgains[pl.ds(1, 1), :] = jnp.sum(e * normed_z, axis=0, keepdims=True)
    weighted = e * gain_m
    dz = inverse_z * (weighted - normed_z * jnp.mean(weighted * normed_z, axis=-1, keepdims=True))
    dz = dz.astype(BF)
    norms[:, pl.ds(1024, 1024)] = dz
    for j in range(4):
        n = me ^ j
        for b in range(3):
            at = pl.ds(256 * b, 256)
            d_act = dot_nt(dz, rows_of(j, 6144 + 1024 * b, 1024))
            u, v = gate[n, :, at], up[n, :, at]
            s = 1.0 / (1.0 + jnp.exp(-u))
            parts[n, :, pl.ds(768 + 256 * b, 256)] = (
                d_act * v * (s * (1.0 + u * (1.0 - s)))
            ).astype(BF)
            parts[n, :, pl.ds(1536 + 256 * b, 256)] = (d_act * (u * s)).astype(BF)
    for n in range(8):
        for k in range(3):
            eighths[n, :, pl.ds(384 * k, 384)] = parts[
                n % 4, :, pl.ds(768 * k + 384 * (n // 4), 384)
            ]
    for j in range(4):
        total = jnp.zeros((ROWS, 256), F32)
        for n in range(4):
            total = total + dot_nt(parts[n, :, pl.ds(768, 768)], rows_of(j, 768 * n, 768))
            total = total + dot_nt(
                parts[n, :, pl.ds(1536, 768)], rows_of(j, 3072 + 768 * n, 768)
            )
        dh[me ^ j] = total
    total = g[...].astype(F32) + jnp.concatenate([dh[n] for n in range(4)], axis=1)
    d_hidden[...] = total
    dgains[pl.ds(0, 1), :] = jnp.sum(total * normed_a, axis=0, keepdims=True)
    weighted = total * gain_a
    d_branch[...] = (
        inverse_a * (weighted - normed_a * jnp.mean(weighted * normed_a, axis=-1, keepdims=True))
    ).astype(BF)


def feed(place, a, hidden, x, g, gains, weights):
    return pl.pallas_call(
        feed_kernel,
        out_shape=(
            jax.ShapeDtypeStruct((ROWS, 1024), BF),
            jax.ShapeDtypeStruct((ROWS, 1024), F32),
            jax.ShapeDtypeStruct((ROWS, 1024), BF),
            jax.ShapeDtypeStruct((ROWS, 2048), BF),
            jax.ShapeDtypeStruct((8, ROWS, 1152), BF),
            jax.ShapeDtypeStruct((2, 1024), F32),
        ),
        in_specs=[SMEM] + [VMEM] * 5 + [ANY] * 8,
        out_specs=(VMEM,) * 6,
        scratch_shapes=[
            pltpu.VMEM((4, 16, 16, 9216), BF),
            pltpu.SemaphoreType.DMA((28,)),
            pltpu.VMEM((4, ROWS, 2304), BF),
            pltpu.VMEM((4, ROWS, 256), BF),
            pltpu.VMEM((4, ROWS, 768), F32),
            pltpu.VMEM((4, ROWS, 768), F32),
            pltpu.VMEM((4, ROWS, 256), F32),
        ],
        compiler_params=LARGE,
        cost_estimate=pl.CostEstimate(
            flops=10_000_000, bytes_accessed=10_000, transcendentals=0
        ),
        name="feed_forward",
    )(
        place,
        a,
        hidden,
        x,
        g,
        gains,
        *[v.reshape(-1, 16, v.shape[1]) for v in weights[:6]],
        *[v.reshape(16, -1, 1024) for v in weights[6:]],
    )


SWAP = [(0, 1), (1, 0)]


def swap(x, axis):
    return lax.ppermute(x, axis, SWAP)


def in_order(place, own, other):
    return jnp.where(place == 0, jnp.stack([own, other]), jnp.stack([other, own]))


def relative(x):
    far = swap(x, "zh")
    return [x, swap(x, "core"), far, swap(far, "core")]


def exchange(x, axes):
    return lax.all_to_all(x, axes, split_axis=0, concat_axis=0, tiled=True)


def after(xs, *others):
    return lax.optimization_barrier((xs,) + others)[0]


def local(
    tokens,
    cotangent,
    doc_ids,
    wq,
    wk,
    wv,
    wo,
    q_gain,
    k_gain,
    attn_gain,
    w_gate,
    w_up,
    w_down,
    mlp_gain,
):
    c = lax.axis_index(CTX)
    f = lax.axis_index(FSDP)
    place = f[None].astype(jnp.int32)
    inputs = tokens.reshape(ROWS, 1024)

    core = lax.axis_index("core")
    wkv = jnp.concatenate([wk, wv], axis=1)
    own, near, quarter = deal(jnp.stack([f, lax.axis_index("x")]).astype(jnp.int32), wq, wkv)
    near = swap(near, "core")
    quarter = swap(quarter, "zh")
    quarter = jnp.stack([quarter[0], swap(quarter[1], "core")])
    quarter = exchange(jnp.broadcast_to(quarter[None], (4, 2, 64, 1024)), ("x",))

    spot = lax.axis_index("y") * 4 + lax.axis_index("x")
    pack = pack_group(
        spot[None].astype(jnp.int32),
        inputs,
        doc_ids,
        (q_gain[None], k_gain[None], jnp.stack([attn_gain, mlp_gain])),
        (w_gate, w_up, w_down),
    )
    group = lax.all_gather(pack, FSDP, axis=0, tiled=True).reshape(4, 288, 1024)
    gains = group[:, ROWS].astype(F32)
    gains_qk = jnp.stack([gains[:, :32].reshape(HEAD), gains[:, 128:160].reshape(HEAD)])
    gains_am = jnp.stack([gains[:, 512:768].reshape(1024), gains[:, 768:].reshape(1024)])
    starts_f = (gains[:, 256:261] * 64.0 + gains[:, 384:389]).astype(jnp.int32)
    far = lax.dynamic_slice(group, (f ^ 2, ROWS + 16, 0), (1, 144, 1024))[0]
    far = lax.all_gather(far, PLANE, axis=0, tiled=True)

    step = jnp.arange(BLOCK, dtype=jnp.int32)
    spot = jnp.concatenate([c * BLOCK + step, (2 * NCTX - 1 - c) * BLOCK + step])
    start = jnp.max(
        jnp.where(starts_f[:, :, None] <= spot[None, None, :], starts_f[:, :, None], 0), axis=1
    )
    position = spot[None, :] - start
    half = jnp.arange(HEAD, dtype=jnp.int32) % (HEAD // 2)
    frequency = jnp.exp(half.astype(F32) * (-2.0 * math.log(THETA) / HEAD))
    angles = position.astype(F32)[:, :, None] * frequency
    sign = jnp.where(jnp.arange(HEAD) < HEAD // 2, -1.0, 1.0).astype(F32)
    cos, sin = jnp.cos(angles), jnp.sin(angles) * sign

    send, qk, tokens_f, w_qkv = project(place, group, own, near, quarter, cos, sin, gains_qk)
    recv = exchange(send, CTX)
    near = (swap(w_gate, "core"), swap(w_up, "core"), swap(w_down, "core"))
    pairs = wo.reshape(2, 2, HEAD, 1024)
    heads = lax.dynamic_index_in_dim(pairs, core, 1, keepdims=False)
    others = swap(lax.dynamic_index_in_dim(pairs, 1 - core, 1, keepdims=False), "core")
    wo = in_order(core, heads, others).reshape(512, 1024)
    recv, near, wo = lax.optimization_barrier((recv, near, wo))
    other = swap(recv, "core")
    my_starts = lax.dynamic_index_in_dim(starts_f, c // 8, 0, keepdims=False)
    meta = [(c % 2)[None].astype(jnp.int32), my_starts, core[None].astype(jnp.int32)]
    meta = jnp.concatenate(meta + [jnp.zeros((1,), jnp.int32)])
    mixed_t, ot, lsum = attend(meta, recv, other)
    far = after(far, mixed_t)
    mixed_t = exchange(mixed_t, CTX)
    feed_weights = (
        w_gate,
        w_up,
        w_down,
        *near,
        far,
        swap(far, "core"),
    )
    mixed, keep, give = merge(place, mixed_t, wo)
    got = swap(give, "core")
    last = swap((keep[1] + got[1].astype(F32)).astype(BF), "zh")
    branch = keep[0] + got[0].astype(F32) + last.astype(F32)
    hidden = branch * rms(branch) * gains_am[0] + inputs.astype(F32)
    hidden = hidden.astype(BF)
    result, d_hidden, d_branch, norms, parts, d_gains_am = feed(
        place, branch, hidden, inputs, cotangent.reshape(ROWS, 1024), gains_am, feed_weights
    )
    norms = lax.all_gather(norms, COLUMN, axis=0, tiled=True)
    d_branches = relative(d_branch)
    drecv = exchange(split(place, d_branches, wo), CTX)

    parts = exchange(after(parts, drecv), COLUMN).reshape(1024, 1152)
    dq, keep, give = attend_back(meta, recv, other, drecv, ot, lsum)
    keep = (keep.astype(F32) + swap(give, "core").astype(F32)).astype(BF)
    back = jnp.concatenate([dq, keep], axis=1)
    parts = after(parts, back)
    back = exchange(after(back, parts), CTX)
    g_feed = feed_grads(parts, norms, mixed, d_branches, d_gains_am.reshape(16, HEAD))
    g_feed = exchange(after(g_feed, back), CTX)

    d_qkv, g_qkv, d_gains_qk = project_back(place, back, qk, cos, sin, gains_qk, tokens_f)

    partial = dot_nt(d_qkv, w_qkv).reshape(4, ROWS, 1024)
    got = swap(jnp.stack([partial[1], partial[3]]).astype(BF), "core").astype(F32)
    last = swap((partial[2] + got[1]).astype(BF), "zh").astype(F32)
    d_inputs = d_hidden + partial[0] + got[0] + last

    g_feed, g_qkv, d_inputs = lax.optimization_barrier((g_feed, g_qkv, d_inputs))
    g_feed = g_feed.reshape(16, 2, 27, 16, HEAD)
    g_out = jnp.sum(g_feed[:, :, 18:].astype(F32), axis=(0, 1))
    d_gains_am = g_out[8]
    g_out = g_out[:8].astype(BF).reshape(2, 4, 16, HEAD)
    others = swap(lax.dynamic_index_in_dim(g_out, 1 - core, 0, keepdims=False), "core")
    g_out = lax.dynamic_index_in_dim(g_out, core, 0, keepdims=False)
    g_out = in_order(core, g_out, others).reshape(8, 16, HEAD)
    g_feed = jnp.sum(g_feed[:, :, :18].astype(F32), axis=0).astype(BF)
    g_gu = g_feed[:, :12].reshape(2, 4, 3, 16, HEAD).swapaxes(0, 1)
    g_gu = jnp.broadcast_to(g_gu[None], (2, 4, 2, 3, 16, HEAD)).reshape(8, 96, HEAD)
    g_gu = exchange(g_gu, COLUMN).reshape(2, 384, HEAD)
    g_feed = jnp.concatenate([g_feed[:, 12:].reshape(12, 16, HEAD), g_out], axis=0)
    g_feed = g_feed.reshape(320, HEAD)
    g_feed = in_order(lax.axis_index("zl"), g_feed, swap(g_feed, "zl"))
    g_feed = jnp.concatenate([g_gu, g_feed], axis=1)
    g_qkv = after(g_qkv, g_feed)
    g_feed = lax.all_gather(g_feed, PLANE, axis=0, tiled=True).reshape(NCTX, 44, 16, HEAD)

    g_qkv = exchange(g_qkv, AXES)
    gains = jnp.concatenate([d_gains_am, d_gains_qk, jnp.zeros((14, HEAD), F32)], axis=0)
    gains = gains + swap(gains.astype(BF), "core").astype(F32)
    gains = gains + swap(gains.astype(BF), "zh").astype(F32)

    g_qkv, gains = lax.optimization_barrier((g_qkv, gains))
    g_qkv = jnp.sum(g_qkv.reshape(NCTX, 4, 16, 512).astype(F32), axis=0)
    g_qkv = g_qkv.swapaxes(0, 1).reshape(16, 2048)
    g_qkv = jnp.concatenate([g_qkv, gains[16:]], axis=1).astype(BF)
    g_qkv = exchange(jnp.broadcast_to(g_qkv[None], (NCTX, 16, 2176)), CTX)
    gate_grad, up_grad, down_grad, out_grad = feed_finish(g_feed)
    g_qkv = after(g_qkv, gate_grad)
    gains_qk = jnp.sum(g_qkv[:, :2, 2048:].astype(F32), axis=0)
    gains_am = lax.dynamic_index_in_dim(gains[:16].reshape(2, 4, 256), f, 1, keepdims=False)

    g_q, g_k, g_v = project_finish(g_qkv)
    gains_qk = lax.dynamic_slice_in_dim(gains_qk, f * 32, 32, 1)
    return (
        result.reshape(tokens.shape),
        d_inputs.reshape(tokens.shape),
        g_q,
        g_k,
        g_v,
        out_grad,
        gains_qk[0],
        gains_qk[1],
        gains_am[0],
        gate_grad,
        up_grad,
        down_grad,
        gains_am[1],
    )


def solution(mesh):
    whole = Mesh(mesh.devices.reshape(4, 4, 2, 2, 2), AXES)
    blocks = P(FSDP, None, CTX, None, None)
    rows = P(FSDP, None)
    vector = P(FSDP)
    return jax.shard_map(
        local,
        mesh=whole,
        in_specs=(
            blocks,
            blocks,
            rows,
            rows,
            rows,
            rows,
            rows,
            vector,
            vector,
            vector,
            rows,
            rows,
            rows,
            vector,
        ),
        out_specs=(
            blocks,
            blocks,
            rows,
            rows,
            rows,
            rows,
            vector,
            vector,
            vector,
            rows,
            rows,
            rows,
            vector,
        ),
        check_vma=False,
    )
```

```python
import math

import jax
import jax.numpy as jnp
from jax import lax
from jax.experimental import pallas as pl
from jax.experimental.pallas import tpu as pltpu
from jax.sharding import Mesh, PartitionSpec as P

HEADS = 16
KV_HEADS = 8
HEAD = 128
EPS = 1e-06
THETA = 500000.0

AXES = ("y", "x", "zl", "zh", "core")
CTX = ("y", "x", "zl")
PLANE = ("y", "x")
FSDP = ("zh", "core")
COLUMN = ("zl", "zh", "core")
NCTX = 32
SEQS = 4
BLOCK = 64
ROWS = 2 * BLOCK
LEN = 4096
DOCS = 5
PART = 32
TILES = 8
QT = 256
KT = 512
CHUNK = 192
BF = jnp.bfloat16
F32 = jnp.float32
SCALE = HEAD**-0.5
LOG2E = math.log2(math.e)


def key_block(j):
    return (j, 0) if j < NCTX else (2 * NCTX - 1 - j, 1)


def tile_bounds(meta, t):
    first, last = t * KT, t * KT + KT - 1
    low = jnp.int32(0)
    high = jnp.int32(0)
    for d in range(1, DOCS):
        start = meta[1 + d]
        low = jnp.where(start <= first, start, low)
        high = jnp.where(start <= last, start, high)
    return lax.div(low, KT), jnp.minimum(lax.div(high + (KT - 1), KT), t)


def row_places(meta, t):
    lane = lax.broadcasted_iota(jnp.int32, (1, QT), 1)
    place = t * KT + lax.div(lane, PART) * BLOCK + meta[0] * PART + lax.rem(lane, PART)
    start = jnp.zeros((1, QT), jnp.int32)
    for d in range(1, DOCS):
        start = jnp.where(place >= meta[1 + d], meta[1 + d], start)
    return place, start


def allowed(kt, place, start):
    key = kt * KT + lax.broadcasted_iota(jnp.int32, (KT, QT), 0)
    return (key <= place) & (key >= start)


def gather_rows(src, t):
    parts = []
    for i in range(8):
        c, b = key_block(8 * t + i)
        parts.append(src[c, pl.ds(b * PART, PART), :])
    return jnp.concatenate(parts, axis=0)


def sort_keys(src, dst):
    for j in range(2 * NCTX):
        c, b = key_block(j)
        dst[pl.ds(j * BLOCK, BLOCK), :] = src[c, pl.ds(64 + b * BLOCK, BLOCK), :]


def sort_both(meta, mine, other, ks, vs):
    @pl.when(meta[6] == 0)
    def _():
        sort_keys(mine, ks)
        sort_keys(other, vs)

    @pl.when(meta[6] != 0)
    def _():
        sort_keys(other, ks)
        sort_keys(mine, vs)


def put_rows(out, t, rows):
    for i in range(8):
        j = 8 * t + i
        half = (j >= NCTX).astype(jnp.int32)
        c = jnp.where(half == 0, j, 2 * NCTX - 1 - j)
        out[c, pl.ds(pl.multiple_of(half * PART, PART), PART), :] = rows[i * PART : (i + 1) * PART]


def transposed(x):
    return x.astype(F32).T.astype(x.dtype)


def forward_kernel(meta, mine, other, out, ot, lsum, ks, vs, vt, qt):
    sort_both(meta, mine, other, ks, vs)
    for i in range(TILES):
        vt[i] = transposed(vs[pl.ds(i * KT, KT), :])
        qt[i] = transposed(gather_rows(mine, i))

    def query_tile(t, _):
        q = qt[t]
        place, start = row_places(meta, t)
        low, clear = tile_bounds(meta, t)

        def step(kt, carry, masked):
            total, mixed = carry
            k = ks[pl.ds(pl.multiple_of(kt * KT, KT), KT), :]
            s = jnp.dot(k, q, preferred_element_type=F32)
            p = jnp.exp2(s * (SCALE * LOG2E))
            if masked:
                p = jnp.where(allowed(kt, place, start), p, 0.0)
            total = total + jnp.sum(p, axis=0, keepdims=True)
            mixed = mixed + jnp.dot(vt[kt], p.astype(BF), preferred_element_type=F32)
            return total, mixed

        carry = (jnp.zeros((1, QT), F32), jnp.zeros((HEAD, QT), F32))
        carry = lax.fori_loop(low, clear, lambda kt, cr: step(kt, cr, True), carry)
        carry = lax.fori_loop(jnp.maximum(low, clear), t, lambda kt, cr: step(kt, cr, False), carry)
        total, mixed = step(t, carry, True)
        mixed = mixed * (1.0 / total)
        ot[t] = mixed
        lsum[t] = total
        rows = mixed.T.astype(BF)
        put_rows(out, t, rows)
        return 0

    lax.fori_loop(0, TILES, query_tile, 0)


def backward_kernel(
    meta, mine, other, drecv, ot, lsum, out, keep, give, ks, vs, kt_, q_, qt, do_, dot_, dk, dv
):
    sort_both(meta, mine, other, ks, vs)
    for i in range(TILES):
        kt_[i] = transposed(ks[pl.ds(i * KT, KT), :])
        rows = gather_rows(mine, i)
        q_[i] = rows
        qt[i] = transposed(rows)
        rows = gather_rows(drecv, i)
        do_[i] = rows
        dot_[i] = transposed(rows)
    dk[...] = jnp.zeros_like(dk)
    dv[...] = jnp.zeros_like(dv)

    def query_tile(t, _):
        q, q_t, d, d_t = q_[t], qt[t], do_[t], dot_[t]
        place, start = row_places(meta, t)
        low, clear = tile_bounds(meta, t)
        delta = jnp.sum(d_t.astype(F32) * ot[t], axis=0, keepdims=True)
        shift = jnp.log2(lsum[t])

        def step(kt, total, masked):
            at = pl.ds(pl.multiple_of(kt * KT, KT), KT)
            s = jnp.dot(ks[at, :], q_t, preferred_element_type=F32)
            p = jnp.exp2(s * (SCALE * LOG2E) - shift)
            if masked:
                p = jnp.where(allowed(kt, place, start), p, 0.0)
            dv[at, :] += jnp.dot(p.astype(BF), d, preferred_element_type=F32)
            dp = jnp.dot(vs[at, :], d_t, preferred_element_type=F32)
            ds = (p * (dp - delta)).astype(BF)
            dk[at, :] += jnp.dot(ds, q, preferred_element_type=F32)
            return total + jnp.dot(kt_[kt], ds, preferred_element_type=F32)

        total = jnp.zeros((HEAD, QT), F32)
        total = lax.fori_loop(low, clear, lambda kt, cr: step(kt, cr, True), total)
        total = lax.fori_loop(jnp.maximum(low, clear), t, lambda kt, cr: step(kt, cr, False), total)
        total = step(t, total, True)
        rows = (total * SCALE).T.astype(BF)
        put_rows(out, t, rows)
        return 0

    lax.fori_loop(0, TILES, query_tile, 0)

    def unsort(src, scale, dst):
        for j in range(2 * NCTX):
            c, b = key_block(j)
            dst[c, pl.ds(b * BLOCK, BLOCK), :] = (src[pl.ds(j * BLOCK, BLOCK), :] * scale).astype(BF)

    @pl.when(meta[6] == 0)
    def _():
        unsort(dk, SCALE, keep)
        unsort(dv, 1.0, give)

    @pl.when(meta[6] != 0)
    def _():
        unsort(dv, 1.0, keep)
        unsort(dk, SCALE, give)


VMEM = pl.BlockSpec(memory_space=pltpu.VMEM)
SMEM = pl.BlockSpec(memory_space=pltpu.SMEM)
ANY = pl.BlockSpec(memory_space=pl.ANY)
PARAMS = pltpu.CompilerParams(vmem_limit_bytes=48 * 1024 * 1024)
LARGE = pltpu.CompilerParams(vmem_limit_bytes=60 * 1024 * 1024)


def attend(meta, mine, other):
    return pl.pallas_call(
        forward_kernel,
        out_shape=(
            jax.ShapeDtypeStruct((NCTX, 64, HEAD), BF),
            jax.ShapeDtypeStruct((TILES, HEAD, QT), F32),
            jax.ShapeDtypeStruct((TILES, 1, QT), F32),
        ),
        in_specs=[SMEM, VMEM, VMEM],
        out_specs=(VMEM, VMEM, VMEM),
        scratch_shapes=[
            pltpu.VMEM((LEN, HEAD), BF),
            pltpu.VMEM((LEN, HEAD), BF),
            pltpu.VMEM((TILES, HEAD, KT), BF),
            pltpu.VMEM((TILES, HEAD, QT), BF),
        ],
        compiler_params=PARAMS,
        cost_estimate=pl.CostEstimate(
            flops=15_000_000_000, bytes_accessed=5_000_000, transcendentals=4_700_000
        ),
        name="attention_forward",
    )(meta, mine, other)


def attend_back(meta, mine, other, drecv, ot, lsum):
    return pl.pallas_call(
        backward_kernel,
        out_shape=(
            jax.ShapeDtypeStruct((NCTX, 64, HEAD), BF),
            jax.ShapeDtypeStruct((NCTX, ROWS, HEAD), BF),
            jax.ShapeDtypeStruct((NCTX, ROWS, HEAD), BF),
        ),
        in_specs=[SMEM] + [VMEM] * 5,
        out_specs=(VMEM,) * 3,
        scratch_shapes=[
            pltpu.VMEM((LEN, HEAD), BF),
            pltpu.VMEM((LEN, HEAD), BF),
            pltpu.VMEM((TILES, HEAD, KT), BF),
            pltpu.VMEM((TILES, QT, HEAD), BF),
            pltpu.VMEM((TILES, HEAD, QT), BF),
            pltpu.VMEM((TILES, QT, HEAD), BF),
            pltpu.VMEM((TILES, HEAD, QT), BF),
            pltpu.VMEM((LEN, HEAD), F32),
            pltpu.VMEM((LEN, HEAD), F32),
        ],
        compiler_params=PARAMS,
        cost_estimate=pl.CostEstimate(
            flops=10_000_000, bytes_accessed=10_000, transcendentals=0
        ),
        name="attention_backward",
    )(meta, mine, other, drecv, ot, lsum)


def rms(u):
    return lax.rsqrt(jnp.mean(u * u, axis=-1, keepdims=True) + EPS)


def dot(a, b):
    return jnp.dot(a, b, preferred_element_type=F32)


def dot_nt(a, b):
    return lax.dot_general(a, b, (((1,), (1,)), ((), ())), preferred_element_type=F32)


def dot_tn(a, b):
    return lax.dot_general(a, b, (((0,), (0,)), ((), ())), preferred_element_type=F32)


def pack_kernel(at, x, docs, q_gain, k_gain, am_gain, gate, up, down, out, row, sem):
    copies = []
    for n in range(3):
        for src, row_at, lane_at, width in (
            (gate, 0, 1024 * n, 1024),
            (up, 0, 1024 * n, 1024),
            (down, 256 * n, 0, 1024),
        ):
            k = len(copies)
            first = pl.multiple_of(row_at + at[0] * 16, 16)
            copies.append(
                pltpu.make_async_copy(
                    src.at[pl.ds(first, 16), pl.ds(lane_at, width)],
                    out.at[pl.ds(144 + 16 * (3 * (k % 3) + n), 16), :],
                    sem.at[k],
                )
            )
            copies[-1].start()
    out[pl.ds(0, ROWS), :] = x[...]
    row[...] = jnp.zeros_like(row)
    row[:, pl.ds(0, 32)] = q_gain[...].astype(F32)
    row[:, pl.ds(128, 32)] = k_gain[...].astype(F32)
    lane = lax.broadcasted_iota(jnp.int32, (1, HEAD), 1)
    high = jnp.zeros((1, HEAD), F32)
    low = jnp.zeros((1, HEAD), F32)
    for d in range(1, DOCS):
        start = jnp.sum((docs[...] < d).astype(F32), axis=1, keepdims=True)
        whole = jnp.floor(start * (1.0 / 64.0))
        high = jnp.where(lane == d, whole, high)
        low = jnp.where(lane == d, start - whole * 64.0, low)
    row[:, pl.ds(256, HEAD)] = high
    row[:, pl.ds(384, HEAD)] = low
    row[:, pl.ds(512, 256)] = am_gain[pl.ds(0, 1), :].astype(F32)
    row[:, pl.ds(768, 256)] = am_gain[pl.ds(1, 1), :].astype(F32)
    out[pl.ds(ROWS, 16), :] = jnp.broadcast_to(row[...], (16, 1024)).astype(BF)
    for copy in copies:
        copy.wait()


def pack_group(at, x, docs, gains, weights):
    return pl.pallas_call(
        pack_kernel,
        out_shape=jax.ShapeDtypeStruct((288, 1024), BF),
        in_specs=[SMEM] + [VMEM] * 5 + [ANY] * 3,
        out_specs=VMEM,
        scratch_shapes=[pltpu.VMEM((1, 1024), F32), pltpu.SemaphoreType.DMA((9,))],
        compiler_params=LARGE,
        name="pack_group",
    )(at, x, docs, *gains, *weights)


def deal_kernel(place, wq, wkv, own, near, far, sem):
    copies = []

    def columns(f, dst, rows):
        zh, core = lax.div(f, 2), lax.rem(f, 2)
        slices = [(wq, (8 * zh + 2 * n + core) * HEAD, HEAD, n * HEAD) for n in range(4)]
        for src, lane, width, at in slices + [(wkv, 1024 * core + 512 * zh, 512, 512)]:
            lanes = pl.ds(pl.multiple_of(lane, HEAD), width)
            copies.append(
                pltpu.make_async_copy(
                    src.at[rows, lanes], dst.at[:, pl.ds(at, width)], sem.at[len(copies)]
                )
            )
            copies[-1].start()

    quarter = pl.ds(pl.multiple_of(place[1] * 64, 64), 64)
    columns(place[0] ^ 2, far.at[0], quarter)
    columns(place[0] ^ 3, far.at[1], quarter)
    columns(place[0] ^ 1, near, pl.ds(0, 256))
    columns(place[0], own, pl.ds(0, 256))
    for copy in copies:
        copy.wait()


def deal(place, wq, wkv):
    return pl.pallas_call(
        deal_kernel,
        out_shape=(
            jax.ShapeDtypeStruct((256, 1024), BF),
            jax.ShapeDtypeStruct((256, 1024), BF),
            jax.ShapeDtypeStruct((2, 64, 1024), BF),
        ),
        in_specs=[SMEM] + [ANY] * 2,
        out_specs=(VMEM,) * 3,
        scratch_shapes=[pltpu.SemaphoreType.DMA((20,))],
        compiler_params=LARGE,
        name="deal",
    )(place, wq, wkv)


def project_kernel(place, group, own, near, far, cos, sin, gains, send, qk, tokens, w):
    w[pl.ds(pl.multiple_of(place[0] * 256, 256), 256), :] = own[...]
    w[pl.ds(pl.multiple_of((place[0] ^ 1) * 256, 256), 256), :] = near[...]
    for i in range(4):
        for k in range(2):
            at = pl.multiple_of((place[0] ^ (2 + k)) * 256 + 64 * i, 64)
            w[pl.ds(at, 64), :] = far[i, k]
    for j in range(4):
        n = place[0] ^ j
        base = n * 8
        rows = pl.ds(j * ROWS, ROWS)
        x = group[n, pl.ds(0, ROWS), :]
        tokens[rows, :] = x
        y = dot(x, w[...])
        c, s = cos[n], sin[n]
        qk[rows, :] = y
        core = lax.rem(place[0], 2)
        for h in range(8):
            v = y[:, h * HEAD : (h + 1) * HEAD]
            u = v * rms(v) * gains[pl.ds(h // 4, 1), :]
            u = u * c + pltpu.roll(u, HEAD // 2, 1) * s
            if h < 4:
                u = u.astype(BF)
                for half in range(2):
                    for b in range(2):
                        at = b * 64 + half * PART
                        send[base + h * 2 + half, pl.ds(b * PART, PART), :] = u[at : at + PART]
            else:
                u = jnp.where(core == 0, u, v).astype(BF)
                for half in range(2):
                    send[base + (h - 4) * 2 + half, pl.ds(64, ROWS), :] = u


def project(place, group, own, near, far, cos, sin, gains):
    return pl.pallas_call(
        project_kernel,
        out_shape=(
            jax.ShapeDtypeStruct((NCTX, CHUNK, HEAD), BF),
            jax.ShapeDtypeStruct((512, 1024), F32),
            jax.ShapeDtypeStruct((512, 1024), BF),
            jax.ShapeDtypeStruct((1024, 1024), BF),
        ),
        in_specs=[SMEM] + [VMEM] * 7,
        out_specs=(VMEM,) * 4,
        compiler_params=PARAMS,
        cost_estimate=pl.CostEstimate(
            flops=60_000_000_000, bytes_accessed=9_000_000, transcendentals=4000
        ),
        name="project",
    )(place, group, own, near, far, cos, sin, gains)


def project_back_kernel(place, back, qk, cos, sin, gains, tokens, out, send, dgains, grads):
    totals = [jnp.zeros((1, HEAD), F32), jnp.zeros((1, HEAD), F32)]
    for j in range(4):
        n = place[0] ^ j
        base = n * 8
        rows = pl.ds(j * ROWS, ROWS)
        c, s = cos[n], sin[n]
        core = lax.rem(place[0], 2)
        for h in range(8):
            at = base + h % 4 * 2
            if h < 4:
                parts = []
                for b in range(2):
                    for half in range(2):
                        parts.append(back[at + half, pl.ds(b * PART, PART), :])
                raw = jnp.concatenate(parts, axis=0).astype(F32)
            else:
                raw = back[at, pl.ds(64, ROWS), :].astype(F32)
                raw = raw + back[at + 1, pl.ds(64, ROWS), :].astype(F32)
            e = raw * c - pltpu.roll(raw, HEAD // 2, 1) * s
            u = qk[rows, pl.ds(h * HEAD, HEAD)]
            inverse = rms(u)
            u = u * inverse
            total = jnp.sum(e * u, axis=0, keepdims=True)
            if h >= 4:
                total = jnp.where(core == 0, total, 0.0)
            totals[h // 4] = totals[h // 4] + total
            e = e * gains[pl.ds(h // 4, 1), :]
            e = inverse * (e - u * jnp.mean(e * u, axis=-1, keepdims=True))
            if h >= 4:
                e = jnp.where(core == 0, e, raw)
            out[rows, pl.ds(h * HEAD, HEAD)] = e.astype(BF)
    grads[...] = dot_tn(tokens[...], out[...])
    for f in range(4):
        for p in range(16):
            for half in range(2):
                send[(p * 2 + half) * 4 + f] = grads[
                    pl.ds(256 * f + 16 * p, 16), pl.ds(512 * half, 512)
                ].astype(BF)
    dgains[...] = jnp.concatenate(totals, axis=0)


def project_back(place, back, qk, cos, sin, gains, tokens):
    return pl.pallas_call(
        project_back_kernel,
        out_shape=(
            jax.ShapeDtypeStruct((512, 1024), BF),
            jax.ShapeDtypeStruct((128, 16, 512), BF),
            jax.ShapeDtypeStruct((2, HEAD), F32),
        ),
        in_specs=[SMEM] + [VMEM] * 6,
        out_specs=(VMEM,) * 3,
        scratch_shapes=[pltpu.VMEM((1024, 1024), F32)],
        compiler_params=PARAMS,
        cost_estimate=pl.CostEstimate(
            flops=60_000_000_000, bytes_accessed=9_000_000, transcendentals=4000
        ),
        name="project_back",
    )(place, back, qk, cos, sin, gains, tokens)


def feed_grads_kernel(pa, hidden, d_mlp, mixed, d0, d1, d2, d3, dgains, send, db, gu, down, out):
    for j, d in enumerate((d0, d1, d2, d3)):
        db[pl.ds(j * ROWS, ROWS), :] = d[...]
    out[...] = dot_tn(mixed[...], db[...])
    gu[...] = dot_tn(hidden[...], pa[:, pl.ds(384, 768)])
    down[...] = dot_tn(pa[:, pl.ds(0, 384)], d_mlp[...])
    for to in range(NCTX):
        p, half = to // 2, to % 2

        def put(tile, ref, row, column):
            send[to, pl.ds(16 * tile, 16), :] = ref[pl.ds(row, 16), pl.ds(column, 128)].astype(BF)

        for f in range(4):
            for k in range(3):
                put(f * 3 + k, gu, 256 * f + 16 * p, 384 * half + 128 * k)
        for k in range(3):
            for i in range(2):
                put(12 + 2 * k + i, down, to // 4 * 48 + 16 * k, to % 4 * 256 + 128 * i)
        for b in range(2):
            for k in range(4):
                put(18 + 4 * b + k, out, 256 * b + 16 * p, 512 * half + 128 * k)
        put(26, dgains, 0, 0)


def feed_grads(parts, hidden, d_mlp, mixed, d_branches, dgains):
    return pl.pallas_call(
        feed_grads_kernel,
        out_shape=jax.ShapeDtypeStruct((NCTX, 432, HEAD), BF),
        in_specs=[VMEM] * 9,
        out_specs=VMEM,
        scratch_shapes=[
            pltpu.VMEM((512, 1024), BF),
            pltpu.VMEM((1024, 768), F32),
            pltpu.VMEM((384, 1024), F32),
            pltpu.VMEM((512, 1024), F32),
        ],
        compiler_params=PARAMS,
        cost_estimate=pl.CostEstimate(
            flops=2_900_000_000, bytes_accessed=12_000_000, transcendentals=0
        ),
        name="feed_grads",
    )(parts, hidden, d_mlp, mixed, *d_branches, dgains)


def feed_finish_kernel(tiles, gate, up, down, out):
    for c in range(NCTX):
        p, half = c // 2, c % 2
        for n in range(24):
            (up if half else gate)[pl.ds(16 * p, 16), pl.ds(128 * n, 128)] = tiles[c, n].astype(F32)
        for zl in range(2):
            for k in range(3):
                for i in range(2):
                    row = 384 * zl + c // 4 * 48 + 16 * k
                    down[pl.ds(row, 16), pl.ds(c % 4 * 256 + 128 * i, 128)] = tiles[
                        c, 24 + zl * 6 + 2 * k + i
                    ].astype(F32)
        for core in range(2):
            for k in range(4):
                row = 128 * (2 * (p // 8) + core) + 16 * (p % 8)
                out[pl.ds(row, 16), pl.ds(512 * half + 128 * k, 128)] = tiles[
                    c, 36 + 4 * core + k
                ].astype(F32)


def feed_finish(tiles):
    return pl.pallas_call(
        feed_finish_kernel,
        out_shape=(
            jax.ShapeDtypeStruct((256, 3072), F32),
            jax.ShapeDtypeStruct((256, 3072), F32),
            jax.ShapeDtypeStruct((768, 1024), F32),
            jax.ShapeDtypeStruct((512, 1024), F32),
        ),
        in_specs=[VMEM],
        out_specs=(VMEM,) * 4,
        compiler_params=PARAMS,
        cost_estimate=pl.CostEstimate(flops=0, bytes_accessed=18_000_000, transcendentals=0),
        name="feed_finish",
    )(tiles)


def project_finish_kernel(parts, gq, gk, gv):
    for p in range(16):
        rows = pl.ds(16 * p, 16)
        for f in range(4):
            zh, core = f // 2, f % 2
            for n in range(4):
                gq[rows, pl.ds((8 * zh + 2 * n + core) * HEAD, HEAD)] = parts[
                    2 * p, :, pl.ds(512 * f + HEAD * n, HEAD)
                ].astype(F32)
            (gv if core else gk)[rows, pl.ds(512 * zh, 512)] = parts[
                2 * p + 1, :, pl.ds(512 * f, 512)
            ].astype(F32)


def project_finish(parts):
    return pl.pallas_call(
        project_finish_kernel,
        out_shape=(
            jax.ShapeDtypeStruct((256, 2048), F32),
            jax.ShapeDtypeStruct((256, 1024), F32),
            jax.ShapeDtypeStruct((256, 1024), F32),
        ),
        in_specs=[VMEM],
        out_specs=(VMEM,) * 3,
        compiler_params=PARAMS,
        cost_estimate=pl.CostEstimate(flops=0, bytes_accessed=6_000_000, transcendentals=0),
        name="project_finish",
    )(parts)


def merge_kernel(place, recv, wo, mixed, keep, give):
    for j in range(4):
        base = (place[0] ^ j) * 8
        for h in range(4):
            parts = []
            for b in range(2):
                for half in range(2):
                    parts.append(recv[base + h * 2 + half, pl.ds(b * PART, PART), :])
            mixed[pl.ds(j * ROWS, ROWS), pl.ds(h * HEAD, HEAD)] = jnp.concatenate(parts, axis=0)
    for j in (1, 3, 0, 2):
        y = dot(mixed[pl.ds(j * ROWS, ROWS), :], wo[...])
        if j % 2:
            give[j // 2] = y.astype(BF)
        else:
            keep[j // 2] = y


def merge(place, recv, wo):
    return pl.pallas_call(
        merge_kernel,
        out_shape=(
            jax.ShapeDtypeStruct((512, 512), BF),
            jax.ShapeDtypeStruct((2, ROWS, 1024), F32),
            jax.ShapeDtypeStruct((2, ROWS, 1024), BF),
        ),
        in_specs=[SMEM] + [VMEM] * 2,
        out_specs=(VMEM, VMEM, VMEM),
        compiler_params=PARAMS,
        cost_estimate=pl.CostEstimate(
            flops=540_000_000, bytes_accessed=4_000_000, transcendentals=0
        ),
        name="merge",
    )(place, recv, wo)


def split_kernel(place, d0, d1, d2, d3, wo, send):
    for j, d in enumerate((d0, d1, d2, d3)):
        base = (place[0] ^ j) * 8
        y = dot_nt(d[...], wo[...]).astype(BF)
        for h in range(4):
            for b in range(2):
                for half in range(2):
                    at = b * 64 + half * PART
                    send[base + h * 2 + half, pl.ds(b * PART, PART), :] = y[
                        at : at + PART, h * HEAD : (h + 1) * HEAD
                    ]


def split(place, ds, wo):
    return pl.pallas_call(
        split_kernel,
        out_shape=jax.ShapeDtypeStruct((NCTX, 64, HEAD), BF),
        in_specs=[SMEM] + [VMEM] * 5,
        out_specs=VMEM,
        compiler_params=PARAMS,
        cost_estimate=pl.CostEstimate(
            flops=10_000_000, bytes_accessed=10_000, transcendentals=0
        ),
        name="split",
    )(place, *ds, wo)


def feed_kernel(
    place,
    a,
    hidden,
    x,
    g,
    gains,
    gate0,
    up0,
    down0,
    gate1,
    up1,
    down1,
    cat2,
    cat3,
    result,
    d_hidden,
    d_branch,
    d_mlp,
    eighths,
    dgains,
    w,
    sems,
    parts,
    hb,
    gate,
    up,
    dh,
):
    copies = []

    def fetch(src, dst):
        copy = pltpu.make_async_copy(src, dst, sems.at[len(copies)])
        copy.start()
        copies.append(copy)

    for j, (gate_src, up_src) in enumerate(((gate0, up0), (gate1, up1))):
        fetch(gate_src, w.at[j, :, :, pl.ds(0, 3072)])
        fetch(up_src, w.at[j, :, :, pl.ds(3072, 3072)])
    for n in range(6):
        for j, src in ((2, cat2), (3, cat3)):
            fetch(src.at[:, pl.ds(16 * n, 16), :], w.at[j, :, :, pl.ds(1024 * n, 1024)])
    first_needed = len(copies)
    for n in range(3):
        at = pl.ds(6144 + 1024 * n, 1024)
        for j, src in ((0, down0), (1, down1)):
            fetch(src.at[pl.ds(16 * n, 16), :, :], w.at[j, :, :, at])
        for j, src in ((2, cat2), (3, cat3)):
            fetch(src.at[:, pl.ds(96 + 16 * n, 16), :], w.at[j, :, :, at])

    def rows_of(j, at, width):
        return w[j, :, :, pl.ds(at, width)].reshape(256, width)

    me = place[0]
    gain_a, gain_m = gains[pl.ds(0, 1), :], gains[pl.ds(1, 1), :]
    inverse_a = rms(a[...])
    normed_a = a[...] * inverse_a
    h = x[...].astype(F32) + normed_a * gain_a
    for n in range(4):
        hb[n] = hidden[:, pl.ds(256 * n, 256)]
    for copy in copies[:first_needed]:
        copy.wait()
    for n in range(4):
        at = 768 * n
        u = dot(hb[me], rows_of(0, at, 768))
        v = dot(hb[me], rows_of(0, 3072 + at, 768))
        for j in range(1, 4):
            u = u + dot(hb[me ^ j], rows_of(j, at, 768))
            v = v + dot(hb[me ^ j], rows_of(j, 3072 + at, 768))
        gate[n] = u
        up[n] = v
        parts[n, :, pl.ds(0, 768)] = (u / (1.0 + jnp.exp(-u)) * v).astype(BF)
    for copy in copies[first_needed:]:
        copy.wait()
    z = jnp.zeros((ROWS, 1024), F32)
    for j in range(4):
        for b in range(3):
            z = z + dot(
                parts[me ^ j, :, pl.ds(256 * b, 256)], rows_of(j, 6144 + 1024 * b, 1024)
            )
    inverse_z = rms(z)
    normed_z = z * inverse_z
    result[...] = (h + normed_z * gain_m).astype(BF)
    e = g[...].astype(F32)
    dgains[pl.ds(1, 1), :] = jnp.sum(e * normed_z, axis=0, keepdims=True)
    weighted = e * gain_m
    dz = inverse_z * (weighted - normed_z * jnp.mean(weighted * normed_z, axis=-1, keepdims=True))
    dz = dz.astype(BF)
    d_mlp[...] = dz
    for j in range(4):
        n = me ^ j
        for b in range(3):
            at = pl.ds(256 * b, 256)
            d_act = dot_nt(dz, rows_of(j, 6144 + 1024 * b, 1024))
            u, v = gate[n, :, at], up[n, :, at]
            s = 1.0 / (1.0 + jnp.exp(-u))
            parts[n, :, pl.ds(768 + 256 * b, 256)] = (
                d_act * v * (s * (1.0 + u * (1.0 - s)))
            ).astype(BF)
            parts[n, :, pl.ds(1536 + 256 * b, 256)] = (d_act * (u * s)).astype(BF)
    for n in range(8):
        for k in range(3):
            eighths[n, :, pl.ds(384 * k, 384)] = parts[
                n % 4, :, pl.ds(768 * k + 384 * (n // 4), 384)
            ]
    for j in range(4):
        total = jnp.zeros((ROWS, 256), F32)
        for n in range(4):
            total = total + dot_nt(parts[n, :, pl.ds(768, 768)], rows_of(j, 768 * n, 768))
            total = total + dot_nt(
                parts[n, :, pl.ds(1536, 768)], rows_of(j, 3072 + 768 * n, 768)
            )
        dh[me ^ j] = total
    total = g[...].astype(F32) + jnp.concatenate([dh[n] for n in range(4)], axis=1)
    d_hidden[...] = total
    dgains[pl.ds(0, 1), :] = jnp.sum(total * normed_a, axis=0, keepdims=True)
    weighted = total * gain_a
    d_branch[...] = (
        inverse_a * (weighted - normed_a * jnp.mean(weighted * normed_a, axis=-1, keepdims=True))
    ).astype(BF)


def feed(place, a, hidden, x, g, gains, weights):
    return pl.pallas_call(
        feed_kernel,
        out_shape=(
            jax.ShapeDtypeStruct((ROWS, 1024), BF),
            jax.ShapeDtypeStruct((ROWS, 1024), F32),
            jax.ShapeDtypeStruct((ROWS, 1024), BF),
            jax.ShapeDtypeStruct((ROWS, 1024), BF),
            jax.ShapeDtypeStruct((8, ROWS, 1152), BF),
            jax.ShapeDtypeStruct((2, 1024), F32),
        ),
        in_specs=[SMEM] + [VMEM] * 5 + [ANY] * 8,
        out_specs=(VMEM,) * 6,
        scratch_shapes=[
            pltpu.VMEM((4, 16, 16, 9216), BF),
            pltpu.SemaphoreType.DMA((28,)),
            pltpu.VMEM((4, ROWS, 2304), BF),
            pltpu.VMEM((4, ROWS, 256), BF),
            pltpu.VMEM((4, ROWS, 768), F32),
            pltpu.VMEM((4, ROWS, 768), F32),
            pltpu.VMEM((4, ROWS, 256), F32),
        ],
        compiler_params=LARGE,
        cost_estimate=pl.CostEstimate(
            flops=10_000_000, bytes_accessed=10_000, transcendentals=0
        ),
        name="feed_forward",
    )(
        place,
        a,
        hidden,
        x,
        g,
        gains,
        *[v.reshape(-1, 16, v.shape[1]) for v in weights[:6]],
        *[v.reshape(16, -1, 1024) for v in weights[6:]],
    )


SWAP = [(0, 1), (1, 0)]


def swap(x, axis):
    return lax.ppermute(x, axis, SWAP)


def in_order(place, own, other):
    return jnp.where(place == 0, jnp.stack([own, other]), jnp.stack([other, own]))


def relative(x):
    far = swap(x, "zh")
    return [x, swap(x, "core"), far, swap(far, "core")]


def exchange(x, axes):
    return lax.all_to_all(x, axes, split_axis=0, concat_axis=0, tiled=True)


def after(xs, *others):
    return lax.optimization_barrier((xs,) + others)[0]


def local(
    tokens,
    cotangent,
    doc_ids,
    wq,
    wk,
    wv,
    wo,
    q_gain,
    k_gain,
    attn_gain,
    w_gate,
    w_up,
    w_down,
    mlp_gain,
):
    c = lax.axis_index(CTX)
    f = lax.axis_index(FSDP)
    place = f[None].astype(jnp.int32)
    inputs = tokens.reshape(ROWS, 1024)

    core = lax.axis_index("core")
    wkv = jnp.concatenate([wk, wv], axis=1)
    own, near, quarter = deal(jnp.stack([f, lax.axis_index("x")]).astype(jnp.int32), wq, wkv)
    near = swap(near, "core")
    quarter = swap(quarter, "zh")
    quarter = jnp.stack([quarter[0], swap(quarter[1], "core")])
    quarter = exchange(jnp.broadcast_to(quarter[None], (4, 2, 64, 1024)), ("x",))

    spot = lax.axis_index("y") * 4 + lax.axis_index("x")
    pack = pack_group(
        spot[None].astype(jnp.int32),
        inputs,
        doc_ids,
        (q_gain[None], k_gain[None], jnp.stack([attn_gain, mlp_gain])),
        (w_gate, w_up, w_down),
    )
    group = lax.all_gather(pack, FSDP, axis=0, tiled=True).reshape(4, 288, 1024)
    gains = group[:, ROWS].astype(F32)
    gains_qk = jnp.stack([gains[:, :32].reshape(HEAD), gains[:, 128:160].reshape(HEAD)])
    gains_am = jnp.stack([gains[:, 512:768].reshape(1024), gains[:, 768:].reshape(1024)])
    starts_f = (gains[:, 256:261] * 64.0 + gains[:, 384:389]).astype(jnp.int32)
    far = lax.dynamic_slice(group, (f ^ 2, ROWS + 16, 0), (1, 144, 1024))[0]
    far = lax.all_gather(far, PLANE, axis=0, tiled=True)

    step = jnp.arange(BLOCK, dtype=jnp.int32)
    spot = jnp.concatenate([c * BLOCK + step, (2 * NCTX - 1 - c) * BLOCK + step])
    start = jnp.max(
        jnp.where(starts_f[:, :, None] <= spot[None, None, :], starts_f[:, :, None], 0), axis=1
    )
    position = spot[None, :] - start
    half = jnp.arange(HEAD, dtype=jnp.int32) % (HEAD // 2)
    frequency = jnp.exp(half.astype(F32) * (-2.0 * math.log(THETA) / HEAD))
    angles = position.astype(F32)[:, :, None] * frequency
    sign = jnp.where(jnp.arange(HEAD) < HEAD // 2, -1.0, 1.0).astype(F32)
    cos, sin = jnp.cos(angles), jnp.sin(angles) * sign

    send, qk, tokens_f, w_qkv = project(place, group, own, near, quarter, cos, sin, gains_qk)
    recv = exchange(send, CTX)
    near = (swap(w_gate, "core"), swap(w_up, "core"), swap(w_down, "core"))
    pairs = wo.reshape(2, 2, HEAD, 1024)
    heads = lax.dynamic_index_in_dim(pairs, core, 1, keepdims=False)
    others = swap(lax.dynamic_index_in_dim(pairs, 1 - core, 1, keepdims=False), "core")
    wo = in_order(core, heads, others).reshape(512, 1024)
    recv, near, wo = lax.optimization_barrier((recv, near, wo))
    other = swap(recv, "core")
    my_starts = lax.dynamic_index_in_dim(starts_f, c // 8, 0, keepdims=False)
    meta = [(c % 2)[None].astype(jnp.int32), my_starts, core[None].astype(jnp.int32)]
    meta = jnp.concatenate(meta + [jnp.zeros((1,), jnp.int32)])
    mixed_t, ot, lsum = attend(meta, recv, other)
    far = after(far, mixed_t)
    mixed_t = exchange(after(mixed_t, far), CTX)
    relayed = swap(far, "core")
    mixed_t, relayed = lax.optimization_barrier((mixed_t, relayed))
    feed_weights = (
        w_gate,
        w_up,
        w_down,
        *near,
        far,
        relayed,
    )
    mixed, keep, give = merge(place, mixed_t, wo)
    got = swap(give, "core")
    last = swap((keep[1] + got[1].astype(F32)).astype(BF), "zh")
    branch = keep[0] + got[0].astype(F32) + last.astype(F32)
    hidden = branch * rms(branch) * gains_am[0] + inputs.astype(F32)
    hidden = hidden.astype(BF)
    hidden_f = lax.all_gather(hidden, COLUMN, axis=0, tiled=True)
    result, d_hidden, d_branch, d_mlp, parts, d_gains_am = feed(
        place, branch, hidden, inputs, cotangent.reshape(ROWS, 1024), gains_am, feed_weights
    )
    d_mlp = lax.all_gather(d_mlp, COLUMN, axis=0, tiled=True)
    d_branches = relative(d_branch)
    drecv = exchange(split(place, d_branches, wo), CTX)

    parts = exchange(after(parts, drecv), COLUMN).reshape(1024, 1152)
    dq, keep, give = attend_back(meta, recv, other, after(drecv, hidden_f), ot, lsum)
    keep = (keep.astype(F32) + swap(give, "core").astype(F32)).astype(BF)
    back = jnp.concatenate([dq, keep], axis=1)
    parts = after(parts, back)
    back = exchange(after(back, parts), CTX)
    g_feed = feed_grads(parts, hidden_f, d_mlp, mixed, d_branches, d_gains_am.reshape(16, HEAD))
    g_feed = exchange(after(g_feed, back), CTX)

    d_qkv, g_qkv, d_gains_qk = project_back(place, back, qk, cos, sin, gains_qk, tokens_f)

    partial = dot_nt(d_qkv, w_qkv).reshape(4, ROWS, 1024)
    got = swap(jnp.stack([partial[1], partial[3]]).astype(BF), "core").astype(F32)
    last = swap((partial[2] + got[1]).astype(BF), "zh").astype(F32)
    d_inputs = d_hidden + partial[0] + got[0] + last

    g_feed, g_qkv, d_inputs = lax.optimization_barrier((g_feed, g_qkv, d_inputs))
    g_feed = g_feed.reshape(16, 2, 27, 16, HEAD)
    g_out = jnp.sum(g_feed[:, :, 18:].astype(F32), axis=(0, 1))
    d_gains_am = g_out[8]
    g_out = g_out[:8].astype(BF).reshape(2, 4, 16, HEAD)
    others = swap(lax.dynamic_index_in_dim(g_out, 1 - core, 0, keepdims=False), "core")
    g_out = lax.dynamic_index_in_dim(g_out, core, 0, keepdims=False)
    g_out = in_order(core, g_out, others).reshape(8, 16, HEAD)
    g_feed = jnp.sum(g_feed[:, :, :18].astype(F32), axis=0).astype(BF)
    g_gu = g_feed[:, :12].reshape(2, 4, 3, 16, HEAD).swapaxes(0, 1)
    g_gu = jnp.broadcast_to(g_gu[None], (2, 4, 2, 3, 16, HEAD)).reshape(8, 96, HEAD)
    g_gu = exchange(g_gu, COLUMN).reshape(2, 384, HEAD)
    g_feed = jnp.concatenate([g_feed[:, 12:].reshape(12, 16, HEAD), g_out], axis=0)
    g_feed = g_feed.reshape(320, HEAD)
    g_feed = in_order(lax.axis_index("zl"), g_feed, swap(g_feed, "zl"))
    g_feed = jnp.concatenate([g_gu, g_feed], axis=1)
    g_qkv = after(g_qkv, g_feed)
    g_feed = lax.all_gather(g_feed, PLANE, axis=0, tiled=True).reshape(NCTX, 44, 16, HEAD)

    g_qkv = exchange(g_qkv, AXES)
    gains = jnp.concatenate([d_gains_am, d_gains_qk, jnp.zeros((14, HEAD), F32)], axis=0)
    gains = gains + swap(gains.astype(BF), "core").astype(F32)
    gains = gains + swap(gains.astype(BF), "zh").astype(F32)

    g_qkv, gains = lax.optimization_barrier((g_qkv, gains))
    g_qkv = jnp.sum(g_qkv.reshape(NCTX, 4, 16, 512).astype(F32), axis=0)
    g_qkv = g_qkv.swapaxes(0, 1).reshape(16, 2048)
    g_qkv = jnp.concatenate([g_qkv, gains[16:]], axis=1).astype(BF)
    g_qkv = exchange(jnp.broadcast_to(g_qkv[None], (NCTX, 16, 2176)), CTX)
    gate_grad, up_grad, down_grad, out_grad = feed_finish(g_feed)
    g_qkv = after(g_qkv, gate_grad)
    gains_qk = jnp.sum(g_qkv[:, :2, 2048:].astype(F32), axis=0)
    gains_am = lax.dynamic_index_in_dim(gains[:16].reshape(2, 4, 256), f, 1, keepdims=False)

    g_q, g_k, g_v = project_finish(g_qkv)
    gains_qk = lax.dynamic_slice_in_dim(gains_qk, f * 32, 32, 1)
    return (
        result.reshape(tokens.shape),
        d_inputs.reshape(tokens.shape),
        g_q,
        g_k,
        g_v,
        out_grad,
        gains_qk[0],
        gains_qk[1],
        gains_am[0],
        gate_grad,
        up_grad,
        down_grad,
        gains_am[1],
    )


def solution(mesh):
    whole = Mesh(mesh.devices.reshape(4, 4, 2, 2, 2), AXES)
    blocks = P(FSDP, None, CTX, None, None)
    rows = P(FSDP, None)
    vector = P(FSDP)
    return jax.shard_map(
        local,
        mesh=whole,
        in_specs=(
            blocks,
            blocks,
            rows,
            rows,
            rows,
            rows,
            rows,
            vector,
            vector,
            vector,
            rows,
            rows,
            rows,
            vector,
        ),
        out_specs=(
            blocks,
            blocks,
            rows,
            rows,
            rows,
            rows,
            vector,
            vector,
            vector,
            rows,
            rows,
            rows,
            vector,
        ),
        check_vma=False,
    )
```

```python
import math

import jax
import jax.numpy as jnp
from jax import lax
from jax.experimental import pallas as pl
from jax.experimental.pallas import tpu as pltpu
from jax.sharding import Mesh, PartitionSpec as P

HEADS = 16
KV_HEADS = 8
HEAD = 128
EPS = 1e-06
THETA = 500000.0

AXES = ("y", "x", "zl", "zh", "core")
CTX = ("y", "x", "zl")
PLANE = ("y", "x")
FSDP = ("zh", "core")
COLUMN = ("zl", "zh", "core")
NCTX = 32
SEQS = 4
BLOCK = 64
ROWS = 2 * BLOCK
LEN = 4096
DOCS = 5
PART = 32
TILES = 8
QT = 256
KT = 512
CHUNK = 192
BF = jnp.bfloat16
F32 = jnp.float32
SCALE = HEAD**-0.5
LOG2E = math.log2(math.e)


def key_block(j):
    return (j, 0) if j < NCTX else (2 * NCTX - 1 - j, 1)


def tile_bounds(meta, t):
    first, last = t * KT, t * KT + KT - 1
    low = jnp.int32(0)
    high = jnp.int32(0)
    for d in range(1, DOCS):
        start = meta[1 + d]
        low = jnp.where(start <= first, start, low)
        high = jnp.where(start <= last, start, high)
    return lax.div(low, KT), jnp.minimum(lax.div(high + (KT - 1), KT), t)


def row_places(meta, t):
    lane = lax.broadcasted_iota(jnp.int32, (1, QT), 1)
    place = t * KT + lax.div(lane, PART) * BLOCK + meta[0] * PART + lax.rem(lane, PART)
    start = jnp.zeros((1, QT), jnp.int32)
    for d in range(1, DOCS):
        start = jnp.where(place >= meta[1 + d], meta[1 + d], start)
    return place, start


def allowed(kt, place, start):
    key = kt * KT + lax.broadcasted_iota(jnp.int32, (KT, QT), 0)
    return (key <= place) & (key >= start)


def gather_rows(src, t):
    parts = []
    for i in range(8):
        c, b = key_block(8 * t + i)
        parts.append(src[c, pl.ds(b * PART, PART), :])
    return jnp.concatenate(parts, axis=0)


def sort_keys(src, dst):
    for j in range(2 * NCTX):
        c, b = key_block(j)
        dst[pl.ds(j * BLOCK, BLOCK), :] = src[c, pl.ds(64 + b * BLOCK, BLOCK), :]


def sort_both(meta, mine, other, ks, vs):
    @pl.when(meta[6] == 0)
    def _():
        sort_keys(mine, ks)
        sort_keys(other, vs)

    @pl.when(meta[6] != 0)
    def _():
        sort_keys(other, ks)
        sort_keys(mine, vs)


def put_rows(out, t, rows):
    for i in range(8):
        j = 8 * t + i
        half = (j >= NCTX).astype(jnp.int32)
        c = jnp.where(half == 0, j, 2 * NCTX - 1 - j)
        out[c, pl.ds(pl.multiple_of(half * PART, PART), PART), :] = rows[i * PART : (i + 1) * PART]


def transposed(x):
    return x.astype(F32).T.astype(x.dtype)


def forward_kernel(meta, mine, other, out, ot, lsum, ks, vs, vt, qt):
    sort_both(meta, mine, other, ks, vs)
    for i in range(TILES):
        vt[i] = transposed(vs[pl.ds(i * KT, KT), :])
        qt[i] = transposed(gather_rows(mine, i))

    def query_tile(t, _):
        q = qt[t]
        place, start = row_places(meta, t)
        low, clear = tile_bounds(meta, t)

        def step(kt, carry, masked):
            total, mixed = carry
            k = ks[pl.ds(pl.multiple_of(kt * KT, KT), KT), :]
            s = jnp.dot(k, q, preferred_element_type=F32)
            p = jnp.exp2(s * (SCALE * LOG2E))
            if masked:
                p = jnp.where(allowed(kt, place, start), p, 0.0)
            total = total + jnp.sum(p, axis=0, keepdims=True)
            mixed = mixed + jnp.dot(vt[kt], p.astype(BF), preferred_element_type=F32)
            return total, mixed

        carry = (jnp.zeros((1, QT), F32), jnp.zeros((HEAD, QT), F32))
        carry = lax.fori_loop(low, clear, lambda kt, cr: step(kt, cr, True), carry)
        begin = jnp.maximum(low, clear)
        pairs = lax.div(t - begin, 2)

        def double(i, cr):
            cr = step(begin + 2 * i, cr, False)
            return step(begin + 2 * i + 1, cr, False)

        carry = lax.fori_loop(0, pairs, double, carry)
        carry = lax.fori_loop(begin + 2 * pairs, t, lambda kt, cr: step(kt, cr, False), carry)
        total, mixed = carry
        for half in range(2):
            lanes = QT // 2 * half
            first = t * KT + KT // 2 * half
            k = ks[pl.ds(pl.multiple_of(first, KT // 2), KT // 2), :]
            s = jnp.dot(k, q[:, lanes:], preferred_element_type=F32)
            key = first + lax.broadcasted_iota(jnp.int32, (KT // 2, QT - lanes), 0)
            seen = (key <= place[:, lanes:]) & (key >= start[:, lanes:])
            p = jnp.where(seen, jnp.exp2(s * (SCALE * LOG2E)), 0.0)
            values = vt[t][:, KT // 2 * half : KT // 2 * (half + 1)]
            sums = jnp.sum(p, axis=0, keepdims=True)
            adds = jnp.dot(values, p.astype(BF), preferred_element_type=F32)
            if half:
                sums = jnp.concatenate([jnp.zeros((1, lanes), F32), sums], axis=1)
                adds = jnp.concatenate([jnp.zeros((HEAD, lanes), F32), adds], axis=1)
            total = total + sums
            mixed = mixed + adds
        mixed = mixed * (1.0 / total)
        ot[t] = mixed
        lsum[t] = total
        rows = mixed.T.astype(BF)
        put_rows(out, t, rows)
        return 0

    lax.fori_loop(0, TILES, query_tile, 0)


def backward_kernel(
    meta, mine, other, drecv, ot, lsum, out, keep, give, ks, vs, kt_, q_, qt, do_, dot_, dk, dv
):
    sort_both(meta, mine, other, ks, vs)
    for i in range(TILES):
        kt_[i] = transposed(ks[pl.ds(i * KT, KT), :])
        rows = gather_rows(mine, i)
        q_[i] = rows
        qt[i] = transposed(rows)
        rows = gather_rows(drecv, i)
        do_[i] = rows
        dot_[i] = transposed(rows)
    dk[...] = jnp.zeros_like(dk)
    dv[...] = jnp.zeros_like(dv)

    def query_tile(t, _):
        q, q_t, d, d_t = q_[t], qt[t], do_[t], dot_[t]
        place, start = row_places(meta, t)
        low, clear = tile_bounds(meta, t)
        delta = jnp.sum(d_t.astype(F32) * ot[t], axis=0, keepdims=True)
        shift = jnp.log2(lsum[t])

        def step(kt, total, masked):
            at = pl.ds(pl.multiple_of(kt * KT, KT), KT)
            s = jnp.dot(ks[at, :], q_t, preferred_element_type=F32)
            p = jnp.exp2(s * (SCALE * LOG2E) - shift)
            if masked:
                p = jnp.where(allowed(kt, place, start), p, 0.0)
            dv[at, :] += jnp.dot(p.astype(BF), d, preferred_element_type=F32)
            dp = jnp.dot(vs[at, :], d_t, preferred_element_type=F32)
            ds = (p * (dp - delta)).astype(BF)
            dk[at, :] += jnp.dot(ds, q, preferred_element_type=F32)
            return total + jnp.dot(kt_[kt], ds, preferred_element_type=F32)

        total = jnp.zeros((HEAD, QT), F32)
        total = lax.fori_loop(low, clear, lambda kt, cr: step(kt, cr, True), total)
        total = lax.fori_loop(jnp.maximum(low, clear), t, lambda kt, cr: step(kt, cr, False), total)
        total = step(t, total, True)
        rows = (total * SCALE).T.astype(BF)
        put_rows(out, t, rows)
        return 0

    lax.fori_loop(0, TILES, query_tile, 0)

    def unsort(src, scale, dst):
        for j in range(2 * NCTX):
            c, b = key_block(j)
            dst[c, pl.ds(b * BLOCK, BLOCK), :] = (src[pl.ds(j * BLOCK, BLOCK), :] * scale).astype(BF)

    @pl.when(meta[6] == 0)
    def _():
        unsort(dk, SCALE, keep)
        unsort(dv, 1.0, give)

    @pl.when(meta[6] != 0)
    def _():
        unsort(dv, 1.0, keep)
        unsort(dk, SCALE, give)


VMEM = pl.BlockSpec(memory_space=pltpu.VMEM)
SMEM = pl.BlockSpec(memory_space=pltpu.SMEM)
ANY = pl.BlockSpec(memory_space=pl.ANY)
PARAMS = pltpu.CompilerParams(vmem_limit_bytes=48 * 1024 * 1024)
LARGE = pltpu.CompilerParams(vmem_limit_bytes=60 * 1024 * 1024)


def attend(meta, mine, other):
    return pl.pallas_call(
        forward_kernel,
        out_shape=(
            jax.ShapeDtypeStruct((NCTX, 64, HEAD), BF),
            jax.ShapeDtypeStruct((TILES, HEAD, QT), F32),
            jax.ShapeDtypeStruct((TILES, 1, QT), F32),
        ),
        in_specs=[SMEM, VMEM, VMEM],
        out_specs=(VMEM, VMEM, VMEM),
        scratch_shapes=[
            pltpu.VMEM((LEN, HEAD), BF),
            pltpu.VMEM((LEN, HEAD), BF),
            pltpu.VMEM((TILES, HEAD, KT), BF),
            pltpu.VMEM((TILES, HEAD, QT), BF),
        ],
        compiler_params=PARAMS,
        cost_estimate=pl.CostEstimate(
            flops=15_000_000_000, bytes_accessed=5_000_000, transcendentals=4_700_000
        ),
        name="attention_forward",
    )(meta, mine, other)


def attend_back(meta, mine, other, drecv, ot, lsum):
    return pl.pallas_call(
        backward_kernel,
        out_shape=(
            jax.ShapeDtypeStruct((NCTX, 64, HEAD), BF),
            jax.ShapeDtypeStruct((NCTX, ROWS, HEAD), BF),
            jax.ShapeDtypeStruct((NCTX, ROWS, HEAD), BF),
        ),
        in_specs=[SMEM] + [VMEM] * 5,
        out_specs=(VMEM,) * 3,
        scratch_shapes=[
            pltpu.VMEM((LEN, HEAD), BF),
            pltpu.VMEM((LEN, HEAD), BF),
            pltpu.VMEM((TILES, HEAD, KT), BF),
            pltpu.VMEM((TILES, QT, HEAD), BF),
            pltpu.VMEM((TILES, HEAD, QT), BF),
            pltpu.VMEM((TILES, QT, HEAD), BF),
            pltpu.VMEM((TILES, HEAD, QT), BF),
            pltpu.VMEM((LEN, HEAD), F32),
            pltpu.VMEM((LEN, HEAD), F32),
        ],
        compiler_params=PARAMS,
        cost_estimate=pl.CostEstimate(
            flops=10_000_000, bytes_accessed=10_000, transcendentals=0
        ),
        name="attention_backward",
    )(meta, mine, other, drecv, ot, lsum)


def rms(u):
    return lax.rsqrt(jnp.mean(u * u, axis=-1, keepdims=True) + EPS)


def dot(a, b):
    return jnp.dot(a, b, preferred_element_type=F32)


def dot_nt(a, b):
    return lax.dot_general(a, b, (((1,), (1,)), ((), ())), preferred_element_type=F32)


def dot_tn(a, b):
    return lax.dot_general(a, b, (((0,), (0,)), ((), ())), preferred_element_type=F32)


def pack_kernel(at, x, docs, q_gain, k_gain, am_gain, gate, up, down, out, row, sem):
    copies = []
    for n in range(3):
        for src, row_at, lane_at, width in (
            (gate, 0, 1024 * n, 1024),
            (up, 0, 1024 * n, 1024),
            (down, 256 * n, 0, 1024),
        ):
            k = len(copies)
            first = pl.multiple_of(row_at + at[0] * 16, 16)
            copies.append(
                pltpu.make_async_copy(
                    src.at[pl.ds(first, 16), pl.ds(lane_at, width)],
                    out.at[pl.ds(144 + 16 * (3 * (k % 3) + n), 16), :],
                    sem.at[k],
                )
            )
            copies[-1].start()
    out[pl.ds(0, ROWS), :] = x[...]
    row[...] = jnp.zeros_like(row)
    row[:, pl.ds(0, 32)] = q_gain[...].astype(F32)
    row[:, pl.ds(128, 32)] = k_gain[...].astype(F32)
    lane = lax.broadcasted_iota(jnp.int32, (1, HEAD), 1)
    high = jnp.zeros((1, HEAD), F32)
    low = jnp.zeros((1, HEAD), F32)
    for d in range(1, DOCS):
        start = jnp.sum((docs[...] < d).astype(F32), axis=1, keepdims=True)
        whole = jnp.floor(start * (1.0 / 64.0))
        high = jnp.where(lane == d, whole, high)
        low = jnp.where(lane == d, start - whole * 64.0, low)
    row[:, pl.ds(256, HEAD)] = high
    row[:, pl.ds(384, HEAD)] = low
    row[:, pl.ds(512, 256)] = am_gain[pl.ds(0, 1), :].astype(F32)
    row[:, pl.ds(768, 256)] = am_gain[pl.ds(1, 1), :].astype(F32)
    out[pl.ds(ROWS, 16), :] = jnp.broadcast_to(row[...], (16, 1024)).astype(BF)
    for copy in copies:
        copy.wait()


def pack_group(at, x, docs, gains, weights):
    return pl.pallas_call(
        pack_kernel,
        out_shape=jax.ShapeDtypeStruct((288, 1024), BF),
        in_specs=[SMEM] + [VMEM] * 5 + [ANY] * 3,
        out_specs=VMEM,
        scratch_shapes=[pltpu.VMEM((1, 1024), F32), pltpu.SemaphoreType.DMA((9,))],
        compiler_params=LARGE,
        name="pack_group",
    )(at, x, docs, *gains, *weights)


def deal_kernel(place, wq, wkv, own, near, far, sem):
    copies = []

    def columns(f, dst, rows):
        zh, core = lax.div(f, 2), lax.rem(f, 2)
        slices = [(wq, (8 * zh + 2 * n + core) * HEAD, HEAD, n * HEAD) for n in range(4)]
        for src, lane, width, at in slices + [(wkv, 1024 * core + 512 * zh, 512, 512)]:
            lanes = pl.ds(pl.multiple_of(lane, HEAD), width)
            copies.append(
                pltpu.make_async_copy(
                    src.at[rows, lanes], dst.at[:, pl.ds(at, width)], sem.at[len(copies)]
                )
            )
            copies[-1].start()

    quarter = pl.ds(pl.multiple_of(place[1] * 64, 64), 64)
    columns(place[0] ^ 2, far.at[0], quarter)
    columns(place[0] ^ 3, far.at[1], quarter)
    columns(place[0] ^ 1, near, pl.ds(0, 256))
    columns(place[0], own, pl.ds(0, 256))
    for copy in copies:
        copy.wait()


def deal(place, wq, wkv):
    return pl.pallas_call(
        deal_kernel,
        out_shape=(
            jax.ShapeDtypeStruct((256, 1024), BF),
            jax.ShapeDtypeStruct((256, 1024), BF),
            jax.ShapeDtypeStruct((2, 64, 1024), BF),
        ),
        in_specs=[SMEM] + [ANY] * 2,
        out_specs=(VMEM,) * 3,
        scratch_shapes=[pltpu.SemaphoreType.DMA((20,))],
        compiler_params=LARGE,
        name="deal",
    )(place, wq, wkv)


def project_kernel(place, group, own, near, far, cos, sin, gains, send, qk, tokens, w):
    w[pl.ds(pl.multiple_of(place[0] * 256, 256), 256), :] = own[...]
    w[pl.ds(pl.multiple_of((place[0] ^ 1) * 256, 256), 256), :] = near[...]
    for i in range(4):
        for k in range(2):
            at = pl.multiple_of((place[0] ^ (2 + k)) * 256 + 64 * i, 64)
            w[pl.ds(at, 64), :] = far[i, k]
    for j in range(4):
        n = place[0] ^ j
        base = n * 8
        rows = pl.ds(j * ROWS, ROWS)
        x = group[n, pl.ds(0, ROWS), :]
        tokens[rows, :] = x
        y = dot(x, w[...])
        c, s = cos[n], sin[n]
        qk[rows, :] = y
        core = lax.rem(place[0], 2)
        for h in range(8):
            v = y[:, h * HEAD : (h + 1) * HEAD]
            u = v * rms(v) * gains[pl.ds(h // 4, 1), :]
            u = u * c + pltpu.roll(u, HEAD // 2, 1) * s
            if h < 4:
                u = u.astype(BF)
                for half in range(2):
                    for b in range(2):
                        at = b * 64 + half * PART
                        send[base + h * 2 + half, pl.ds(b * PART, PART), :] = u[at : at + PART]
            else:
                u = jnp.where(core == 0, u, v).astype(BF)
                for half in range(2):
                    send[base + (h - 4) * 2 + half, pl.ds(64, ROWS), :] = u


def project(place, group, own, near, far, cos, sin, gains):
    return pl.pallas_call(
        project_kernel,
        out_shape=(
            jax.ShapeDtypeStruct((NCTX, CHUNK, HEAD), BF),
            jax.ShapeDtypeStruct((512, 1024), F32),
            jax.ShapeDtypeStruct((512, 1024), BF),
            jax.ShapeDtypeStruct((1024, 1024), BF),
        ),
        in_specs=[SMEM] + [VMEM] * 7,
        out_specs=(VMEM,) * 4,
        compiler_params=PARAMS,
        cost_estimate=pl.CostEstimate(
            flops=60_000_000_000, bytes_accessed=9_000_000, transcendentals=4000
        ),
        name="project",
    )(place, group, own, near, far, cos, sin, gains)


def project_back_kernel(place, back, qk, cos, sin, gains, tokens, out, send, dgains, grads):
    totals = [jnp.zeros((1, HEAD), F32), jnp.zeros((1, HEAD), F32)]
    for j in range(4):
        n = place[0] ^ j
        base = n * 8
        rows = pl.ds(j * ROWS, ROWS)
        c, s = cos[n], sin[n]
        core = lax.rem(place[0], 2)
        for h in range(8):
            at = base + h % 4 * 2
            if h < 4:
                parts = []
                for b in range(2):
                    for half in range(2):
                        parts.append(back[at + half, pl.ds(b * PART, PART), :])
                raw = jnp.concatenate(parts, axis=0).astype(F32)
            else:
                raw = back[at, pl.ds(64, ROWS), :].astype(F32)
                raw = raw + back[at + 1, pl.ds(64, ROWS), :].astype(F32)
            e = raw * c - pltpu.roll(raw, HEAD // 2, 1) * s
            u = qk[rows, pl.ds(h * HEAD, HEAD)]
            inverse = rms(u)
            u = u * inverse
            total = jnp.sum(e * u, axis=0, keepdims=True)
            if h >= 4:
                total = jnp.where(core == 0, total, 0.0)
            totals[h // 4] = totals[h // 4] + total
            e = e * gains[pl.ds(h // 4, 1), :]
            e = inverse * (e - u * jnp.mean(e * u, axis=-1, keepdims=True))
            if h >= 4:
                e = jnp.where(core == 0, e, raw)
            out[rows, pl.ds(h * HEAD, HEAD)] = e.astype(BF)
    grads[...] = dot_tn(tokens[...], out[...])
    for f in range(4):
        for p in range(16):
            for half in range(2):
                send[(p * 2 + half) * 4 + f] = grads[
                    pl.ds(256 * f + 16 * p, 16), pl.ds(512 * half, 512)
                ].astype(BF)
    dgains[...] = jnp.concatenate(totals, axis=0)


def project_back(place, back, qk, cos, sin, gains, tokens):
    return pl.pallas_call(
        project_back_kernel,
        out_shape=(
            jax.ShapeDtypeStruct((512, 1024), BF),
            jax.ShapeDtypeStruct((128, 16, 512), BF),
            jax.ShapeDtypeStruct((2, HEAD), F32),
        ),
        in_specs=[SMEM] + [VMEM] * 6,
        out_specs=(VMEM,) * 3,
        scratch_shapes=[pltpu.VMEM((1024, 1024), F32)],
        compiler_params=PARAMS,
        cost_estimate=pl.CostEstimate(
            flops=60_000_000_000, bytes_accessed=9_000_000, transcendentals=4000
        ),
        name="project_back",
    )(place, back, qk, cos, sin, gains, tokens)


def feed_grads_kernel(pa, norms, mixed, d0, d1, d2, d3, dgains, send, db, gu, down, out):
    for j, d in enumerate((d0, d1, d2, d3)):
        db[pl.ds(j * ROWS, ROWS), :] = d[...]
    out[...] = dot_tn(mixed[...], db[...])
    gu[...] = dot_tn(norms[:, pl.ds(0, 1024)], pa[:, pl.ds(384, 768)])
    down[...] = dot_tn(pa[:, pl.ds(0, 384)], norms[:, pl.ds(1024, 1024)])
    for to in range(NCTX):
        p, half = to // 2, to % 2

        def put(tile, ref, row, column):
            send[to, pl.ds(16 * tile, 16), :] = ref[pl.ds(row, 16), pl.ds(column, 128)].astype(BF)

        for f in range(4):
            for k in range(3):
                put(f * 3 + k, gu, 256 * f + 16 * p, 384 * half + 128 * k)
        for k in range(3):
            for i in range(2):
                put(12 + 2 * k + i, down, to // 4 * 48 + 16 * k, to % 4 * 256 + 128 * i)
        for b in range(2):
            for k in range(4):
                put(18 + 4 * b + k, out, 256 * b + 16 * p, 512 * half + 128 * k)
        put(26, dgains, 0, 0)


def feed_grads(parts, norms, mixed, d_branches, dgains):
    return pl.pallas_call(
        feed_grads_kernel,
        out_shape=jax.ShapeDtypeStruct((NCTX, 432, HEAD), BF),
        in_specs=[VMEM] * 8,
        out_specs=VMEM,
        scratch_shapes=[
            pltpu.VMEM((512, 1024), BF),
            pltpu.VMEM((1024, 768), F32),
            pltpu.VMEM((384, 1024), F32),
            pltpu.VMEM((512, 1024), F32),
        ],
        compiler_params=PARAMS,
        cost_estimate=pl.CostEstimate(
            flops=2_900_000_000, bytes_accessed=12_000_000, transcendentals=0
        ),
        name="feed_grads",
    )(parts, norms, mixed, *d_branches, dgains)


def feed_finish_kernel(tiles, gate, up, down, out):
    for c in range(NCTX):
        p, half = c // 2, c % 2
        for n in range(24):
            (up if half else gate)[pl.ds(16 * p, 16), pl.ds(128 * n, 128)] = tiles[c, n].astype(F32)
        for zl in range(2):
            for k in range(3):
                for i in range(2):
                    row = 384 * zl + c // 4 * 48 + 16 * k
                    down[pl.ds(row, 16), pl.ds(c % 4 * 256 + 128 * i, 128)] = tiles[
                        c, 24 + zl * 6 + 2 * k + i
                    ].astype(F32)
        for core in range(2):
            for k in range(4):
                row = 128 * (2 * (p // 8) + core) + 16 * (p % 8)
                out[pl.ds(row, 16), pl.ds(512 * half + 128 * k, 128)] = tiles[
                    c, 36 + 4 * core + k
                ].astype(F32)


def feed_finish(tiles):
    return pl.pallas_call(
        feed_finish_kernel,
        out_shape=(
            jax.ShapeDtypeStruct((256, 3072), F32),
            jax.ShapeDtypeStruct((256, 3072), F32),
            jax.ShapeDtypeStruct((768, 1024), F32),
            jax.ShapeDtypeStruct((512, 1024), F32),
        ),
        in_specs=[VMEM],
        out_specs=(VMEM,) * 4,
        compiler_params=PARAMS,
        cost_estimate=pl.CostEstimate(flops=0, bytes_accessed=18_000_000, transcendentals=0),
        name="feed_finish",
    )(tiles)


def project_finish_kernel(parts, gq, gk, gv):
    for p in range(16):
        rows = pl.ds(16 * p, 16)
        for f in range(4):
            zh, core = f // 2, f % 2
            for n in range(4):
                gq[rows, pl.ds((8 * zh + 2 * n + core) * HEAD, HEAD)] = parts[
                    2 * p, :, pl.ds(512 * f + HEAD * n, HEAD)
                ].astype(F32)
            (gv if core else gk)[rows, pl.ds(512 * zh, 512)] = parts[
                2 * p + 1, :, pl.ds(512 * f, 512)
            ].astype(F32)


def project_finish(parts):
    return pl.pallas_call(
        project_finish_kernel,
        out_shape=(
            jax.ShapeDtypeStruct((256, 2048), F32),
            jax.ShapeDtypeStruct((256, 1024), F32),
            jax.ShapeDtypeStruct((256, 1024), F32),
        ),
        in_specs=[VMEM],
        out_specs=(VMEM,) * 3,
        compiler_params=PARAMS,
        cost_estimate=pl.CostEstimate(flops=0, bytes_accessed=6_000_000, transcendentals=0),
        name="project_finish",
    )(parts)


def merge_kernel(place, recv, wo, mixed, keep, give):
    for j in range(4):
        base = (place[0] ^ j) * 8
        for h in range(4):
            parts = []
            for b in range(2):
                for half in range(2):
                    parts.append(recv[base + h * 2 + half, pl.ds(b * PART, PART), :])
            mixed[pl.ds(j * ROWS, ROWS), pl.ds(h * HEAD, HEAD)] = jnp.concatenate(parts, axis=0)
    for j in (1, 3, 0, 2):
        y = dot(mixed[pl.ds(j * ROWS, ROWS), :], wo[...])
        if j % 2:
            give[j // 2] = y.astype(BF)
        else:
            keep[j // 2] = y


def merge(place, recv, wo):
    return pl.pallas_call(
        merge_kernel,
        out_shape=(
            jax.ShapeDtypeStruct((512, 512), BF),
            jax.ShapeDtypeStruct((2, ROWS, 1024), F32),
            jax.ShapeDtypeStruct((2, ROWS, 1024), BF),
        ),
        in_specs=[SMEM] + [VMEM] * 2,
        out_specs=(VMEM, VMEM, VMEM),
        compiler_params=PARAMS,
        cost_estimate=pl.CostEstimate(
            flops=540_000_000, bytes_accessed=4_000_000, transcendentals=0
        ),
        name="merge",
    )(place, recv, wo)


def split_kernel(place, d0, d1, d2, d3, wo, send):
    for j, d in enumerate((d0, d1, d2, d3)):
        base = (place[0] ^ j) * 8
        y = dot_nt(d[...], wo[...]).astype(BF)
        for h in range(4):
            for b in range(2):
                for half in range(2):
                    at = b * 64 + half * PART
                    send[base + h * 2 + half, pl.ds(b * PART, PART), :] = y[
                        at : at + PART, h * HEAD : (h + 1) * HEAD
                    ]


def split(place, ds, wo):
    return pl.pallas_call(
        split_kernel,
        out_shape=jax.ShapeDtypeStruct((NCTX, 64, HEAD), BF),
        in_specs=[SMEM] + [VMEM] * 5,
        out_specs=VMEM,
        compiler_params=PARAMS,
        cost_estimate=pl.CostEstimate(
            flops=10_000_000, bytes_accessed=10_000, transcendentals=0
        ),
        name="split",
    )(place, *ds, wo)


def feed_kernel(
    place,
    a,
    hidden,
    x,
    g,
    gains,
    gate0,
    up0,
    down0,
    gate1,
    up1,
    down1,
    cat2,
    cat3,
    result,
    d_hidden,
    d_branch,
    norms,
    eighths,
    dgains,
    w,
    sems,
    parts,
    hb,
    gate,
    up,
    dh,
):
    copies = []

    def fetch(src, dst):
        copy = pltpu.make_async_copy(src, dst, sems.at[len(copies)])
        copy.start()
        copies.append(copy)

    for j, (gate_src, up_src) in enumerate(((gate0, up0), (gate1, up1))):
        fetch(gate_src, w.at[j, :, :, pl.ds(0, 3072)])
        fetch(up_src, w.at[j, :, :, pl.ds(3072, 3072)])
    for n in range(6):
        for j, src in ((2, cat2), (3, cat3)):
            fetch(src.at[:, pl.ds(16 * n, 16), :], w.at[j, :, :, pl.ds(1024 * n, 1024)])
    first_needed = len(copies)
    for n in range(3):
        at = pl.ds(6144 + 1024 * n, 1024)
        for j, src in ((0, down0), (1, down1)):
            fetch(src.at[pl.ds(16 * n, 16), :, :], w.at[j, :, :, at])
        for j, src in ((2, cat2), (3, cat3)):
            fetch(src.at[:, pl.ds(96 + 16 * n, 16), :], w.at[j, :, :, at])

    def rows_of(j, at, width):
        return w[j, :, :, pl.ds(at, width)].reshape(256, width)

    me = place[0]
    gain_a, gain_m = gains[pl.ds(0, 1), :], gains[pl.ds(1, 1), :]
    inverse_a = rms(a[...])
    normed_a = a[...] * inverse_a
    h = x[...].astype(F32) + normed_a * gain_a
    for n in range(4):
        hb[n] = hidden[:, pl.ds(256 * n, 256)]
    norms[:, pl.ds(0, 1024)] = hidden[...]
    for copy in copies[:first_needed]:
        copy.wait()
    for n in range(4):
        at = 768 * n
        u = dot(hb[me], rows_of(0, at, 768))
        v = dot(hb[me], rows_of(0, 3072 + at, 768))
        for j in range(1, 4):
            u = u + dot(hb[me ^ j], rows_of(j, at, 768))
            v = v + dot(hb[me ^ j], rows_of(j, 3072 + at, 768))
        gate[n] = u
        up[n] = v
        parts[n, :, pl.ds(0, 768)] = (u / (1.0 + jnp.exp(-u)) * v).astype(BF)
    for copy in copies[first_needed:]:
        copy.wait()
    z = jnp.zeros((ROWS, 1024), F32)
    for j in range(4):
        for b in range(3):
            z = z + dot(
                parts[me ^ j, :, pl.ds(256 * b, 256)], rows_of(j, 6144 + 1024 * b, 1024)
            )
    inverse_z = rms(z)
    normed_z = z * inverse_z
    result[...] = (h + normed_z * gain_m).astype(BF)
    e = g[...].astype(F32)
    dgains[pl.ds(1, 1), :] = jnp.sum(e * normed_z, axis=0, keepdims=True)
    weighted = e * gain_m
    dz = inverse_z * (weighted - normed_z * jnp.mean(weighted * normed_z, axis=-1, keepdims=True))
    dz = dz.astype(BF)
    norms[:, pl.ds(1024, 1024)] = dz
    for j in range(4):
        n = me ^ j
        for b in range(3):
            at = pl.ds(256 * b, 256)
            d_act = dot_nt(dz, rows_of(j, 6144 + 1024 * b, 1024))
            u, v = gate[n, :, at], up[n, :, at]
            s = 1.0 / (1.0 + jnp.exp(-u))
            parts[n, :, pl.ds(768 + 256 * b, 256)] = (
                d_act * v * (s * (1.0 + u * (1.0 - s)))
            ).astype(BF)
            parts[n, :, pl.ds(1536 + 256 * b, 256)] = (d_act * (u * s)).astype(BF)
    for n in range(8):
        for k in range(3):
            eighths[n, :, pl.ds(384 * k, 384)] = parts[
                n % 4, :, pl.ds(768 * k + 384 * (n // 4), 384)
            ]
    for j in range(4):
        total = jnp.zeros((ROWS, 256), F32)
        for n in range(4):
            total = total + dot_nt(parts[n, :, pl.ds(768, 768)], rows_of(j, 768 * n, 768))
            total = total + dot_nt(
                parts[n, :, pl.ds(1536, 768)], rows_of(j, 3072 + 768 * n, 768)
            )
        dh[me ^ j] = total
    total = g[...].astype(F32) + jnp.concatenate([dh[n] for n in range(4)], axis=1)
    d_hidden[...] = total
    dgains[pl.ds(0, 1), :] = jnp.sum(total * normed_a, axis=0, keepdims=True)
    weighted = total * gain_a
    d_branch[...] = (
        inverse_a * (weighted - normed_a * jnp.mean(weighted * normed_a, axis=-1, keepdims=True))
    ).astype(BF)


def feed(place, a, hidden, x, g, gains, weights):
    return pl.pallas_call(
        feed_kernel,
        out_shape=(
            jax.ShapeDtypeStruct((ROWS, 1024), BF),
            jax.ShapeDtypeStruct((ROWS, 1024), F32),
            jax.ShapeDtypeStruct((ROWS, 1024), BF),
            jax.ShapeDtypeStruct((ROWS, 2048), BF),
            jax.ShapeDtypeStruct((8, ROWS, 1152), BF),
            jax.ShapeDtypeStruct((2, 1024), F32),
        ),
        in_specs=[SMEM] + [VMEM] * 5 + [ANY] * 8,
        out_specs=(VMEM,) * 6,
        scratch_shapes=[
            pltpu.VMEM((4, 16, 16, 9216), BF),
            pltpu.SemaphoreType.DMA((28,)),
            pltpu.VMEM((4, ROWS, 2304), BF),
            pltpu.VMEM((4, ROWS, 256), BF),
            pltpu.VMEM((4, ROWS, 768), F32),
            pltpu.VMEM((4, ROWS, 768), F32),
            pltpu.VMEM((4, ROWS, 256), F32),
        ],
        compiler_params=LARGE,
        cost_estimate=pl.CostEstimate(
            flops=10_000_000, bytes_accessed=10_000, transcendentals=0
        ),
        name="feed_forward",
    )(
        place,
        a,
        hidden,
        x,
        g,
        gains,
        *[v.reshape(-1, 16, v.shape[1]) for v in weights[:6]],
        *[v.reshape(16, -1, 1024) for v in weights[6:]],
    )


SWAP = [(0, 1), (1, 0)]


def swap(x, axis):
    return lax.ppermute(x, axis, SWAP)


def in_order(place, own, other):
    return jnp.where(place == 0, jnp.stack([own, other]), jnp.stack([other, own]))


def relative(x):
    far = swap(x, "zh")
    return [x, swap(x, "core"), far, swap(far, "core")]


def exchange(x, axes):
    return lax.all_to_all(x, axes, split_axis=0, concat_axis=0, tiled=True)


def after(xs, *others):
    return lax.optimization_barrier((xs,) + others)[0]


def local(
    tokens,
    cotangent,
    doc_ids,
    wq,
    wk,
    wv,
    wo,
    q_gain,
    k_gain,
    attn_gain,
    w_gate,
    w_up,
    w_down,
    mlp_gain,
):
    c = lax.axis_index(CTX)
    f = lax.axis_index(FSDP)
    place = f[None].astype(jnp.int32)
    inputs = tokens.reshape(ROWS, 1024)

    core = lax.axis_index("core")
    wkv = jnp.concatenate([wk, wv], axis=1)
    own, near, quarter = deal(jnp.stack([f, lax.axis_index("x")]).astype(jnp.int32), wq, wkv)
    near = swap(near, "core")
    quarter = swap(quarter, "zh")
    quarter = jnp.stack([quarter[0], swap(quarter[1], "core")])
    quarter = exchange(jnp.broadcast_to(quarter[None], (4, 2, 64, 1024)), ("x",))

    spot = lax.axis_index("y") * 4 + lax.axis_index("x")
    pack = pack_group(
        spot[None].astype(jnp.int32),
        inputs,
        doc_ids,
        (q_gain[None], k_gain[None], jnp.stack([attn_gain, mlp_gain])),
        (w_gate, w_up, w_down),
    )
    group = lax.all_gather(pack, FSDP, axis=0, tiled=True).reshape(4, 288, 1024)
    gains = group[:, ROWS].astype(F32)
    gains_qk = jnp.stack([gains[:, :32].reshape(HEAD), gains[:, 128:160].reshape(HEAD)])
    gains_am = jnp.stack([gains[:, 512:768].reshape(1024), gains[:, 768:].reshape(1024)])
    starts_f = (gains[:, 256:261] * 64.0 + gains[:, 384:389]).astype(jnp.int32)
    far = lax.dynamic_slice(group, (f ^ 2, ROWS + 16, 0), (1, 144, 1024))[0]
    far = lax.all_gather(far, PLANE, axis=0, tiled=True)

    step = jnp.arange(BLOCK, dtype=jnp.int32)
    spot = jnp.concatenate([c * BLOCK + step, (2 * NCTX - 1 - c) * BLOCK + step])
    start = jnp.max(
        jnp.where(starts_f[:, :, None] <= spot[None, None, :], starts_f[:, :, None], 0), axis=1
    )
    position = spot[None, :] - start
    half = jnp.arange(HEAD, dtype=jnp.int32) % (HEAD // 2)
    frequency = jnp.exp(half.astype(F32) * (-2.0 * math.log(THETA) / HEAD))
    angles = position.astype(F32)[:, :, None] * frequency
    sign = jnp.where(jnp.arange(HEAD) < HEAD // 2, -1.0, 1.0).astype(F32)
    cos, sin = jnp.cos(angles), jnp.sin(angles) * sign

    send, qk, tokens_f, w_qkv = project(place, group, own, near, quarter, cos, sin, gains_qk)
    recv = exchange(send, CTX)
    near = (swap(w_gate, "core"), swap(w_up, "core"), swap(w_down, "core"))
    pairs = wo.reshape(2, 2, HEAD, 1024)
    heads = lax.dynamic_index_in_dim(pairs, core, 1, keepdims=False)
    others = swap(lax.dynamic_index_in_dim(pairs, 1 - core, 1, keepdims=False), "core")
    wo = in_order(core, heads, others).reshape(512, 1024)
    recv, near, wo = lax.optimization_barrier((recv, near, wo))
    other = swap(recv, "core")
    my_starts = lax.dynamic_index_in_dim(starts_f, c // 8, 0, keepdims=False)
    meta = [(c % 2)[None].astype(jnp.int32), my_starts, core[None].astype(jnp.int32)]
    meta = jnp.concatenate(meta + [jnp.zeros((1,), jnp.int32)])
    mixed_t, ot, lsum = attend(meta, recv, other)
    far = after(far, mixed_t)
    mixed_t = exchange(mixed_t, CTX)
    feed_weights = (
        w_gate,
        w_up,
        w_down,
        *near,
        far,
        swap(far, "core"),
    )
    mixed, keep, give = merge(place, mixed_t, wo)
    got = swap(give, "core")
    last = swap((keep[1] + got[1].astype(F32)).astype(BF), "zh")
    branch = keep[0] + got[0].astype(F32) + last.astype(F32)
    hidden = branch * rms(branch) * gains_am[0] + inputs.astype(F32)
    hidden = hidden.astype(BF)
    result, d_hidden, d_branch, norms, parts, d_gains_am = feed(
        place, branch, hidden, inputs, cotangent.reshape(ROWS, 1024), gains_am, feed_weights
    )
    norms = lax.all_gather(norms, COLUMN, axis=0, tiled=True)
    d_branches = relative(d_branch)
    drecv = exchange(split(place, d_branches, wo), CTX)

    parts = exchange(after(parts, drecv), COLUMN).reshape(1024, 1152)
    dq, keep, give = attend_back(meta, recv, other, drecv, ot, lsum)
    keep = (keep.astype(F32) + swap(give, "core").astype(F32)).astype(BF)
    back = jnp.concatenate([dq, keep], axis=1)
    parts = after(parts, back)
    back = exchange(after(back, parts), CTX)
    g_feed = feed_grads(parts, norms, mixed, d_branches, d_gains_am.reshape(16, HEAD))
    g_feed = exchange(after(g_feed, back), CTX)

    d_qkv, g_qkv, d_gains_qk = project_back(place, back, qk, cos, sin, gains_qk, tokens_f)

    partial = dot_nt(d_qkv, w_qkv).reshape(4, ROWS, 1024)
    got = swap(jnp.stack([partial[1], partial[3]]).astype(BF), "core").astype(F32)
    last = swap((partial[2] + got[1]).astype(BF), "zh").astype(F32)
    d_inputs = d_hidden + partial[0] + got[0] + last

    g_feed, g_qkv, d_inputs = lax.optimization_barrier((g_feed, g_qkv, d_inputs))
    g_feed = g_feed.reshape(16, 2, 27, 16, HEAD)
    g_out = jnp.sum(g_feed[:, :, 18:].astype(F32), axis=(0, 1))
    d_gains_am = g_out[8]
    g_out = g_out[:8].astype(BF).reshape(2, 4, 16, HEAD)
    others = swap(lax.dynamic_index_in_dim(g_out, 1 - core, 0, keepdims=False), "core")
    g_out = lax.dynamic_index_in_dim(g_out, core, 0, keepdims=False)
    g_out = in_order(core, g_out, others).reshape(8, 16, HEAD)
    g_feed = jnp.sum(g_feed[:, :, :18].astype(F32), axis=0).astype(BF)
    g_gu = g_feed[:, :12].reshape(2, 4, 3, 16, HEAD).swapaxes(0, 1)
    g_gu = jnp.broadcast_to(g_gu[None], (2, 4, 2, 3, 16, HEAD)).reshape(8, 96, HEAD)
    g_gu = exchange(g_gu, COLUMN).reshape(2, 384, HEAD)
    g_feed = jnp.concatenate([g_feed[:, 12:].reshape(12, 16, HEAD), g_out], axis=0)
    g_feed = g_feed.reshape(320, HEAD)
    g_feed = in_order(lax.axis_index("zl"), g_feed, swap(g_feed, "zl"))
    g_feed = jnp.concatenate([g_gu, g_feed], axis=1)
    g_qkv = after(g_qkv, g_feed)
    g_feed = lax.all_gather(g_feed, PLANE, axis=0, tiled=True).reshape(NCTX, 44, 16, HEAD)

    g_qkv = exchange(g_qkv, AXES)
    gains = jnp.concatenate([d_gains_am, d_gains_qk, jnp.zeros((14, HEAD), F32)], axis=0)
    gains = gains + swap(gains.astype(BF), "core").astype(F32)
    gains = gains + swap(gains.astype(BF), "zh").astype(F32)

    g_qkv, gains = lax.optimization_barrier((g_qkv, gains))
    g_qkv = jnp.sum(g_qkv.reshape(NCTX, 4, 16, 512).astype(F32), axis=0)
    g_qkv = g_qkv.swapaxes(0, 1).reshape(16, 2048)
    g_qkv = jnp.concatenate([g_qkv, gains[16:]], axis=1).astype(BF)
    g_qkv = exchange(jnp.broadcast_to(g_qkv[None], (NCTX, 16, 2176)), CTX)
    gate_grad, up_grad, down_grad, out_grad = feed_finish(g_feed)
    g_qkv = after(g_qkv, gate_grad)
    gains_qk = jnp.sum(g_qkv[:, :2, 2048:].astype(F32), axis=0)
    gains_am = lax.dynamic_index_in_dim(gains[:16].reshape(2, 4, 256), f, 1, keepdims=False)

    g_q, g_k, g_v = project_finish(g_qkv)
    gains_qk = lax.dynamic_slice_in_dim(gains_qk, f * 32, 32, 1)
    return (
        result.reshape(tokens.shape),
        d_inputs.reshape(tokens.shape),
        g_q,
        g_k,
        g_v,
        out_grad,
        gains_qk[0],
        gains_qk[1],
        gains_am[0],
        gate_grad,
        up_grad,
        down_grad,
        gains_am[1],
    )


def solution(mesh):
    whole = Mesh(mesh.devices.reshape(4, 4, 2, 2, 2), AXES)
    blocks = P(FSDP, None, CTX, None, None)
    rows = P(FSDP, None)
    vector = P(FSDP)
    return jax.shard_map(
        local,
        mesh=whole,
        in_specs=(
            blocks,
            blocks,
            rows,
            rows,
            rows,
            rows,
            rows,
            vector,
            vector,
            vector,
            rows,
            rows,
            rows,
            vector,
        ),
        out_specs=(
            blocks,
            blocks,
            rows,
            rows,
            rows,
            rows,
            vector,
            vector,
            vector,
            rows,
            rows,
            rows,
            vector,
        ),
        check_vma=False,
    )
```
